256 devices in a mesh: row: 32 (over y_lo, z, core), col: 8 (over x, y_hi).
Axes of the slice: x: 4, y: 4 (y_hi: 2, y_lo: 2; y = y_hi * 2 + y_lo), z: 8, core: 2. Of those that a mesh axis runs over, the one named last changes fastest.
Arguments:
- features: bfloat16 [32, 1024, 4096], P(None, 'row', 'col'), may hold values from -6 to 6
- mask: int32 [1024, 4096], P('row', 'col'), may hold values from 0 to 1, as said below
- mask_gain: float32 [32], replicated, may hold values from -3 to 3
- conv_one: bfloat16 [9, 32, 32], replicated, may hold values from -0.375 to 0.375
- conv_two: bfloat16 [9, 32, 32], replicated, may hold values from -0.375 to 0.375
- spec_real: bfloat16 [2048, 32, 32], P(('row', 'col')), may hold values from -5 to 5
- spec_imag: bfloat16 [2048, 32, 32], P(('row', 'col')), may hold values from -5 to 5
- cotangent: bfloat16 [32, 1024, 4096], P(None, 'row', 'col'), may hold values from -6 to 6
Outputs:
- output: bfloat16 [32, 1024, 4096], P(None, 'row', 'col')
- grad_conv_one: float32 [9, 32, 32], replicated
- grad_conv_two: float32 [9, 32, 32], replicated
- grad_spec_real: float32 [2048, 32, 32], P(('row', 'col'))
- grad_spec_imag: float32 [2048, 32, 32], P(('row', 'col'))
The draws below stay inside these ranges and needn't reach their ends.
Inputs may be any that keep to these rules, and one draw needn't show every extreme that they name: `mask`: layout pixels, each exactly 0 or 1.
All inputs are finite; a program needn't handle non-finite values.
Results may differ from the reference program's by a relative error of at most 0.006.
Values may be sent and summed in bfloat16 or wider, within the bound.
A program may use at most 192 MiB of HBM per device.

```python
import math
import jax
import jax.numpy as jnp
from jax import lax

C = 32
M = 32
RATIO = 8
TR = 32
NX = 1024
NY = 4096
N1 = 128
N2 = 512
MODES = 2048
N_ROW = 32


def draw_mask(key, part):
    key = jax.random.fold_in(key, 11)
    key_level, key_pixel = jax.random.split(key)
    level = jax.random.randint(key_level, (NX // RATIO, 1, NY // RATIO, 1), 0, RATIO + 1)
    pixel = jax.random.randint(key_pixel, (NX // RATIO, RATIO, NY // RATIO, RATIO), 0, RATIO)
    return (pixel < level).astype(jnp.int32).reshape(NX, NY)


def block_scale(key, shape, shards, low, high):
    level = 1.0
    for dim, parts in shards:
        steps = jax.random.uniform(jax.random.fold_in(jax.random.fold_in(key, 6), dim), (parts,), jnp.float32, low / len(shards), high / len(shards))
        level = level * jnp.repeat(jnp.exp(steps), shape[dim] // parts).reshape((-1,) + (1,) * (len(shape) - 1 - dim))
    return level


def gaussian(stream_key, extent, scale, limit, cuts=(), held_as=jnp.bfloat16):
    drawn = jax.random.normal(stream_key, extent, jnp.float32) * scale
    if len(cuts) > 0:
        drawn = block_scale(stream_key, extent, cuts, -0.22, 0.18) * drawn
    return jnp.clip(drawn, min=-limit, max=limit).astype(held_as)


def setup_inputs(seed: int = 0) -> dict:
    arg_keys = jax.random.split(jax.random.key(seed), 9)
    features = gaussian(arg_keys[0], (C, NX, NY), 1.0, 6.0, ((1, 32), (2, 8)))
    mask = draw_mask(jax.random.fold_in(arg_keys[8], 71), 0)
    mask_gain = gaussian(arg_keys[2], (C,), 1.0, 3.0, (), jnp.float32)
    conv_one = gaussian(arg_keys[3], (9, C, C), (9 * C) ** -0.5, 0.375)
    conv_two = gaussian(arg_keys[4], (9, C, C), (9 * C) ** -0.5, 0.375)
    spec_real = gaussian(arg_keys[5], (MODES, C, C), 1.0, 5.0, ((0, 256),))
    spec_imag = gaussian(arg_keys[6], (MODES, C, C), 1.0, 5.0, ((0, 256),))
    cotangent = gaussian(arg_keys[7], (C, NX, NY), 1.0, 6.0, ((1, 32), (2, 8)))
    return dict(features=features, mask=mask, mask_gain=mask_gain, conv_one=conv_one, conv_two=conv_two, spec_real=spec_real, spec_imag=spec_imag, cotangent=cotangent)


exact_mode = lax.Precision.HIGHEST

def bilinear_weights():
    offsets = (jnp.arange(RATIO, dtype=jnp.float32) + 0.5 - RATIO / 2) / RATIO
    return jnp.stack([jnp.maximum(-offsets, 0.0), 1.0 - jnp.abs(offsets), jnp.maximum(offsets, 0.0)])

def fourier_tables(rows_glob, cols_glob, n_one, n_two, modes):
    index_q = jnp.arange(2 * modes, dtype=jnp.int32)
    freq_one = jnp.where(index_q < modes, index_q, n_one - 2 * modes + index_q)
    freq_two = jnp.arange(modes, dtype=jnp.int32)
    phase_row = (freq_one[:, None] * rows_glob[None, :] % n_one).astype(jnp.float32) * (2.0 * math.pi / n_one)
    phase_col = (cols_glob[:, None] * freq_two[None, :] % n_two).astype(jnp.float32) * (2.0 * math.pi / n_two)
    return (jnp.cos(phase_row), jnp.sin(phase_row), jnp.cos(phase_col), jnp.sin(phase_col))

def mode_factor(modes):
    return jnp.where(jnp.arange(modes) == 0, 1.0, 2.0).astype(jnp.float32)

def analyse(field, tables, scaling):
    cos_row, sin_row, cos_col, sin_col = tables
    along_cos = jnp.einsum('cij,jk->cik', field, cos_col, precision=exact_mode)
    along_sin = jnp.einsum('cij,jk->cik', field, sin_col, precision=exact_mode)
    real_part = (jnp.einsum('qi,cik->qkc', cos_row, along_cos, precision=exact_mode) - jnp.einsum('qi,cik->qkc', sin_row, along_sin, precision=exact_mode)) * scaling
    imag_part = -(jnp.einsum('qi,cik->qkc', sin_row, along_cos, precision=exact_mode) + jnp.einsum('qi,cik->qkc', cos_row, along_sin, precision=exact_mode)) * scaling
    stacked = jnp.stack([real_part, imag_part], axis=2)
    return stacked.reshape(-1, 2, field.shape[0])

def synthesise(mixed, tables, scaling):
    cos_row, sin_row, cos_col, sin_col = tables
    modes = cos_col.shape[1]
    weighted = mixed.reshape(-1, modes, 2, mixed.shape[2]) * mode_factor(modes)[None, :, None, None]
    real_part = weighted[:, :, 0]
    imag_part = weighted[:, :, 1]
    first = jnp.einsum('qko,qi->oik', real_part, cos_row, precision=exact_mode) - jnp.einsum('qko,qi->oik', imag_part, sin_row, precision=exact_mode)
    second = jnp.einsum('qko,qi->oik', real_part, sin_row, precision=exact_mode) + jnp.einsum('qko,qi->oik', imag_part, cos_row, precision=exact_mode)
    return (jnp.einsum('oik,jk->oij', first, cos_col, precision=exact_mode) - jnp.einsum('oik,jk->oij', second, sin_col, precision=exact_mode)) * scaling

def synthesis_adjoint(grad, tables, scaling):
    cos_row, sin_row, cos_col, sin_col = tables
    modes = cos_col.shape[1]
    first = jnp.einsum('oij,jk->oik', grad, cos_col, precision=exact_mode) * scaling
    second = -jnp.einsum('oij,jk->oik', grad, sin_col, precision=exact_mode) * scaling
    real_part = jnp.einsum('oik,qi->qko', first, cos_row, precision=exact_mode) + jnp.einsum('oik,qi->qko', second, sin_row, precision=exact_mode)
    imag_part = -jnp.einsum('oik,qi->qko', first, sin_row, precision=exact_mode) + jnp.einsum('oik,qi->qko', second, cos_row, precision=exact_mode)
    factor = mode_factor(modes)[None, :, None]
    stacked = jnp.stack([real_part * factor, imag_part * factor], axis=2)
    return stacked.reshape(-1, 2, grad.shape[0])

def mix_modes(w_real, w_imag, spectrum):
    real_in = spectrum[:, 0]
    imag_in = spectrum[:, 1]
    weight_real = w_real.astype(jnp.float32)
    weight_imag = w_imag.astype(jnp.float32)
    real_out = jnp.einsum('koc,kc->ko', weight_real, real_in, precision=exact_mode) - jnp.einsum('koc,kc->ko', weight_imag, imag_in, precision=exact_mode)
    imag_out = jnp.einsum('koc,kc->ko', weight_real, imag_in, precision=exact_mode) + jnp.einsum('koc,kc->ko', weight_imag, real_in, precision=exact_mode)
    return jnp.stack([real_out, imag_out], axis=1)

def mix_gradient(grad, spectrum):
    grad_re = grad[:, 0]
    grad_im = grad[:, 1]
    spec_re = spectrum[:, 0]
    spec_im = spectrum[:, 1]
    grad_real = grad_re[:, :, None] * spec_re[:, None, :] + grad_im[:, :, None] * spec_im[:, None, :]
    grad_imag = grad_im[:, :, None] * spec_re[:, None, :] - grad_re[:, :, None] * spec_im[:, None, :]
    return (grad_real, grad_imag)

def tap_window(field, first_row, first_col, out_rows, out_cols):
    zero = jnp.zeros((), jnp.int32)
    window = lax.dynamic_slice(field, (zero, first_row.astype(jnp.int32), first_col.astype(jnp.int32)), (field.shape[0], out_rows, out_cols))
    return window.reshape(field.shape[0], out_rows * out_cols)

def convolve(field, weight, out_rows, out_cols):

    def add_tap(tap, total):
        window = tap_window(field, tap // 3, tap % 3, out_rows, out_cols)
        return total + jnp.dot(weight[tap], window, preferred_element_type=jnp.float32)
    total = jnp.zeros((weight.shape[1], out_rows * out_cols), jnp.float32)
    total = lax.fori_loop(jnp.int32(0), jnp.int32(9), add_tap, total)
    return total.reshape(weight.shape[1], out_rows, out_cols)

def convolve_adjoint(grad_ext, weight, offset, out_rows, out_cols):

    def add_tap(tap, total):
        window = tap_window(grad_ext, offset + 1 - tap // 3, offset + 1 - tap % 3, out_rows, out_cols)
        return total + lax.dot_general(weight[tap], window, (((0,), (0,)), ((), ())), preferred_element_type=jnp.float32)
    total = jnp.zeros((weight.shape[2], out_rows * out_cols), jnp.float32)
    total = lax.fori_loop(jnp.int32(0), jnp.int32(9), add_tap, total)
    return total.reshape(weight.shape[2], out_rows, out_cols)

def weight_grad(grad, field, offset, out_rows, out_cols):
    flat_grad = grad.reshape(grad.shape[0], out_rows * out_cols)

    def add_tap(tap, stacked):
        window = tap_window(field, offset - 1 + tap // 3, offset - 1 + tap % 3, out_rows, out_cols)
        term = lax.dot_general(flat_grad, window, (((1,), (1,)), ((), ())), preferred_element_type=jnp.float32)
        return lax.dynamic_update_slice(stacked, term[None], (tap, jnp.zeros((), jnp.int32), jnp.zeros((), jnp.int32)))
    stacked = jnp.zeros((9, grad.shape[0], field.shape[0]), jnp.float32)
    return lax.fori_loop(jnp.int32(0), jnp.int32(9), add_tap, stacked)

def prolong(coarse_ext, coarse_rows, coarse_cols):
    weights = bilinear_weights()
    channels = coarse_ext.shape[0]
    upward = jnp.zeros((channels, coarse_rows, RATIO, coarse_cols + 2), jnp.float32)
    for step_row in (-1, 0, 1):
        upward = upward + weights[step_row + 1][None, None, :, None] * coarse_ext[:, 1 + step_row:1 + step_row + coarse_rows, None, :]
    result = jnp.zeros((channels, coarse_rows, RATIO, coarse_cols, RATIO), jnp.float32)
    for step_col in (-1, 0, 1):
        result = result + weights[step_col + 1][None, None, None, None, :] * upward[:, :, :, 1 + step_col:1 + step_col + coarse_cols, None]
    return result.reshape(channels, coarse_rows * RATIO, coarse_cols * RATIO)

def adjoint_restrict(blocks, coarse_rows, coarse_cols):
    weights = bilinear_weights()
    wide = blocks.astype(jnp.float32)
    across = jnp.zeros(wide.shape[:3] + (coarse_cols,), jnp.float32)
    for step_col in (-1, 0, 1):
        summed = jnp.einsum('q,ckplq->ckpl', weights[step_col + 1], wide, precision=exact_mode)
        across = across + summed[..., 1 - step_col:1 - step_col + coarse_cols]
    result = jnp.zeros((wide.shape[0], coarse_rows, coarse_cols), jnp.float32)
    for step_row in (-1, 0, 1):
        result = result + jnp.einsum('p,ckpl->ckl', weights[step_row + 1], across[:, 1 - step_row:1 - step_row + coarse_rows], precision=exact_mode)
    return result

def wrap_cols(field, width):
    return jnp.concatenate([field[..., -width:], field, field[..., :width]], axis=-1)

def reference(features, mask, mask_gain, conv_one, conv_two, spec_real, spec_imag, cotangent):
    layer = (features.astype(jnp.float32) + mask_gain[:, None, None] * (mask.astype(jnp.float32) - 0.5)[None]).astype(jnp.bfloat16)
    coarse = layer.reshape(C, N1, RATIO, N2, RATIO).astype(jnp.float32).mean(axis=(2, 4))
    tables = fourier_tables(jnp.arange(N1, dtype=jnp.int32), jnp.arange(N2, dtype=jnp.int32), N1, N2, M)
    scaling = 1.0 / math.sqrt(N1 * N2)
    spectrum = analyse(coarse, tables, scaling)
    mixed = mix_modes(spec_real, spec_imag, spectrum)
    smooth = synthesise(mixed, tables, scaling)
    coarse_rows = TR // RATIO

    def band_work(band):
        band = band.astype(jnp.int32)
        fine_index = ((band * TR - 2 + jnp.arange(TR + 4, dtype=jnp.int32)) % NX).astype(jnp.int32)
        layer_band = wrap_cols(jnp.take(layer, fine_index, axis=1), 2)
        pre_ext = convolve(layer_band, conv_one, TR + 2, NY + 2)
        hidden_ext = jax.nn.gelu(pre_ext).astype(jnp.bfloat16)
        local = convolve(hidden_ext, conv_two, TR, NY)
        coarse_index = ((band * coarse_rows - 1 + jnp.arange(coarse_rows + 2, dtype=jnp.int32)) % N1).astype(jnp.int32)
        smooth_band = wrap_cols(jnp.take(smooth, coarse_index, axis=1), 1)
        output_band = (local + prolong(smooth_band, coarse_rows, N2)).astype(jnp.bfloat16)
        grad_index = ((band * TR - 1 + jnp.arange(TR + 2, dtype=jnp.int32)) % NX).astype(jnp.int32)
        grad_band = wrap_cols(jnp.take(cotangent, grad_index, axis=1), 1)
        own_grad = grad_band[:, 1:-1, 1:-1]
        hidden_grad = convolve_adjoint(grad_band, conv_two, 1, TR, NY)
        pre_grad = jax.vjp(jax.nn.gelu, pre_ext[:, 1:-1, 1:-1])[1](hidden_grad)[0].astype(jnp.bfloat16)
        grad_two = weight_grad(own_grad, hidden_ext, 1, TR, NY)
        grad_one = weight_grad(pre_grad, layer_band, 2, TR, NY)
        return (output_band, grad_one, grad_two)
    outputs, grads_one, grads_two = lax.map(band_work, jnp.arange(N_ROW, dtype=jnp.int32))
    output = outputs.transpose(1, 0, 2, 3).reshape(C, NX, NY)
    scale = 1.0 / math.sqrt(NX * NY)
    grad_conv_one = lax.optimization_barrier(jnp.sum(grads_one, axis=0)) * scale
    grad_conv_two = lax.optimization_barrier(jnp.sum(grads_two, axis=0)) * scale

    def channel_grad(plane):
        tall = jnp.concatenate([plane[-RATIO:], plane, plane[:RATIO]], axis=0)
        wide = wrap_cols(tall, RATIO)
        blocks = wide.reshape(1, N1 + 2, RATIO, N2 + 2, RATIO)
        return adjoint_restrict(blocks, N1, N2)[0]
    smooth_grad = lax.map(channel_grad, cotangent)
    mixed_grad = synthesis_adjoint(smooth_grad, tables, scaling)
    grad_spec_real, grad_spec_imag = mix_gradient(mixed_grad, spectrum)
    return (output, grad_conv_one, grad_conv_two, grad_spec_real, grad_spec_imag)
```

```python
import functools
import math

import jax
import jax.numpy as jnp
import numpy as np
from jax import lax
from jax.experimental import pallas as pl
from jax.experimental.pallas import tpu as pltpu
from jax.sharding import PartitionSpec as P

C = 32
M = 32
RATIO = 8
MESH = pl.DeviceIdType.MESH
HIGH = lax.Precision.HIGHEST
F32 = jnp.float32
BF16 = jnp.bfloat16
GELU_A = math.sqrt(2.0 / math.pi)
GELU_B = 0.044715
VMEM_LIMIT = 48 * 2**20
NT = (((1,), (1,)), ((), ()))
TN = (((0,), (0,)), ((), ()))
NN = (((1,), (0,)), ((), ()))


def dot(a, b, dims, precision=None):
    return lax.dot_general(a, b, dims, preferred_element_type=F32, precision=precision)


def weights_np():
    d = (np.arange(RATIO) + 0.5 - RATIO / 2) / RATIO
    return np.stack([np.maximum(-d, 0.0), 1.0 - np.abs(d), np.maximum(d, 0.0)])


def column_tables(n_col):
    w = weights_np()
    n_two = 64 * n_col
    r = np.arange(M)
    out = np.zeros((n_col, 2, 64, 512))
    for j in range(n_col):
        fine = np.arange(512)
        cell, s = 64 * j + fine // RATIO, fine % RATIO

        def wave(at):
            return np.exp(-2j * np.pi * ((r[:, None] * at[None, :]) % n_two) / n_two)

        mean = wave(cell) / 64.0
        restrict = sum(w[b + 1][s][None, :] * wave(cell + b) for b in (-1, 0, 1))
        for kind, value in enumerate((mean, restrict)):
            parts = np.stack([value.real, value.imag], axis=0).reshape(2, 4, 8, 512)
            out[j, kind] = parts.transpose(1, 0, 2, 3).reshape(64, 512)
    return out.astype(np.float32)


def row_tables(n_row):
    n_one = 4 * n_row
    q_all = np.arange(2 * n_row)
    f1 = np.where(q_all < n_row, q_all, n_one - 2 * n_row + q_all)
    out = np.zeros((2 * n_row, n_row, 16))
    for i in range(n_row):
        for h in range(2):
            q = 2 * np.arange(n_row) + h
            for kk in range(6):
                phase = 2 * np.pi * ((f1[q] * (4 * i + kk - 1)) % n_one) / n_one
                out[2 * i + h, :, 2 * kk] = np.cos(phase)
                out[2 * i + h, :, 2 * kk + 1] = np.sin(phase)
    out = out.reshape(2 * n_row, n_row * 16)
    out = np.pad(out, ((0, 0), (0, -out.shape[1] % 128)))
    return out.reshape(2 * n_row, -1, 128).astype(np.float32)


def prolong_table():
    w = weights_np()
    out = np.zeros((C, RATIO, 3, C))
    for c in range(C):
        out[c, :, :, c] = w.T
    return out.reshape(C * RATIO, 3 * C).astype(np.float32)


def expand_table():
    return np.repeat(np.eye(C), RATIO, axis=0).astype(np.float32)


def lane_group(shape):
    return lax.broadcasted_iota(jnp.int32, shape, len(shape) - 1) // 32


def place(value, source, target):
    shift = (32 * (target - source)) % 128
    moved = pltpu.roll(value, shift, 1) if shift else value
    return jnp.where(lane_group(value.shape) == target, moved, 0.0)


def everywhere(value):
    value = value + pltpu.roll(value, 64, 1)
    return value + pltpu.roll(value, 32, 1)


def remote(src, dst, send, recv, row, col):
    return pltpu.make_async_remote_copy(
        src_ref=src,
        dst_ref=dst,
        send_sem=send,
        recv_sem=recv,
        device_id=(row, col),
        device_id_type=MESH,
    )


def greet(i, j, n_row, n_col, diagonals):
    barrier = pltpu.get_barrier_semaphore()

    def to_row(d, _):
        pl.semaphore_signal(barrier, inc=1, device_id=((i + d) % n_row, j), device_id_type=MESH)
        return 0

    def to_col(d, _):
        pl.semaphore_signal(barrier, inc=1, device_id=(i, (j + d) % n_col), device_id_type=MESH)
        return 0

    lax.fori_loop(1, n_row, to_row, 0)
    lax.fori_loop(1, n_col, to_col, 0)
    count = n_row + n_col - 2
    if diagonals:
        for di in (1, n_row - 1):
            for dj in (1, n_col - 1):
                pl.semaphore_signal(
                    barrier,
                    inc=1,
                    device_id=((i + di) % n_row, (j + dj) % n_col),
                    device_id_type=MESH,
                )
        count += 4
    return barrier, count


def prepare(feat, mask, gain, cot, lext, cext, field):
    w = weights_np()
    for half in range(2):

        def tile(t, _, half=half):
            lanes = pl.ds(pl.multiple_of(t * 128, 128), 128)
            rows = pl.ds(16 * half, 16)
            raised = mask[rows, lanes].astype(F32) - 0.5
            layer = feat[:, rows, lanes].astype(F32) + gain[...][:, :, None] * raised[None]
            layer = layer.astype(BF16).astype(F32)
            layer = jnp.swapaxes(layer, 0, 1)
            lext[pl.ds(4 + 16 * half, 16), :, lanes] = layer.astype(BF16)
            grad = jnp.swapaxes(cot[:, rows, lanes].astype(F32), 0, 1)
            cext[pl.ds(4 + 16 * half, 16), :, lanes] = grad.astype(BF16)
            sums = [None] * 4
            for cell in range(2):
                total = layer[8 * cell]
                for p in range(1, 8):
                    total = total + layer[8 * cell + p]
                field[2 * half + cell, :, lanes] = total
                for p in range(8):
                    for a in (-1, 0, 1):
                        weight = float(w[a + 1][p])
                        if weight == 0.0:
                            continue
                        term = grad[8 * cell + p] * weight
                        at = cell + a + 1
                        sums[at] = term if sums[at] is None else sums[at] + term
            for at in range(4):
                slot = 4 + 2 * half + at
                if half == 1 and at < 2:
                    field[slot, :, lanes] = field[slot, :, lanes] + sums[at]
                else:
                    field[slot, :, lanes] = sums[at]
            return 0

        lax.fori_loop(0, 4, tile, 0)


def pick(shape, pairs):
    row = lax.broadcasted_iota(jnp.int32, shape, 0)
    lane = lax.broadcasted_iota(jnp.int32, shape, 1)
    hit = jnp.zeros(shape, jnp.bool_)
    for r, l in pairs:
        hit = hit | ((row == r) & (lane == l))
    return jnp.where(hit, 1.0, 0.0).astype(BF16)


def exchange_kernel(
    n_row, n_col, scaling,
    feat, mask, gain, cot, w_real, w_imag, col_tab, row_tab,
    lext, cext, high, low, g_real, g_imag,
    field, tab, twiddle, share, share_in, part, part_in, mixed, mixed_in, folded, folded_in,
    left, right, side_in, rows_in, row_c_in,
    local_sem, halo_send, halo_recv, a_send, a_recv, b_send, b_recv, c_send, c_recv, d_send, d_recv,
):
    i = lax.axis_index("row")
    j = lax.axis_index("col")
    half = j // 4
    copy_tab = pltpu.make_async_copy(col_tab.at[j], tab, local_sem.at[0])
    copy_tab.start()
    copy_twiddle = pltpu.make_async_copy(row_tab.at[2 * i + half], twiddle, local_sem.at[1])
    copy_twiddle.start()
    barrier, count = greet(i, j, n_row, n_col, True)
    prepare(feat, mask, gain, cot, lext, cext, field)
    copy_tab.wait()

    share[...] = jnp.zeros_like(share)
    share[:, 0:128] = dot(tab[0], field[0:4].reshape(128, 512), NT, HIGH)
    share[:, 128:320] = dot(tab[1], field[4:10].reshape(192, 512), NT, HIGH)
    pl.semaphore_wait(barrier, count)

    def a_copy(d):
        to = (j + d) % n_col
        group = pl.ds(pl.multiple_of(16 * (to % 4), 16), 16)
        return remote(share.at[group], share_in.at[j], a_send.at[d], a_recv.at[d], i, to)

    for d in range(1, n_col):
        a_copy(d).start()
    share_in[j] = share[pl.ds(pl.multiple_of(16 * (j % 4), 16), 16), :]

    first_l = lext[4:36, :, 0:128].reshape(1024, 128)
    last_l = lext[4:36, :, 384:512].reshape(1024, 128)
    first_c = cext[4:36, :, 0:128].reshape(1024, 128)
    last_c = cext[4:36, :, 384:512].reshape(1024, 128)
    sel = (16, 128)
    left[...] = (
        dot(pick(sel, ((0, 0), (1, 1))), first_l, NT) + dot(pick(sel, ((2, 0),)), first_c, NT)
    )[0:4]
    right[...] = (
        dot(pick(sel, ((0, 126), (1, 127))), last_l, NT) + dot(pick(sel, ((2, 127),)), last_c, NT)
    )[0:4]
    up, down = (i + n_row - 1) % n_row, (i + 1) % n_row
    west, east = (j + n_col - 1) % n_col, (j + 1) % n_col
    plan = [
        (lext.at[4:6, :, 0:512], rows_in.at[1], up, j),
        (lext.at[34:36, :, 0:512], rows_in.at[0], down, j),
        (cext.at[4:5, :, 0:512], row_c_in.at[1], up, j),
        (cext.at[35:36, :, 0:512], row_c_in.at[0], down, j),
        (left, side_in.at[1, :, 128:1152], i, west),
        (right, side_in.at[0, :, 128:1152], i, east),
        (left.at[:, 0:128], side_in.at[1, :, 1152:1280], up, west),
        (right.at[:, 0:128], side_in.at[0, :, 1152:1280], up, east),
        (left.at[:, 896:1024], side_in.at[1, :, 0:128], down, west),
        (right.at[:, 896:1024], side_in.at[0, :, 0:128], down, east),
    ]
    halos = [
        remote(src, dst, halo_send.at[n], halo_recv.at[n], row, col)
        for n, (src, dst, row, col) in enumerate(plan)
    ]
    for copy in halos:
        copy.start()

    copy_twiddle.wait()
    for d in range(1, n_col):
        a_copy(d).wait_recv()
    total = share_in[0]
    for k in range(1, n_col):
        total = total + share_in[k]

    ps, qs = [], []
    for kk in range(6):
        re, im = [], []
        for out, rows in ((re, slice(0, 8)), (im, slice(8, 16))):
            if 1 <= kk <= 4:
                out.append((total[rows, 0:128], kk - 1, 0))
            at = 128 + 32 * kk
            tile = at // 128
            out.append((total[rows, 128 * tile : 128 * tile + 128], (at % 128) // 32, 1))
        p_sum = jnp.zeros((8, 128), F32)
        q_sum = jnp.zeros((8, 128), F32)
        for value, source, kind in re:
            p_sum = p_sum + place(value, source, kind)
            q_sum = q_sum - place(value, source, kind + 2)
        for value, source, kind in im:
            p_sum = p_sum + place(value, source, kind + 2)
            q_sum = q_sum + place(value, source, kind)
        ps.append(p_sum)
        qs.append(q_sum)

    def factor(q, n):
        at = q * 16 + n
        return twiddle[at // 128, at % 128]

    def row_transform(q, _):
        out = jnp.zeros((8, 128), F32)
        for kk in range(6):
            out = out + factor(q, 2 * kk) * ps[kk] + factor(q, 2 * kk + 1) * qs[kk]
        part[q] = out
        return 0

    lax.fori_loop(0, n_row, row_transform, 0)

    def b_copy(d):
        to = (i + d) % n_row
        return remote(part.at[to], part_in.at[i], b_send.at[d], b_recv.at[d], to, j)

    def start(copy):
        def step(d, _):
            copy(d).start()
            return 0

        lax.fori_loop(1, n_row, step, 0)

    def arrive(copy):
        def step(d, _):
            copy(d).wait_recv()
            return 0

        lax.fori_loop(1, n_row, step, 0)

    def leave(copy):
        def step(d, _):
            copy(d).wait_send()
            return 0

        lax.fori_loop(1, n_row, step, 0)

    start(b_copy)
    part_in[i] = part[i]
    arrive(b_copy)
    spectrum = part_in[0]
    for k in range(1, n_row):
        spectrum = spectrum + part_in[k]

    group = lane_group((8, 128))
    row = lax.broadcasted_iota(jnp.int32, (8, 128), 0)
    first = (row == 0) & (j % 4 == 0)
    twice = jnp.where(first, 1.0, 2.0)
    spectrum = spectrum * jnp.where(group % 2 == 1, twice * scaling, scaling)
    s_re = everywhere(jnp.where(group == 0, spectrum, 0.0))
    m_re = everywhere(jnp.where(group == 1, spectrum, 0.0))
    s_im = everywhere(jnp.where(group == 2, spectrum, 0.0))
    m_im = everywhere(jnp.where(group == 3, spectrum, 0.0))
    wide = lane_group((16, 256)) == lax.broadcasted_iota(jnp.int32, (16, 256), 0) % 8
    both = jnp.concatenate([s_re, s_im], axis=0)[:, 0:32]
    by_real = jnp.where(wide, dot(both, w_real[...].reshape(256, 32).astype(F32), NT, HIGH), 0.0)
    by_imag = jnp.where(wide, dot(both, w_imag[...].reshape(256, 32).astype(F32), NT, HIGH), 0.0)
    mixed_re = by_real[0:8] - by_imag[8:16]
    mixed_im = by_real[8:16] + by_imag[0:8]
    mixed_re = everywhere(mixed_re[:, 0:128] + mixed_re[:, 128:256])
    mixed_im = everywhere(mixed_im[:, 0:128] + mixed_im[:, 128:256])
    mixed[...] = jnp.where(
        group == 1, mixed_im, jnp.where(group == 2, -mixed_im, mixed_re)
    )

    def c_copy(d):
        to = (i + d) % n_row
        return remote(mixed, mixed_in.at[i], c_send.at[d], c_recv.at[d], to, j)

    start(c_copy)
    mixed_in[i] = mixed[...]

    grads = jnp.concatenate(
        [jnp.concatenate([m_re, m_re], axis=1), jnp.concatenate([m_im, m_im], axis=1)], axis=0
    )
    grads = jnp.where(wide, grads, 0.0)
    fields = jnp.concatenate(
        [jnp.where(group == 0, s_re, -s_im), jnp.where(group == 0, s_im, s_re)], axis=0
    )
    outer = dot(grads, fields, TN, HIGH)
    g_real[...] = outer[:, 0:32].reshape(8, 32, 32)
    g_imag[...] = outer[:, 32:64].reshape(8, 32, 32)

    for copy in halos:
        copy.wait()
    lext[2:4, :, 0:512] = rows_in[0]
    lext[36:38, :, 0:512] = rows_in[1]
    cext[3:4, :, 0:512] = row_c_in[0]
    cext[36:37, :, 0:512] = row_c_in[1]
    sides = jnp.concatenate([side_in[0], side_in[1]], axis=0).astype(BF16)
    at_l = pick((8, 128), ((0, 126), (1, 127), (4, 0), (5, 1)))
    at_c = pick((8, 128), ((2, 127), (6, 0)))
    lext[:, :, 512:640] = dot(sides, at_l, TN).astype(BF16).reshape(40, 32, 128)
    cext[:, :, 512:640] = dot(sides, at_c, TN).astype(BF16).reshape(40, 32, 128)

    arrive(c_copy)

    def inverse(q, sums):
        value = mixed_in[q]
        out = []
        for kk in range(6):
            out.append(sums[2 * kk] + factor(q, 2 * kk) * value)
            out.append(sums[2 * kk + 1] + factor(q, 2 * kk + 1) * value)
        return tuple(out)

    zero = jnp.zeros((8, 128), F32)
    sums = lax.fori_loop(0, n_row, inverse, (zero,) * 12)
    grown = twice * scaling
    tiles = [zero] * 4
    for kk in range(6):
        value = (sums[2 * kk] + pltpu.roll(sums[2 * kk + 1], 64, 1)) * grown
        tiles[kk // 4] = tiles[kk // 4] + place(value, 0, kk % 4)
        tiles[2 + kk // 4] = tiles[2 + kk // 4] + place(value, 1, kk % 4)
    folded[0:8, 0:128] = tiles[0]
    folded[0:8, 128:256] = tiles[1]
    folded[8:16, 0:128] = tiles[2]
    folded[8:16, 128:256] = tiles[3]

    def d_copy(d):
        to = (j + d) % n_col
        return remote(folded, folded_in.at[j], d_send.at[d], d_recv.at[d], i, to)

    for d in range(1, n_col):
        d_copy(d).start()
    folded_in[j] = folded[...]
    leave(b_copy)
    leave(c_copy)
    for d in range(1, n_col):
        a_copy(d).wait_send()
    for d in range(1, n_col):
        d_copy(d).wait_recv()
    waves = (folded_in[0:4] + folded_in[4:8]).reshape(64, 256)
    smooth = dot(waves, tab[1], TN, HIGH)[0:192]
    upper = smooth.astype(BF16)
    high[...] = upper
    low[...] = (smooth - upper.astype(F32)).astype(BF16)
    for d in range(1, n_col):
        d_copy(d).wait_send()


def tiled(value):
    wide = jnp.concatenate([value, jnp.zeros((32, 96), value.dtype)], axis=1)
    return everywhere(wide)


def conv_kernel(
    lext, cext, high, low, w_one, w_two, spread, stretch,
    out, grads,
    l_shift, c_shift, h_shift, slope, band_one, band_two, band_back, sum_one, sum_two,
):
    eye = jnp.where(
        lax.broadcasted_iota(jnp.int32, (32, 32), 0) == lax.broadcasted_iota(jnp.int32, (32, 32), 1),
        1.0,
        0.0,
    ).astype(BF16)
    block = lane_group((32, 256))
    line = lax.broadcasted_iota(jnp.int32, (256, 384), 0) % 8
    wide_block = lane_group((256, 384))
    for v in range(3):
        ones, backs, twos = [], [], []
        for u in range(3):
            one = tiled(w_one[3 * u + v].astype(F32))
            ones.append(jnp.concatenate([one, one], axis=1))
            back = tiled(dot(eye, w_two[3 * u + v], NT))
            backs.append(jnp.concatenate([back, back], axis=1))
            two = tiled(w_two[3 * u + v].astype(F32))
            twos.append(jnp.concatenate([two, two, two], axis=1).astype(BF16))
        for r in range(6):
            one = jnp.zeros((32, 256), F32)
            back = jnp.zeros((32, 256), F32)
            for u in range(3):
                one = one + jnp.where(block == r + u, ones[u], 0.0)
                back = back + jnp.where(block == r + 2 - u, backs[u], 0.0)
            band_one[v, 32 * r : 32 * r + 32, :] = one.astype(BF16)
            band_back[v, 32 * r : 32 * r + 32, :] = back.astype(BF16)
        total = jnp.zeros((256, 384), F32)
        for u in range(3):
            total = total + jnp.where(
                wide_block - line == u, dot(spread[...], twos[u], NN), 0.0
            )
        band_two[v] = total[:, 0:320].astype(BF16)

    def move(k, _):
        rows = pl.ds(2 + 4 * k, 4)
        value = lext[rows].reshape(128, 640)
        l_shift[0, rows] = shifted(value, 1).reshape(4, 32, 640)
        l_shift[1, rows] = shifted(value, -1).reshape(4, 32, 640)
        value = cext[rows].reshape(128, 640)
        c_shift[0, rows] = shifted(value, 1)[:, 0:512].reshape(4, 32, 512)
        c_shift[1, rows] = shifted(value, -1)[:, 0:512].reshape(4, 32, 512)
        return 0

    lax.fori_loop(0, 9, move, 0)

    def forward(k, _):
        at = jnp.minimum(6 * k, 28)
        rows = pl.ds(at + 2, 8)
        pre = dot(band_one[1], lext[rows].reshape(256, 640), NN)
        pre = pre + dot(band_one[0], l_shift[0, rows].reshape(256, 640), NN)
        pre = pre + dot(band_one[2], l_shift[1, rows].reshape(256, 640), NN)
        square = pre * pre
        bend = jnp.tanh(GELU_A * (pre + GELU_B * (square * pre)))
        half = 0.5 * (1.0 + bend)
        hidden = (pre * half).astype(BF16)
        rise = half + 0.5 * pre * (1.0 - bend * bend) * (GELU_A * (1.0 + 3.0 * GELU_B * square))
        slope[pl.ds(at, 6)] = rise[:, 0:512].reshape(6, 32, 512)
        to = pl.ds(at, 6)
        h_shift[1, to] = hidden[:, 0:512].reshape(6, 32, 512)
        h_shift[0, to] = shifted(hidden, 1)[:, 0:512].reshape(6, 32, 512)
        h_shift[2, to] = shifted(hidden, -1)[:, 0:512].reshape(6, 32, 512)
        return 0

    lax.fori_loop(0, 6, forward, 0)

    def window(t):
        rows = pl.ds(8 * t, 10)
        coarse = pl.ds(pl.multiple_of(32 * t, 32), 96)
        total = dot(stretch[...], high[coarse, :], NN) + dot(stretch[...], low[coarse, :], NN)
        for v in range(3):
            total = total + dot(band_two[v], h_shift[v, rows].reshape(320, 512), NN)
        return total.reshape(32, 8, 512)

    def second(t, _):
        value = jnp.concatenate([window(2 * t), window(2 * t + 1)], axis=1)
        out[:, pl.ds(pl.multiple_of(16 * t, 16), 16), :] = value.astype(BF16)
        return 0

    lax.fori_loop(0, 2, second, 0)

    sum_one[...] = jnp.zeros_like(sum_one)
    sum_two[...] = jnp.zeros_like(sum_two)
    line6 = lax.broadcasted_iota(jnp.int32, (192, 512), 0) // 32

    def backward(k, _):
        at = jnp.minimum(6 * k, 26)
        rows = pl.ds(at + 3, 8)
        grad = dot(band_back[1], cext[rows, :, 0:512].reshape(256, 512), NN)
        grad = grad + dot(band_back[0], c_shift[1, rows].reshape(256, 512), NN)
        grad = grad + dot(band_back[2], c_shift[0, rows].reshape(256, 512), NN)
        fresh = line6 + at >= 6 * k
        pre_grad = grad * slope[pl.ds(at + 1, 6)].reshape(192, 512)
        pre_grad = jnp.where(fresh, pre_grad, 0.0).astype(BF16)
        own = cext[pl.ds(at + 4, 6), :, 0:512].reshape(192, 512)
        own = jnp.where(fresh, own.astype(F32), 0.0).astype(BF16)
        for v in range(3):
            sum_two[v] += dot(own, h_shift[v, pl.ds(at, 8)].reshape(256, 512), NT)
            if v == 1:
                layer = lext[rows, :, 0:512]
            else:
                layer = l_shift[v // 2, rows, :, 0:512]
            sum_one[v] += dot(pre_grad, layer.reshape(256, 512), NT)
        return 0

    lax.fori_loop(0, 6, backward, 0)
    for n, sums in enumerate((sum_one, sum_two)):
        for v in range(3):
            total = jnp.zeros((32, 256), F32)
            for r in range(6):
                value = sums[v, 32 * r : 32 * r + 32, :]
                total = total + (pltpu.roll(value, 256 - 32 * r, 1) if r else value)
            at = 96 * n + 32 * v
            grads[at : at + 32, :] = total[:, 0:128]


def shifted(value, by):
    if by > 0:
        return jnp.concatenate([value[:, 640 - by :], value[:, : 640 - by]], axis=1)
    return jnp.concatenate([value[:, -by:], value[:, :-by]], axis=1)


def sum_kernel(
    n_row, n_col, scale, grads,
    out_one, out_two,
    mine, row_in, chunk, col_in, done, total, r_send, r_recv, c_send, c_recv, g_send, g_recv,
):
    i = lax.axis_index("row")
    j = lax.axis_index("col")
    size = mine.shape[1]
    owners = 192 // size
    barrier, count = greet(i, j, n_row, n_col, False)
    mine[...] = grads[...].reshape(owners, size, 128)
    pl.semaphore_wait(barrier, count)

    def r_copy(d):
        to = (i + d) % n_row
        return to, remote(
            mine.at[jnp.minimum(to, owners - 1)], row_in.at[i], r_send.at[d], r_recv.at[d], to, j
        )

    def c_copy(d):
        return remote(chunk, col_in.at[j], c_send.at[d], c_recv.at[d], i, (j + d) % n_col)

    def g_copy(d):
        return remote(
            done, total.at[jnp.minimum(i, owners - 1)], g_send.at[d], g_recv.at[d], (i + d) % n_row, j
        )

    def over_row(step):
        def one(d, _):
            step(d)
            return 0

        lax.fori_loop(1, n_row, one, 0)

    def send_piece(d):
        to, copy = r_copy(d)

        @pl.when(to < owners)
        def _():
            copy.start()

    def piece_left(d):
        to, copy = r_copy(d)

        @pl.when(to < owners)
        def _():
            copy.wait_send()

    over_row(send_piece)

    @pl.when(i < owners)
    def _():
        row_in[i] = mine[i]
        over_row(lambda d: r_copy(d)[1].wait_recv())
        value = row_in[0]
        for k in range(1, n_row):
            value = value + row_in[k]
        chunk[...] = value
        for d in range(1, n_col):
            c_copy(d).start()
        col_in[j] = value
        for d in range(1, n_col):
            c_copy(d).wait_recv()
        value = col_in[0]
        for k in range(1, n_col):
            value = value + col_in[k]
        value = value * scale
        done[...] = value
        total[i] = value
        over_row(lambda d: g_copy(d).start())
        for d in range(1, n_col):
            c_copy(d).wait_send()
        over_row(lambda d: g_copy(d).wait_send())

    def from_owner(d):
        source = (i + n_row - d) % n_row

        @pl.when(source < owners)
        def _():
            g_copy(d).wait_recv()

    over_row(from_owner)
    over_row(piece_left)
    value = total[...].reshape(192, 128)
    for n, out in enumerate((out_one, out_two)):
        for v in range(3):
            at = 96 * n + 32 * v
            for u in range(3):
                out[3 * u + v] = value[at : at + 32, 32 * u : 32 * u + 32]


def body(n_row, n_col, features, mask, mask_gain, conv_one, conv_two, spec_real, spec_imag, cotangent):
    total_rows, total_cols = 32 * n_row, 512 * n_col
    scaling = 1.0 / math.sqrt((total_rows // RATIO) * (total_cols // RATIO))
    vmem = pl.BlockSpec(memory_space=pltpu.VMEM)
    hbm = pl.BlockSpec(memory_space=pl.ANY)
    col_tab = jnp.asarray(column_tables(n_col))
    row_tab = jnp.asarray(row_tables(n_row))
    dma = pltpu.SemaphoreType.DMA
    lext, cext, high, low, g_real, g_imag = pl.pallas_call(
        functools.partial(exchange_kernel, n_row, n_col, scaling),
        out_shape=[
            jax.ShapeDtypeStruct((40, 32, 640), BF16),
            jax.ShapeDtypeStruct((40, 32, 640), BF16),
            jax.ShapeDtypeStruct((192, 512), BF16),
            jax.ShapeDtypeStruct((192, 512), BF16),
            jax.ShapeDtypeStruct((8, 32, 32), F32),
            jax.ShapeDtypeStruct((8, 32, 32), F32),
        ],
        in_specs=[vmem] * 6 + [hbm] * 2,
        out_specs=[vmem] * 6,
        scratch_shapes=[
            pltpu.VMEM((10, 32, 512), F32),
            pltpu.VMEM((2, 64, 512), F32),
            pltpu.SMEM(row_tab.shape[1:], F32),
            pltpu.VMEM((64, 384), F32),
            pltpu.VMEM((n_col, 16, 384), F32),
            pltpu.VMEM((n_row, 8, 128), F32),
            pltpu.VMEM((n_row, 8, 128), F32),
            pltpu.VMEM((8, 128), F32),
            pltpu.VMEM((n_row, 8, 128), F32),
            pltpu.VMEM((16, 256), F32),
            pltpu.VMEM((n_col, 16, 256), F32),
            pltpu.VMEM((4, 1024), F32),
            pltpu.VMEM((4, 1024), F32),
            pltpu.VMEM((2, 4, 1280), F32),
            pltpu.VMEM((2, 2, 32, 512), BF16),
            pltpu.VMEM((2, 1, 32, 512), BF16),
            dma((2,)),
            dma((10,)),
            dma((10,)),
            dma((n_col,)),
            dma((n_col,)),
            dma((n_row,)),
            dma((n_row,)),
            dma((n_row,)),
            dma((n_row,)),
            dma((n_col,)),
            dma((n_col,)),
        ],
        compiler_params=pltpu.CompilerParams(
            collective_id=0, has_side_effects=True, vmem_limit_bytes=VMEM_LIMIT
        ),
        name="exchange",
    )(features, mask, mask_gain[:, None], cotangent, spec_real, spec_imag, col_tab, row_tab)

    output, grads = pl.pallas_call(
        conv_kernel,
        out_shape=[
            jax.ShapeDtypeStruct((32, 32, 512), BF16),
            jax.ShapeDtypeStruct((192, 128), F32),
        ],
        in_specs=[vmem] * 8,
        out_specs=[vmem] * 2,
        scratch_shapes=[
            pltpu.VMEM((2, 40, 32, 640), BF16),
            pltpu.VMEM((2, 40, 32, 512), BF16),
            pltpu.VMEM((3, 34, 32, 512), BF16),
            pltpu.VMEM((34, 32, 512), F32),
            pltpu.VMEM((3, 192, 256), BF16),
            pltpu.VMEM((3, 256, 320), BF16),
            pltpu.VMEM((3, 192, 256), BF16),
            pltpu.VMEM((3, 192, 256), F32),
            pltpu.VMEM((3, 192, 256), F32),
        ],
        compiler_params=pltpu.CompilerParams(vmem_limit_bytes=VMEM_LIMIT),
        name="convolve",
    )(
        lext, cext, high, low, conv_one, conv_two,
        jnp.asarray(expand_table(), BF16), jnp.asarray(prolong_table(), BF16),
    )

    size = 8 * max(1, 24 // n_row)
    owners = 192 // size
    grad_one, grad_two = pl.pallas_call(
        functools.partial(sum_kernel, n_row, n_col, 1.0 / math.sqrt(total_rows * total_cols)),
        out_shape=[jax.ShapeDtypeStruct((9, 32, 32), F32)] * 2,
        in_specs=[vmem],
        out_specs=[vmem] * 2,
        scratch_shapes=[
            pltpu.VMEM((owners, size, 128), F32),
            pltpu.VMEM((n_row, size, 128), F32),
            pltpu.VMEM((size, 128), F32),
            pltpu.VMEM((n_col, size, 128), F32),
            pltpu.VMEM((size, 128), F32),
            pltpu.VMEM((owners, size, 128), F32),
            dma((n_row,)),
            dma((n_row,)),
            dma((n_col,)),
            dma((n_col,)),
            dma((n_row,)),
            dma((n_row,)),
        ],
        compiler_params=pltpu.CompilerParams(
            collective_id=1, has_side_effects=True, vmem_limit_bytes=VMEM_LIMIT
        ),
        name="total",
    )(grads)
    return output, grad_one, grad_two, g_real, g_imag


def solution(mesh):
    n_row, n_col = mesh.shape["row"], mesh.shape["col"]
    placed = (
        P(None, "row", "col"),
        P("row", "col"),
        P(),
        P(),
        P(),
        P(("row", "col"), None, None),
        P(("row", "col"), None, None),
        P(None, "row", "col"),
    )
    return jax.shard_map(
        functools.partial(body, n_row, n_col),
        mesh=mesh,
        in_specs=placed,
        out_specs=(
            P(None, "row", "col"),
            P(),
            P(),
            P(("row", "col"), None, None),
            P(("row", "col"), None, None),
        ),
        check_vma=False,
    )
```

```python
import functools
import math

import jax
import jax.numpy as jnp
import numpy as np
from jax import lax
from jax.experimental import pallas as pl
from jax.experimental.pallas import tpu as pltpu
from jax.sharding import PartitionSpec as P

C = 32
M = 32
RATIO = 8
MESH = pl.DeviceIdType.MESH
HIGH = lax.Precision.HIGHEST
F32 = jnp.float32
BF16 = jnp.bfloat16
GELU_A = math.sqrt(2.0 / math.pi)
GELU_B = 0.044715
VMEM_LIMIT = 56 * 2**20
NT = (((1,), (1,)), ((), ()))
TN = (((0,), (0,)), ((), ()))
NN = (((1,), (0,)), ((), ()))


def dot(a, b, dims, precision=None):
    return lax.dot_general(a, b, dims, preferred_element_type=F32, precision=precision)


def weights_np():
    d = (np.arange(RATIO) + 0.5 - RATIO / 2) / RATIO
    return np.stack([np.maximum(-d, 0.0), 1.0 - np.abs(d), np.maximum(d, 0.0)])


def column_tables(n_col):
    w = weights_np()
    n_two = 64 * n_col
    r = np.arange(M)
    out = np.zeros((n_col, 2, 64, 512))
    for j in range(n_col):
        fine = np.arange(512)
        cell, s = 64 * j + fine // RATIO, fine % RATIO

        def wave(at):
            return np.exp(-2j * np.pi * ((r[:, None] * at[None, :]) % n_two) / n_two)

        mean = wave(cell) / 64.0
        restrict = sum(w[b + 1][s][None, :] * wave(cell + b) for b in (-1, 0, 1))
        for kind, value in enumerate((mean, restrict)):
            parts = np.stack([value.real, value.imag], axis=0).reshape(2, 4, 8, 512)
            out[j, kind] = parts.transpose(1, 0, 2, 3).reshape(64, 512)
    return out.astype(np.float32)


def row_tables(n_row):
    n_z = n_row // 4
    peers = np.arange(n_row).reshape(2, n_z, 2).transpose(1, 0, 2).reshape(-1)
    n_one = 4 * n_row
    q_all = np.arange(2 * n_row)
    f1 = np.where(q_all < n_row, q_all, n_one - 2 * n_row + q_all)
    out = np.zeros((2 * n_row, n_row, 16))
    for i in range(n_row):
        for h in range(2):
            q = 2 * peers + h
            for kk in range(6):
                phase = 2 * np.pi * ((f1[q] * (4 * i + kk - 1)) % n_one) / n_one
                out[2 * i + h, :, 2 * kk] = np.cos(phase)
                out[2 * i + h, :, 2 * kk + 1] = np.sin(phase)
    out = out.reshape(2 * n_row, n_row * 16)
    out = np.pad(out, ((0, 0), (0, -out.shape[1] % 128)))
    return out.reshape(2 * n_row, -1, 128).astype(np.float32)


def prolong_table():
    w = weights_np()
    out = np.zeros((C, RATIO, 3, C))
    for c in range(C):
        out[c, :, :, c] = w.T
    return out.reshape(C * RATIO, 3 * C).astype(np.float32)


def expand_table():
    return np.repeat(np.eye(C), RATIO, axis=0).astype(np.float32)


def lane_group(shape):
    return lax.broadcasted_iota(jnp.int32, shape, len(shape) - 1) // 32


def place(value, source, target):
    shift = (32 * (target - source)) % 128
    moved = pltpu.roll(value, shift, 1) if shift else value
    return jnp.where(lane_group(value.shape) == target, moved, 0.0)


def everywhere(value):
    value = value + pltpu.roll(value, 64, 1)
    return value + pltpu.roll(value, 32, 1)


def remote(src, dst, send, recv, row, col):
    return pltpu.make_async_remote_copy(
        src_ref=src,
        dst_ref=dst,
        send_sem=send,
        recv_sem=recv,
        device_id=(row, col),
        device_id_type=MESH,
    )


def remote_to(plan, send, recv):
    return [
        remote(src, dst, send.at[n], recv.at[n], row, col)
        for n, (src, dst, row, col) in enumerate(plan)
    ]


def begin(copies):
    for copy in copies:
        copy.start()


def arrive(copies):
    for copy in copies:
        copy.wait_recv()


def leave(copies):
    for copy in copies:
        copy.wait_send()


def prepare(feat, mask, gain, cot, lext, cext, field, ready):
    w = weights_np()
    for half in range(2):
        ready[half]()

        def tile(t, _, half=half):
            lanes = pl.ds(pl.multiple_of(t * 128, 128), 128)
            rows = pl.ds(16 * half, 16)
            raised = mask[rows, lanes].astype(F32) - 0.5
            layer = jnp.stack(
                [feat[c, rows, lanes].astype(F32) + gain[c] * raised for c in range(C)]
            )
            layer = layer.astype(BF16).astype(F32)
            layer = jnp.swapaxes(layer, 0, 1)
            lext[pl.ds(4 + 16 * half, 16), :, lanes] = layer.astype(BF16)
            grad = jnp.swapaxes(cot[:, rows, lanes].astype(F32), 0, 1)
            cext[pl.ds(4 + 16 * half, 16), :, lanes] = grad.astype(BF16)
            sums = [None] * 4
            for cell in range(2):
                total = layer[8 * cell]
                for p in range(1, 8):
                    total = total + layer[8 * cell + p]
                field[2 * half + cell, :, lanes] = total
                for p in range(8):
                    for a in (-1, 0, 1):
                        weight = float(w[a + 1][p])
                        if weight == 0.0:
                            continue
                        term = grad[8 * cell + p] * weight
                        at = cell + a + 1
                        sums[at] = term if sums[at] is None else sums[at] + term
            for at in range(4):
                slot = 4 + 2 * half + at
                if half == 1 and at < 2:
                    field[slot, :, lanes] = field[slot, :, lanes] + sums[at]
                else:
                    field[slot, :, lanes] = sums[at]
            return 0

        lax.fori_loop(0, 4, tile, 0)


def pick(shape, pairs):
    row = lax.broadcasted_iota(jnp.int32, shape, 0)
    lane = lax.broadcasted_iota(jnp.int32, shape, 1)
    hit = jnp.zeros(shape, jnp.bool_)
    for r, l in pairs:
        hit = hit | ((row == r) & (lane == l))
    return jnp.where(hit, 1.0, 0.0).astype(BF16)


def tiled(value):
    wide = jnp.concatenate([value, jnp.zeros((32, 96), value.dtype)], axis=1)
    return everywhere(wide)


def shifted(value, by):
    if by > 0:
        return jnp.concatenate([value[:, 640 - by :], value[:, : 640 - by]], axis=1)
    return jnp.concatenate([value[:, -by:], value[:, :-by]], axis=1)


def main_kernel(
    n_row, n_col, scaling, scale,
    feat_h, mask_h, gain, cot_h, real_h, imag_h, one_h, two_h, spread_h, stretch_h, col_tab, row_tab,
    stage, total_out, outer_out,
    feat, mask, cot, w_real, w_imag, w_one, w_two, spread, stretch,
    lext, cext, high, low, field, tab, twiddle,
    share, share_in, part, part_z, quad_sum, part_q, quad, mixed_in, folded, folded_in,
    left, right, side_in, rows_in, row_c_in,
    l_shift, c_shift, h_shift, slope, band_one, band_two, band_back, sum_one, sum_two,
    mine, sum_c, chunk_c, sum_q, chunk_q, sum_z, done, gathered,
    local_sem, halo_send, halo_recv, a_send, a_recv, bz_send, bz_recv, bq_send, bq_recv,
    cq_send, cq_recv, cz_send, cz_recv, d_send, d_recv,
    r_send, r_recv, rq_send, rq_recv, rz_send, rz_recv, g_send, g_recv,
):
    i = lax.axis_index("row")
    j = lax.axis_index("col")
    half = j // 4
    n_z = n_row // 4
    y, z, core = i // (2 * n_z), (i // 2) % n_z, i % 2
    quarter = 2 * y + core
    up, down = (i + n_row - 1) % n_row, (i + 1) % n_row
    west, east = (j + n_col - 1) % n_col, (j + 1) % n_col
    cols = [(j + d) % n_col for d in range(1, n_col)]
    levels = [(z + d) % n_z for d in range(1, n_z)]
    quarters = [(y, 1 - core), (1 - y, core), (1 - y, 1 - core)]

    def row_at(y, z, core):
        return (y * n_z + z) * 2 + core

    loads = [
        pltpu.make_async_copy(src, dst, local_sem.at[n])
        for n, (src, dst) in enumerate(
            (
                (mask_h, mask),
                (feat_h.at[:, 0:16], feat.at[:, 0:16]),
                (cot_h.at[:, 0:16], cot.at[:, 0:16]),
                (feat_h.at[:, 16:32], feat.at[:, 16:32]),
                (cot_h.at[:, 16:32], cot.at[:, 16:32]),
                (col_tab.at[j], tab),
                (row_tab.at[2 * i + half], twiddle),
                (one_h, w_one),
                (two_h, w_two),
                (spread_h, spread),
                (stretch_h, stretch),
                (real_h, w_real),
                (imag_h, w_imag),
            )
        )
    ]
    begin(loads)

    barrier = pltpu.get_barrier_semaphore()
    partners = (
        [(i, c) for c in cols]
        + [(row_at(y, l, core), j) for l in levels]
        + [(row_at(a, z, b), j) for a, b in quarters]
        + [(r, c) for r in (up, down) for c in (j, west, east)]
    )
    for partner in partners:
        pl.semaphore_signal(barrier, inc=1, device_id=partner, device_id_type=MESH)

    def first_half():
        for load in loads[0:3]:
            load.wait()

    def second_half():
        for load in loads[3:5]:
            load.wait()

    prepare(feat, mask, gain, cot, lext, cext, field, (first_half, second_half))

    loads[5].wait()
    share[:, 0:128] = dot(tab[0], field[0:4].reshape(128, 512), NT, HIGH)
    share[:, 128:320] = dot(tab[1], field[4:10].reshape(192, 512), NT, HIGH)
    share[:, 320:384] = jnp.zeros((64, 64), F32)
    pl.semaphore_wait(barrier, len(partners))

    def group(c):
        return pl.ds(pl.multiple_of(16 * (c % 4), 16), 16)

    a_copies = remote_to([(share.at[group(c)], share_in.at[j], i, c) for c in cols], a_send, a_recv)
    begin(a_copies)
    share_in[j] = share[group(j), :]

    first_l = lext[4:36, :, 0:128].reshape(1024, 128)
    last_l = lext[4:36, :, 384:512].reshape(1024, 128)
    first_c = cext[4:36, :, 0:128].reshape(1024, 128)
    last_c = cext[4:36, :, 384:512].reshape(1024, 128)
    sel = (16, 128)
    left[...] = (
        dot(pick(sel, ((0, 0), (1, 1))), first_l, NT) + dot(pick(sel, ((2, 0),)), first_c, NT)
    )[0:4]
    right[...] = (
        dot(pick(sel, ((0, 126), (1, 127))), last_l, NT) + dot(pick(sel, ((2, 127),)), last_c, NT)
    )[0:4]
    plan = [
        (lext.at[4:6, :, 0:512], rows_in.at[1], up, j),
        (lext.at[34:36, :, 0:512], rows_in.at[0], down, j),
        (cext.at[4:5, :, 0:512], row_c_in.at[1], up, j),
        (cext.at[35:36, :, 0:512], row_c_in.at[0], down, j),
        (left, side_in.at[1, :, 128:1152], i, west),
        (right, side_in.at[0, :, 128:1152], i, east),
        (left.at[:, 0:128], side_in.at[1, :, 1152:1280], up, west),
        (right.at[:, 0:128], side_in.at[0, :, 1152:1280], up, east),
        (left.at[:, 896:1024], side_in.at[1, :, 0:128], down, west),
        (right.at[:, 896:1024], side_in.at[0, :, 0:128], down, east),
    ]
    halos = remote_to(plan, halo_send, halo_recv)
    begin(halos)

    for load in loads[6:]:
        load.wait()
    eye = jnp.where(
        lax.broadcasted_iota(jnp.int32, (32, 32), 0) == lax.broadcasted_iota(jnp.int32, (32, 32), 1),
        1.0,
        0.0,
    ).astype(BF16)
    block = lane_group((32, 256))
    line = lax.broadcasted_iota(jnp.int32, (256, 384), 0) % 8
    wide_block = lane_group((256, 384))
    for v in range(3):
        ones, backs, twos = [], [], []
        for u in range(3):
            one = tiled(w_one[3 * u + v].astype(F32))
            ones.append(jnp.concatenate([one, one], axis=1))
            back = tiled(dot(eye, w_two[3 * u + v], NT))
            backs.append(jnp.concatenate([back, back], axis=1))
            two = tiled(w_two[3 * u + v].astype(F32))
            twos.append(jnp.concatenate([two, two, two], axis=1).astype(BF16))
        for r in range(6):
            one = jnp.zeros((32, 256), F32)
            back = jnp.zeros((32, 256), F32)
            for u in range(3):
                one = one + jnp.where(block == r + u, ones[u], 0.0)
                back = back + jnp.where(block == r + 2 - u, backs[u], 0.0)
            band_one[v, 32 * r : 32 * r + 32, :] = one.astype(BF16)
            band_back[v, 32 * r : 32 * r + 32, :] = back.astype(BF16)
        total = jnp.zeros((256, 384), F32)
        for u in range(3):
            total = total + jnp.where(
                wide_block - line == u, dot(spread[...], twos[u], NN), 0.0
            )
        band_two[v] = total[:, 0:320].astype(BF16)

    arrive(halos)
    lext[2:4, :, 0:512] = rows_in[0]
    lext[36:38, :, 0:512] = rows_in[1]
    cext[3:4, :, 0:512] = row_c_in[0]
    cext[36:37, :, 0:512] = row_c_in[1]
    sides = jnp.concatenate([side_in[0], side_in[1]], axis=0).astype(BF16)
    at_l = pick((8, 128), ((0, 126), (1, 127), (4, 0), (5, 1)))
    at_c = pick((8, 128), ((2, 127), (6, 0)))
    lext[:, :, 512:640] = dot(sides, at_l, TN).astype(BF16).reshape(40, 32, 128)
    cext[:, :, 512:640] = dot(sides, at_c, TN).astype(BF16).reshape(40, 32, 128)

    def move(k, _):
        rows = pl.ds(2 + 4 * k, 4)
        value = lext[rows].reshape(128, 640)
        l_shift[0, rows] = shifted(value, 1).reshape(4, 32, 640)
        l_shift[1, rows] = shifted(value, -1).reshape(4, 32, 640)
        value = cext[rows].reshape(128, 640)
        c_shift[0, rows] = shifted(value, 1)[:, 0:512].reshape(4, 32, 512)
        c_shift[1, rows] = shifted(value, -1)[:, 0:512].reshape(4, 32, 512)
        return 0

    lax.fori_loop(0, 9, move, 0)

    def forward(k, _):
        at = jnp.minimum(6 * k, 28)
        rows = pl.ds(at + 2, 8)
        pre = dot(band_one[1], lext[rows].reshape(256, 640), NN)
        pre = pre + dot(band_one[0], l_shift[0, rows].reshape(256, 640), NN)
        pre = pre + dot(band_one[2], l_shift[1, rows].reshape(256, 640), NN)
        square = pre * pre
        bend = jnp.tanh(GELU_A * (pre + GELU_B * (square * pre)))
        half = 0.5 * (1.0 + bend)
        hidden = (pre * half).astype(BF16)
        rise = half + 0.5 * pre * (1.0 - bend * bend) * (GELU_A * (1.0 + 3.0 * GELU_B * square))
        slope[pl.ds(at, 6)] = rise[:, 0:512].reshape(6, 32, 512)
        to = pl.ds(at, 6)
        h_shift[1, to] = hidden[:, 0:512].reshape(6, 32, 512)
        h_shift[0, to] = shifted(hidden, 1)[:, 0:512].reshape(6, 32, 512)
        h_shift[2, to] = shifted(hidden, -1)[:, 0:512].reshape(6, 32, 512)
        return 0

    lax.fori_loop(0, 3, forward, 0)

    arrive(a_copies)
    total_a = share_in[0]
    for k in range(1, n_col):
        total_a = total_a + share_in[k]
    ps, qs = [], []
    for kk in range(6):
        re, im = [], []
        for out, rows in ((re, slice(0, 8)), (im, slice(8, 16))):
            if 1 <= kk <= 4:
                out.append((total_a[rows, 0:128], kk - 1, 0))
            at = 128 + 32 * kk
            tile = at // 128
            out.append((total_a[rows, 128 * tile : 128 * tile + 128], (at % 128) // 32, 1))
        p_sum = jnp.zeros((8, 128), F32)
        q_sum = jnp.zeros((8, 128), F32)
        for value, source, kind in re:
            p_sum = p_sum + place(value, source, kind)
            q_sum = q_sum - place(value, source, kind + 2)
        for value, source, kind in im:
            p_sum = p_sum + place(value, source, kind + 2)
            q_sum = q_sum + place(value, source, kind)
        ps.append(p_sum)
        qs.append(q_sum)

    def factor(q, n):
        at = q * 16 + n
        return twiddle[at // 128, at % 128]

    def row_transform(q, _):
        out = jnp.zeros((8, 128), F32)
        for kk in range(6):
            out = out + factor(q, 2 * kk) * ps[kk] + factor(q, 2 * kk + 1) * qs[kk]
        part[q] = out
        return 0

    lax.fori_loop(0, n_row, row_transform, 0)

    def four(z):
        return pl.ds(pl.multiple_of(4 * z, 4), 4)

    bz_copies = remote_to(
        [(part.at[four(l)], part_z.at[z], row_at(y, l, core), j) for l in levels], bz_send, bz_recv
    )
    begin(bz_copies)
    part_z[z] = part[four(z)]
    lax.fori_loop(3, 6, forward, 0)
    arrive(bz_copies)
    value = part_z[0]
    for k in range(1, n_z):
        value = value + part_z[k]
    quad_sum[...] = value
    bq_copies = remote_to(
        [(quad_sum.at[2 * a + b], part_q.at[quarter], row_at(a, z, b), j) for a, b in quarters],
        bq_send, bq_recv,
    )
    begin(bq_copies)
    part_q[quarter] = quad_sum[quarter]
    sum_one[...] = jnp.zeros_like(sum_one)
    sum_two[...] = jnp.zeros_like(sum_two)
    line6 = lax.broadcasted_iota(jnp.int32, (192, 512), 0) // 32

    def backward(k, _):
        at = jnp.minimum(6 * k, 26)
        rows = pl.ds(at + 3, 8)
        grad = dot(band_back[1], cext[rows, :, 0:512].reshape(256, 512), NN)
        grad = grad + dot(band_back[0], c_shift[1, rows].reshape(256, 512), NN)
        grad = grad + dot(band_back[2], c_shift[0, rows].reshape(256, 512), NN)
        fresh = line6 + at >= 6 * k
        pre_grad = grad * slope[pl.ds(at + 1, 6)].reshape(192, 512)
        pre_grad = jnp.where(fresh, pre_grad, 0.0).astype(BF16)
        own = cext[pl.ds(at + 4, 6), :, 0:512].reshape(192, 512)
        own = jnp.where(fresh, own.astype(F32), 0.0).astype(BF16)
        for v in range(3):
            sum_two[v] += dot(own, h_shift[v, pl.ds(at, 8)].reshape(256, 512), NT)
            if v == 1:
                layer = lext[rows, :, 0:512]
            else:
                layer = l_shift[v // 2, rows, :, 0:512]
            sum_one[v] += dot(pre_grad, layer.reshape(256, 512), NT)
        return 0

    lax.fori_loop(0, 1, backward, 0)
    arrive(bq_copies)
    spectrum = part_q[0] + part_q[1] + part_q[2] + part_q[3]

    groups = lane_group((8, 128))
    row = lax.broadcasted_iota(jnp.int32, (8, 128), 0)
    first = (row == 0) & (j % 4 == 0)
    twice = jnp.where(first, 1.0, 2.0)
    spectrum = spectrum * jnp.where(groups % 2 == 1, twice * scaling, scaling)
    s_re = everywhere(jnp.where(groups == 0, spectrum, 0.0))
    m_re = everywhere(jnp.where(groups == 1, spectrum, 0.0))
    s_im = everywhere(jnp.where(groups == 2, spectrum, 0.0))
    m_im = everywhere(jnp.where(groups == 3, spectrum, 0.0))
    wide = lane_group((16, 256)) == lax.broadcasted_iota(jnp.int32, (16, 256), 0) % 8
    both = jnp.concatenate([s_re, s_im], axis=0)[:, 0:32]
    by_real = jnp.where(wide, dot(both, w_real[...].reshape(256, 32).astype(F32), NT, HIGH), 0.0)
    by_imag = jnp.where(wide, dot(both, w_imag[...].reshape(256, 32).astype(F32), NT, HIGH), 0.0)
    mixed_re = by_real[0:8] - by_imag[8:16]
    mixed_im = by_real[8:16] + by_imag[0:8]
    mixed_re = everywhere(mixed_re[:, 0:128] + mixed_re[:, 128:256])
    mixed_im = everywhere(mixed_im[:, 0:128] + mixed_im[:, 128:256])
    quad[quarter] = jnp.where(
        groups == 1, mixed_im, jnp.where(groups == 2, -mixed_im, mixed_re)
    )

    cq_copies = remote_to(
        [(quad.at[quarter], quad.at[quarter], row_at(a, z, b), j) for a, b in quarters], cq_send, cq_recv
    )
    begin(cq_copies)
    grads = jnp.concatenate(
        [jnp.concatenate([m_re, m_re], axis=1), jnp.concatenate([m_im, m_im], axis=1)], axis=0
    )
    grads = jnp.where(wide, grads, 0.0)
    fields = jnp.concatenate(
        [jnp.where(groups == 0, s_re, -s_im), jnp.where(groups == 0, s_im, s_re)], axis=0
    )
    outer = dot(grads, fields, TN, HIGH)
    outer_out[...] = outer

    lax.fori_loop(1, 3, backward, 0)
    arrive(cq_copies)
    cz_copies = remote_to(
        [(quad, mixed_in.at[four(z)], row_at(y, l, core), j) for l in levels], cz_send, cz_recv
    )
    begin(cz_copies)
    mixed_in[four(z)] = quad[...]
    lax.fori_loop(3, 6, backward, 0)

    for n, sums in enumerate((sum_one, sum_two)):
        for v in range(3):
            total = jnp.zeros((32, 256), F32)
            for r in range(6):
                value = sums[v, 32 * r : 32 * r + 32, :]
                total = total + (pltpu.roll(value, 256 - 32 * r, 1) if r else value)
            for e in range(4):
                at = 12 * n + 4 * v + e
                mine[at // 3, 8 * (at % 3) : 8 * (at % 3) + 8, :] = total[8 * e : 8 * e + 8, 0:128]

    r_copies = remote_to([(mine.at[c], sum_c.at[j], i, c) for c in cols], r_send, r_recv)
    begin(r_copies)
    sum_c[j] = mine[j]

    arrive(cz_copies)
    def inverse(q, sums):
        value = mixed_in[q]
        out = []
        for kk in range(6):
            out.append(sums[2 * kk] + factor(q, 2 * kk) * value)
            out.append(sums[2 * kk + 1] + factor(q, 2 * kk + 1) * value)
        return tuple(out)

    zero = jnp.zeros((8, 128), F32)
    sums = lax.fori_loop(0, n_row, inverse, (zero,) * 12)
    grown = twice * scaling
    tiles = [zero] * 4
    for kk in range(6):
        value = (sums[2 * kk] + pltpu.roll(sums[2 * kk + 1], 64, 1)) * grown
        tiles[kk // 4] = tiles[kk // 4] + place(value, 0, kk % 4)
        tiles[2 + kk // 4] = tiles[2 + kk // 4] + place(value, 1, kk % 4)
    folded[0:8, 0:128] = tiles[0]
    folded[0:8, 128:256] = tiles[1]
    folded[8:16, 0:128] = tiles[2]
    folded[8:16, 128:256] = tiles[3]

    d_copies = remote_to([(folded, folded_in.at[j], i, c) for c in cols], d_send, d_recv)
    begin(d_copies)
    folded_in[j] = folded[...]

    arrive(r_copies)
    value = sum_c[0]
    for k in range(1, n_col):
        value = value + sum_c[k]
    chunk_c[...] = value
    rq_copies = remote_to(
        [(chunk_c, sum_q.at[quarter], row_at(a, z, b), j) for a, b in quarters], rq_send, rq_recv
    )
    begin(rq_copies)
    sum_q[quarter] = value

    arrive(d_copies)
    waves = (folded_in[0:4] + folded_in[4:8]).reshape(64, 256)
    smooth = dot(waves, tab[1], TN, HIGH)[0:192]
    upper = smooth.astype(BF16)
    high[...] = upper
    low[...] = (smooth - upper.astype(F32)).astype(BF16)

    arrive(rq_copies)
    value = sum_q[0] + sum_q[1] + sum_q[2] + sum_q[3]
    chunk_q[...] = value
    rz_copies = remote_to(
        [(chunk_q, sum_z.at[z], row_at(y, l, core), j) for l in levels], rz_send, rz_recv
    )
    begin(rz_copies)
    sum_z[z] = value

    def window(t):
        rows = pl.ds(8 * t, 10)
        coarse = pl.ds(pl.multiple_of(32 * t, 32), 96)
        total = dot(stretch[...], high[coarse, :], NN) + dot(stretch[...], low[coarse, :], NN)
        for v in range(3):
            total = total + dot(band_two[v], h_shift[v, rows].reshape(320, 512), NN)
        return total.reshape(32, 8, 512)

    def second(t, _):
        value = jnp.concatenate([window(2 * t), window(2 * t + 1)], axis=1)
        stage[:, pl.ds(pl.multiple_of(16 * t, 16), 16), :] = value.astype(BF16)
        return 0

    lax.fori_loop(0, 1, second, 0)
    arrive(rz_copies)
    value = sum_z[0]
    for k in range(1, n_z):
        value = value + sum_z[k]
    value = value * scale
    done[...] = value
    g_copies = remote_to([(done, gathered.at[j], i, c) for c in cols], g_send, g_recv)
    begin(g_copies)
    gathered[j] = value
    lax.fori_loop(1, 2, second, 0)
    for copies in (
        a_copies, halos, bz_copies, bq_copies, cq_copies, cz_copies, r_copies, d_copies, rq_copies, rz_copies
    ):
        leave(copies)
    arrive(g_copies)
    total_out[...] = gathered[...]
    leave(g_copies)


def finish_kernel(stage, total, outer, out, out_one, out_two, g_real, g_imag):
    out[...] = stage[...]
    value = total[...].reshape(192, 128)
    for n, grad in enumerate((out_one, out_two)):
        for v in range(3):
            at = 96 * n + 32 * v
            for u in range(3):
                grad[3 * u + v] = value[at : at + 32, 32 * u : 32 * u + 32]
    g_real[...] = outer[:, 0:32].reshape(8, 32, 32)
    g_imag[...] = outer[:, 32:64].reshape(8, 32, 32)


def body(n_row, n_col, features, mask, mask_gain, conv_one, conv_two, spec_real, spec_imag, cotangent):
    total_rows, total_cols = 32 * n_row, 512 * n_col
    scaling = 1.0 / math.sqrt((total_rows // RATIO) * (total_cols // RATIO))
    vmem = pl.BlockSpec(memory_space=pltpu.VMEM)
    hbm = pl.BlockSpec(memory_space=pl.ANY)
    col_tab = jnp.asarray(column_tables(n_col))
    row_tab = jnp.asarray(row_tables(n_row))
    spread = jnp.asarray(expand_table(), BF16)
    stretch = jnp.asarray(prolong_table(), BF16)
    n_z = n_row // 4
    dma = pltpu.SemaphoreType.DMA
    stage, total, outer = pl.pallas_call(
        functools.partial(
            main_kernel, n_row, n_col, scaling, 1.0 / math.sqrt(total_rows * total_cols)
        ),
        out_shape=[
            jax.ShapeDtypeStruct((32, 32, 512), BF16),
            jax.ShapeDtypeStruct((n_col, 24, 128), F32),
            jax.ShapeDtypeStruct((256, 128), F32),
        ],
        in_specs=[hbm] * 2 + [pl.BlockSpec(memory_space=pltpu.SMEM)] + [hbm] * 9,
        out_specs=[vmem] * 3,
        scratch_shapes=[
            pltpu.VMEM((32, 32, 512), BF16),
            pltpu.VMEM((32, 512), jnp.int32),
            pltpu.VMEM((32, 32, 512), BF16),
            pltpu.VMEM((8, 32, 32), BF16),
            pltpu.VMEM((8, 32, 32), BF16),
            pltpu.VMEM((9, 32, 32), BF16),
            pltpu.VMEM((9, 32, 32), BF16),
            pltpu.VMEM(spread.shape, BF16),
            pltpu.VMEM(stretch.shape, BF16),
            pltpu.VMEM((40, 32, 640), BF16),
            pltpu.VMEM((40, 32, 640), BF16),
            pltpu.VMEM((192, 512), BF16),
            pltpu.VMEM((192, 512), BF16),
            pltpu.VMEM((10, 32, 512), F32),
            pltpu.VMEM((2, 64, 512), F32),
            pltpu.SMEM(row_tab.shape[1:], F32),
            pltpu.VMEM((64, 384), F32),
            pltpu.VMEM((n_col, 16, 384), F32),
            pltpu.VMEM((n_row, 8, 128), F32),
            pltpu.VMEM((n_z, 4, 8, 128), F32),
            pltpu.VMEM((4, 8, 128), F32),
            pltpu.VMEM((4, 8, 128), F32),
            pltpu.VMEM((4, 8, 128), F32),
            pltpu.VMEM((n_row, 8, 128), F32),
            pltpu.VMEM((16, 256), F32),
            pltpu.VMEM((n_col, 16, 256), F32),
            pltpu.VMEM((4, 1024), F32),
            pltpu.VMEM((4, 1024), F32),
            pltpu.VMEM((2, 4, 1280), F32),
            pltpu.VMEM((2, 2, 32, 512), BF16),
            pltpu.VMEM((2, 1, 32, 512), BF16),
            pltpu.VMEM((2, 40, 32, 640), BF16),
            pltpu.VMEM((2, 40, 32, 512), BF16),
            pltpu.VMEM((3, 34, 32, 512), BF16),
            pltpu.VMEM((34, 32, 512), F32),
            pltpu.VMEM((3, 192, 256), BF16),
            pltpu.VMEM((3, 256, 320), BF16),
            pltpu.VMEM((3, 192, 256), BF16),
            pltpu.VMEM((3, 192, 256), F32),
            pltpu.VMEM((3, 192, 256), F32),
            pltpu.VMEM((n_col, 24, 128), F32),
            pltpu.VMEM((n_col, 24, 128), F32),
            pltpu.VMEM((24, 128), F32),
            pltpu.VMEM((4, 24, 128), F32),
            pltpu.VMEM((24, 128), F32),
            pltpu.VMEM((n_z, 24, 128), F32),
            pltpu.VMEM((24, 128), F32),
            pltpu.VMEM((n_col, 24, 128), F32),
            dma((13,)),
            dma((10,)),
            dma((10,)),
            *[dma((7,))] * 20,
        ],
        compiler_params=pltpu.CompilerParams(
            collective_id=0, has_side_effects=True, vmem_limit_bytes=VMEM_LIMIT
        ),
        name="layer",
    )(
        features, mask, mask_gain, cotangent, spec_real, spec_imag, conv_one, conv_two,
        spread, stretch, col_tab, row_tab,
    )
    return pl.pallas_call(
        finish_kernel,
        out_shape=[
            jax.ShapeDtypeStruct((32, 32, 512), BF16),
            jax.ShapeDtypeStruct((9, 32, 32), F32),
            jax.ShapeDtypeStruct((9, 32, 32), F32),
            jax.ShapeDtypeStruct((8, 32, 32), F32),
            jax.ShapeDtypeStruct((8, 32, 32), F32),
        ],
        in_specs=[vmem] * 3,
        out_specs=[vmem] * 5,
        name="finish",
    )(stage, total, outer)


def solution(mesh):
    n_row, n_col = mesh.shape["row"], mesh.shape["col"]
    placed = (
        P(None, "row", "col"),
        P("row", "col"),
        P(),
        P(),
        P(),
        P(("row", "col"), None, None),
        P(("row", "col"), None, None),
        P(None, "row", "col"),
    )
    return jax.shard_map(
        functools.partial(body, n_row, n_col),
        mesh=mesh,
        in_specs=placed,
        out_specs=(
            P(None, "row", "col"),
            P(),
            P(),
            P(("row", "col"), None, None),
            P(("row", "col"), None, None),
        ),
        check_vma=False,
    )
```

```python
import functools
import math

import jax
import jax.numpy as jnp
import ml_dtypes
import numpy as np
from jax import lax
from jax.experimental import pallas as pl
from jax.experimental.pallas import tpu as pltpu
from jax.sharding import PartitionSpec as P

C = 32
M = 32
RATIO = 8
MESH = pl.DeviceIdType.MESH
HIGH = lax.Precision.HIGHEST
F32 = jnp.float32
BF16 = jnp.bfloat16
GELU_A = math.sqrt(2.0 / math.pi)
GELU_B = 0.044715
VMEM_LIMIT = 56 * 2**20
NT = (((1,), (1,)), ((), ()))
TN = (((0,), (0,)), ((), ()))
NN = (((1,), (0,)), ((), ()))


def dot(a, b, dims, precision=None):
    return lax.dot_general(a, b, dims, preferred_element_type=F32, precision=precision)


def weights_np():
    d = (np.arange(RATIO) + 0.5 - RATIO / 2) / RATIO
    return np.stack([np.maximum(-d, 0.0), 1.0 - np.abs(d), np.maximum(d, 0.0)])


def column_tables(n_col):
    w = weights_np()
    n_two = 64 * n_col
    r = np.arange(M)
    out = np.zeros((n_col, 2, 64, 512))
    for j in range(n_col):
        fine = np.arange(512)
        cell, s = 64 * j + fine // RATIO, fine % RATIO

        def wave(at):
            return np.exp(-2j * np.pi * ((r[:, None] * at[None, :]) % n_two) / n_two)

        mean = wave(cell) / 64.0
        restrict = sum(w[b + 1][s][None, :] * wave(cell + b) for b in (-1, 0, 1))
        for kind, value in enumerate((mean, restrict)):
            parts = np.stack([value.real, value.imag], axis=0).reshape(2, 4, 8, 512)
            out[j, kind] = parts.transpose(1, 0, 2, 3).reshape(64, 512)
    out = out.astype(np.float32)
    upper = out.astype(ml_dtypes.bfloat16)
    lower = (out - upper.astype(np.float32)).astype(ml_dtypes.bfloat16)
    return np.concatenate([upper, lower], axis=2)


def row_tables(n_row):
    n_z = n_row // 4
    peers = np.arange(n_row).reshape(2, n_z, 2).transpose(1, 0, 2).reshape(-1)
    n_one = 4 * n_row
    q_all = np.arange(2 * n_row)
    f1 = np.where(q_all < n_row, q_all, n_one - 2 * n_row + q_all)
    out = np.zeros((2 * n_row, n_row, 16))
    for i in range(n_row):
        for h in range(2):
            q = 2 * peers + h
            for kk in range(6):
                phase = 2 * np.pi * ((f1[q] * (4 * i + kk - 1)) % n_one) / n_one
                out[2 * i + h, :, 2 * kk] = np.cos(phase)
                out[2 * i + h, :, 2 * kk + 1] = np.sin(phase)
    out = out.reshape(2 * n_row, n_z, 64)
    return np.pad(out, ((0, 0), (0, 0), (0, 64))).astype(np.float32)


def prolong_table():
    w = weights_np()
    out = np.zeros((C, RATIO, 3, C))
    for c in range(C):
        out[c, :, :, c] = w.T
    return out.reshape(C * RATIO, 3 * C).astype(np.float32)


def turn_table():
    w = weights_np()
    sums = np.zeros((2, C, C, 16))
    turn = np.zeros((16, C, C, 16))
    restrict = np.zeros((4, C, C, 16))
    for c in range(C):
        for row in range(16):
            cell, p = row // RATIO, row % RATIO
            sums[cell, c, c, row] = 1.0
            turn[row, c, c, row] = 1.0
            for a in (-1, 0, 1):
                restrict[cell + a + 1, c, c, row] = w[a + 1][p]
    return np.concatenate([t.reshape(-1, C * 16) for t in (sums, turn, restrict)], axis=0).astype(np.float32)


def expand_table():
    return np.repeat(np.eye(C), RATIO, axis=0).astype(np.float32)


def lane_group(shape):
    return lax.broadcasted_iota(jnp.int32, shape, len(shape) - 1) // 32


def place(value, source, target):
    shift = (32 * (target - source)) % 128
    moved = pltpu.roll(value, shift, 1) if shift else value
    return jnp.where(lane_group(value.shape) == target, moved, 0.0)


def everywhere(value):
    value = value + pltpu.roll(value, 64, 1)
    return value + pltpu.roll(value, 32, 1)


def remote(src, dst, send, recv, row, col):
    return pltpu.make_async_remote_copy(
        src_ref=src,
        dst_ref=dst,
        send_sem=send,
        recv_sem=recv,
        device_id=(row, col),
        device_id_type=MESH,
    )


def remote_to(plan, send, recv):
    return [
        remote(src, dst, send.at[n], recv.at[n], row, col)
        for n, (src, dst, row, col) in enumerate(plan)
    ]


def begin(copies):
    for copy in copies:
        copy.start()


def arrive(copies):
    for copy in copies:
        copy.wait_recv()


def leave(copies):
    for copy in copies:
        copy.wait_send()


def prepare(feat, mask, gain, cot, turn, lext, cext, field, ready):
    for half in range(2):
        ready[half]()
        rows = slice(16 * half, 16 * half + 16)
        to = slice(4 + 16 * half, 20 + 16 * half)
        raised = mask[rows, :].astype(F32) - 0.5
        for c in range(C):
            feat[c, rows, :] = (feat[c, rows, :].astype(F32) + gain[c] * raised).astype(BF16)
        turned = dot(turn[0:576], feat[:, rows, :].reshape(512, 512), NN)
        field[2 * half : 2 * half + 2] = turned[0:64].reshape(2, 32, 512)
        lext[to, :, 0:512] = turned[64:576].astype(BF16).reshape(16, 32, 512)
        turned = dot(turn[64:704], cot[:, rows, :].reshape(512, 512), NN)
        cext[to, :, 0:512] = turned[0:512].astype(BF16).reshape(16, 32, 512)
        sums = turned[512:640].reshape(4, 32, 512)
        if half == 0:
            field[4:8] = sums
        else:
            field[6:8] = field[6:8] + sums[0:2]
            field[8:10] = sums[2:4]


def parts_of(value, count):
    out = []
    for _ in range(count):
        part = value.astype(BF16)
        out.append(part)
        value = value - part.astype(F32)
    return out


def transform(table, value):
    upper, lower = parts_of(value, 2)
    whole = dot(table, upper, NT)
    return whole[0:64] + whole[64:128] + dot(table[0:64], lower, NT)


def pick(shape, pairs):
    row = lax.broadcasted_iota(jnp.int32, shape, 0)
    lane = lax.broadcasted_iota(jnp.int32, shape, 1)
    hit = jnp.zeros(shape, jnp.bool_)
    for r, l in pairs:
        hit = hit | ((row == r) & (lane == l))
    return jnp.where(hit, 1.0, 0.0).astype(BF16)


def tiled(value):
    wide = jnp.concatenate([value, jnp.zeros((32, 96), value.dtype)], axis=1)
    return everywhere(wide)


def shifted(value, by):
    if by > 0:
        return jnp.concatenate([value[:, 640 - by :], value[:, : 640 - by]], axis=1)
    return jnp.concatenate([value[:, -by:], value[:, :-by]], axis=1)


def main_kernel(
    n_row, n_col, scaling, scale,
    feat_h, mask_h, gain, cot_h, real_h, imag_h, one_h, two_h, spread_h, stretch_h, turn_h, col_tab, row_tab,
    stage_out, total_out, outer_out,
    feat, mask, cot, w_real, w_imag, w_one, w_two, spread, stretch, turn, stage,
    lext, cext, high, low, field, tab, twiddle,
    share, share_in, part, part_z, quad_sum, part_q, quad, mixed_in, folded, folded_in,
    left, right, side_in, rows_in, row_c_in,
    l_shift, c_shift, h_shift, slope, band_one, band_two, band_tail, band_back, sum_one, sum_two,
    mine, sum_c, chunk_c, sum_q, chunk_q, sum_z, done, gathered,
    local_sem, halo_send, halo_recv, a_send, a_recv, bz_send, bz_recv, bq_send, bq_recv,
    cq_send, cq_recv, cz_send, cz_recv, d_send, d_recv,
    r_send, r_recv, rq_send, rq_recv, rz_send, rz_recv, g_send, g_recv,
):
    i = lax.axis_index("row")
    j = lax.axis_index("col")
    half = j // 4
    n_z = n_row // 4
    y, z, core = i // (2 * n_z), (i // 2) % n_z, i % 2
    quarter = 2 * y + core
    up, down = (i + n_row - 1) % n_row, (i + 1) % n_row
    west, east = (j + n_col - 1) % n_col, (j + 1) % n_col
    cols = [(j + d) % n_col for d in range(1, n_col)]
    levels = [(z + d) % n_z for d in range(1, n_z)]
    quarters = [(y, 1 - core), (1 - y, core), (1 - y, 1 - core)]

    def row_at(y, z, core):
        return (y * n_z + z) * 2 + core

    loads = [
        pltpu.make_async_copy(src, dst, local_sem.at[n])
        for n, (src, dst) in enumerate(
            (
                (mask_h, mask),
                (feat_h.at[:, 0:16], feat.at[:, 0:16]),
                (turn_h, turn),
                (cot_h.at[:, 0:16], cot.at[:, 0:16]),
                (feat_h.at[:, 16:32], feat.at[:, 16:32]),
                (cot_h.at[:, 16:32], cot.at[:, 16:32]),
                (col_tab.at[j], tab),
                (row_tab.at[2 * i + half], twiddle),
                (one_h, w_one),
                (two_h, w_two),
                (spread_h, spread),
                (stretch_h, stretch),
                (real_h, w_real),
                (imag_h, w_imag),
            )
        )
    ]
    begin(loads)

    barrier = pltpu.get_barrier_semaphore()
    partners = (
        [(i, c) for c in cols]
        + [(row_at(y, l, core), j) for l in levels]
        + [(row_at(a, z, b), j) for a, b in quarters]
        + [(r, c) for r in (up, down) for c in (j, west, east)]
    )
    for partner in partners:
        pl.semaphore_signal(barrier, inc=1, device_id=partner, device_id_type=MESH)

    def first_half():
        for load in loads[0:4]:
            load.wait()

    def second_half():
        for load in loads[4:6]:
            load.wait()

    prepare(feat, mask, gain, cot, turn, lext, cext, field, (first_half, second_half))

    loads[6].wait()
    share[:, 0:128] = transform(tab[0], field[0:4].reshape(128, 512))
    share[:, 128:320] = transform(tab[1], field[4:10].reshape(192, 512))
    share[:, 320:384] = jnp.zeros((64, 64), F32)
    pl.semaphore_wait(barrier, len(partners))

    def group(c):
        return pl.ds(pl.multiple_of(16 * (c % 4), 16), 16)

    a_copies = remote_to([(share.at[group(c)], share_in.at[j], i, c) for c in cols], a_send, a_recv)
    begin(a_copies)
    share_in[j] = share[group(j), :]

    first_l = lext[4:36, :, 0:128].reshape(1024, 128)
    last_l = lext[4:36, :, 384:512].reshape(1024, 128)
    first_c = cext[4:36, :, 0:128].reshape(1024, 128)
    last_c = cext[4:36, :, 384:512].reshape(1024, 128)
    sel = (16, 128)
    left[...] = (
        dot(pick(sel, ((0, 0), (1, 1))), first_l, NT) + dot(pick(sel, ((2, 0),)), first_c, NT)
    )[0:4]
    right[...] = (
        dot(pick(sel, ((0, 126), (1, 127))), last_l, NT) + dot(pick(sel, ((2, 127),)), last_c, NT)
    )[0:4]
    plan = [
        (lext.at[4:6, :, 0:512], rows_in.at[1], up, j),
        (lext.at[34:36, :, 0:512], rows_in.at[0], down, j),
        (cext.at[4:5, :, 0:512], row_c_in.at[1], up, j),
        (cext.at[35:36, :, 0:512], row_c_in.at[0], down, j),
        (left, side_in.at[1, :, 128:1152], i, west),
        (right, side_in.at[0, :, 128:1152], i, east),
        (left.at[:, 0:128], side_in.at[1, :, 1152:1280], up, west),
        (right.at[:, 0:128], side_in.at[0, :, 1152:1280], up, east),
        (left.at[:, 896:1024], side_in.at[1, :, 0:128], down, west),
        (right.at[:, 896:1024], side_in.at[0, :, 0:128], down, east),
    ]
    halos = remote_to(plan, halo_send, halo_recv)
    begin(halos)

    for load in loads[7:]:
        load.wait()
    eye = jnp.where(
        lax.broadcasted_iota(jnp.int32, (32, 32), 0) == lax.broadcasted_iota(jnp.int32, (32, 32), 1),
        1.0,
        0.0,
    ).astype(BF16)
    block = lane_group((32, 256))
    line = lax.broadcasted_iota(jnp.int32, (256, 384), 0) % 8
    wide_block = lane_group((256, 384))
    for v in range(3):
        ones, backs, twos = [], [], []
        for u in range(3):
            one = tiled(w_one[3 * u + v].astype(F32))
            ones.append(jnp.concatenate([one, one], axis=1))
            back = tiled(dot(eye, w_two[3 * u + v], NT))
            backs.append(jnp.concatenate([back, back], axis=1))
            two = tiled(w_two[3 * u + v].astype(F32))
            twos.append(jnp.concatenate([two, two, two], axis=1).astype(BF16))
        for r in range(6):
            one = jnp.zeros((32, 256), F32)
            back = jnp.zeros((32, 256), F32)
            for u in range(3):
                one = one + jnp.where(block == r + u, ones[u], 0.0)
                back = back + jnp.where(block == r + 2 - u, backs[u], 0.0)
            band_one[v, 32 * r : 32 * r + 32, :] = one.astype(BF16)
            band_back[v, 32 * r : 32 * r + 32, :] = back.astype(BF16)
        total = jnp.zeros((256, 384), F32)
        for u in range(3):
            total = total + jnp.where(
                wide_block - line == u, dot(spread[...], twos[u], NN), 0.0
            )
        band_two[v] = total[:, 0:256].astype(BF16)
        band_tail[:, 64 * v : 64 * v + 64] = total[:, 256:320].astype(BF16)
    band_tail[:, 192:288] = stretch[...]
    band_tail[:, 288:384] = stretch[...]

    arrive(halos)
    lext[2:4, :, 0:512] = rows_in[0]
    lext[36:38, :, 0:512] = rows_in[1]
    cext[3:4, :, 0:512] = row_c_in[0]
    cext[36:37, :, 0:512] = row_c_in[1]
    sides = jnp.concatenate([side_in[0], side_in[1]], axis=0).astype(BF16)
    at_l = pick((8, 128), ((0, 126), (1, 127), (4, 0), (5, 1)))
    at_c = pick((8, 128), ((2, 127), (6, 0)))
    lext[:, :, 512:640] = dot(sides, at_l, TN).astype(BF16).reshape(40, 32, 128)
    cext[:, :, 512:640] = dot(sides, at_c, TN).astype(BF16).reshape(40, 32, 128)

    def move(k):
        rows = pl.ds(2 + 4 * k, 4)
        value = lext[rows].reshape(128, 640)
        l_shift[0, rows] = shifted(value, 1).reshape(4, 32, 640)
        l_shift[1, rows] = shifted(value, -1).reshape(4, 32, 640)
        value = cext[rows].reshape(128, 640)
        c_shift[0, rows] = shifted(value, 1)[:, 0:512].reshape(4, 32, 512)
        c_shift[1, rows] = shifted(value, -1)[:, 0:512].reshape(4, 32, 512)

    for k in range(9):
        move(k)

    arrive(a_copies)
    total_a = share_in[0]
    for k in range(1, n_col):
        total_a = total_a + share_in[k]
    ps, qs = [], []
    for kk in range(6):
        re, im = [], []
        for out, rows in ((re, slice(0, 8)), (im, slice(8, 16))):
            if 1 <= kk <= 4:
                out.append((total_a[rows, 0:128], kk - 1, 0))
            at = 128 + 32 * kk
            tile = at // 128
            out.append((total_a[rows, 128 * tile : 128 * tile + 128], (at % 128) // 32, 1))
        p_sum = jnp.zeros((8, 128), F32)
        q_sum = jnp.zeros((8, 128), F32)
        for value, source, kind in re:
            p_sum = p_sum + place(value, source, kind)
            q_sum = q_sum - place(value, source, kind + 2)
        for value, source, kind in im:
            p_sum = p_sum + place(value, source, kind + 2)
            q_sum = q_sum + place(value, source, kind)
        ps.append(p_sum)
        qs.append(q_sum)

    def row_transform(l, _):
        for b in range(4):
            out = jnp.zeros((8, 128), F32)
            for kk in range(6):
                at = 16 * b + 2 * kk
                out = out + twiddle[l, at] * ps[kk] + twiddle[l, at + 1] * qs[kk]
            part[4 * l + b] = out
        return 0

    lax.fori_loop(0, n_z, row_transform, 0)

    def four(z):
        return pl.ds(pl.multiple_of(4 * z, 4), 4)

    bz_copies = remote_to(
        [(part.at[four(l)], part_z.at[z], row_at(y, l, core), j) for l in levels], bz_send, bz_recv
    )
    begin(bz_copies)
    part_z[z] = part[four(z)]

    def forward(k):
        at = min(6 * k, 28)
        rows = pl.ds(at + 2, 8)
        pre = dot(band_one[1], lext[rows].reshape(256, 640), NN)
        pre = pre + dot(band_one[0], l_shift[0, rows].reshape(256, 640), NN)
        pre = pre + dot(band_one[2], l_shift[1, rows].reshape(256, 640), NN)
        square = pre * pre
        bend = jnp.tanh(pre * (GELU_A + (GELU_A * GELU_B) * square))
        half = 0.5 + 0.5 * bend
        hidden = (pre * half).astype(BF16)
        rise = half + pre * (0.5 - 0.5 * (bend * bend)) * (GELU_A + (3.0 * GELU_A * GELU_B) * square)
        slope[pl.ds(at, 6)] = rise[:, 0:512].reshape(6, 32, 512)
        to = pl.ds(at, 6)
        h_shift[1, to] = hidden[:, 0:512].reshape(6, 32, 512)
        h_shift[0, to] = shifted(hidden, 1)[:, 0:512].reshape(6, 32, 512)
        h_shift[2, to] = shifted(hidden, -1)[:, 0:512].reshape(6, 32, 512)

    for k in range(6):
        forward(k)
    arrive(bz_copies)
    value = part_z[0]
    for k in range(1, n_z):
        value = value + part_z[k]
    quad_sum[...] = value
    bq_copies = remote_to(
        [(quad_sum.at[2 * a + b], part_q.at[quarter], row_at(a, z, b), j) for a, b in quarters],
        bq_send, bq_recv,
    )
    begin(bq_copies)
    part_q[quarter] = quad_sum[quarter]
    sum_one[...] = jnp.zeros_like(sum_one)
    sum_two[...] = jnp.zeros_like(sum_two)
    counted = lax.broadcasted_iota(jnp.int32, (192, 512), 0) < 128

    def backward(k):
        at = min(6 * k, 26)
        rows = pl.ds(at + 3, 8)
        grad = dot(band_back[1], cext[rows, :, 0:512].reshape(256, 512), NN)
        grad = grad + dot(band_back[0], c_shift[1, rows].reshape(256, 512), NN)
        grad = grad + dot(band_back[2], c_shift[0, rows].reshape(256, 512), NN)
        pre_grad = grad * slope[pl.ds(at + 1, 6)].reshape(192, 512)
        if k == 5:
            pre_grad = jnp.where(counted, 0.0, pre_grad)
        pre_grad = pre_grad.astype(BF16)
        own = cext[pl.ds(at + 4, 6), :, 0:512].reshape(192, 512)
        if k == 5:
            own = jnp.where(counted, 0.0, own.astype(F32)).astype(BF16)
        for v in range(3):
            sum_two[v] += dot(own, h_shift[v, pl.ds(at, 8)].reshape(256, 512), NT)
            if v == 1:
                layer = lext[rows, :, 0:512]
            else:
                layer = l_shift[v // 2, rows, :, 0:512]
            sum_one[v] += dot(pre_grad, layer.reshape(256, 512), NT)

    for k in range(2):
        backward(k)
    arrive(bq_copies)
    spectrum = part_q[0] + part_q[1] + part_q[2] + part_q[3]

    groups = lane_group((8, 128))
    row = lax.broadcasted_iota(jnp.int32, (8, 128), 0)
    first = (row == 0) & (j % 4 == 0)
    twice = jnp.where(first, 1.0, 2.0)
    spectrum = spectrum * jnp.where(groups % 2 == 1, twice * scaling, scaling)
    s_re = everywhere(jnp.where(groups == 0, spectrum, 0.0))
    m_re = everywhere(jnp.where(groups == 1, spectrum, 0.0))
    s_im = everywhere(jnp.where(groups == 2, spectrum, 0.0))
    m_im = everywhere(jnp.where(groups == 3, spectrum, 0.0))
    wide = lane_group((16, 256)) == lax.broadcasted_iota(jnp.int32, (16, 256), 0) % 8
    both = jnp.concatenate([s_re, s_im], axis=0)[:, 0:32]
    both = jnp.concatenate(parts_of(both, 3), axis=0)
    by = dot(both, jnp.concatenate([w_real[...].reshape(256, 32), w_imag[...].reshape(256, 32)], axis=0), NT)
    by = by[0:16] + by[16:32] + by[32:48]
    by_real = jnp.where(wide, by[:, 0:256], 0.0)
    by_imag = jnp.where(wide, by[:, 256:512], 0.0)
    mixed_re = by_real[0:8] - by_imag[8:16]
    mixed_im = by_real[8:16] + by_imag[0:8]
    mixed_re = everywhere(mixed_re[:, 0:128] + mixed_re[:, 128:256])
    mixed_im = everywhere(mixed_im[:, 0:128] + mixed_im[:, 128:256])
    quad[quarter] = jnp.where(
        groups == 1, mixed_im, jnp.where(groups == 2, -mixed_im, mixed_re)
    )

    cq_copies = remote_to(
        [(quad.at[quarter], quad.at[quarter], row_at(a, z, b), j) for a, b in quarters], cq_send, cq_recv
    )
    begin(cq_copies)
    grads = jnp.concatenate(
        [jnp.concatenate([m_re, m_re], axis=1), jnp.concatenate([m_im, m_im], axis=1)], axis=0
    )
    grads = jnp.where(wide, grads, 0.0)
    fields = jnp.concatenate(
        [jnp.where(groups == 0, s_re, -s_im), jnp.where(groups == 0, s_im, s_re)], axis=0
    )
    outer = dot(grads, fields, TN, HIGH)
    outer_out[...] = outer

    for k in range(2, 4):
        backward(k)
    arrive(cq_copies)
    cz_copies = remote_to(
        [(quad, mixed_in.at[four(z)], row_at(y, l, core), j) for l in levels], cz_send, cz_recv
    )
    begin(cz_copies)
    mixed_in[four(z)] = quad[...]
    for k in range(4, 6):
        backward(k)

    for n, sums in enumerate((sum_one, sum_two)):
        for v in range(3):
            total = jnp.zeros((32, 256), F32)
            for r in range(6):
                value = sums[v, 32 * r : 32 * r + 32, :]
                total = total + (pltpu.roll(value, 256 - 32 * r, 1) if r else value)
            for e in range(4):
                at = 12 * n + 4 * v + e
                mine[at // 3, 8 * (at % 3) : 8 * (at % 3) + 8, :] = total[8 * e : 8 * e + 8, 0:128]

    r_copies = remote_to([(mine.at[c], sum_c.at[j], i, c) for c in cols], r_send, r_recv)
    begin(r_copies)
    sum_c[j] = mine[j]

    arrive(cz_copies)
    def inverse(l, sums):
        sums = list(sums)
        for b in range(4):
            value = mixed_in[4 * l + b]
            for n in range(12):
                sums[n] = sums[n] + twiddle[l, 16 * b + n] * value
        return tuple(sums)

    zero = jnp.zeros((8, 128), F32)
    sums = lax.fori_loop(0, n_z, inverse, (zero,) * 12)
    grown = twice * scaling
    tiles = [zero] * 4
    for kk in range(6):
        value = (sums[2 * kk] + pltpu.roll(sums[2 * kk + 1], 64, 1)) * grown
        tiles[kk // 4] = tiles[kk // 4] + place(value, 0, kk % 4)
        tiles[2 + kk // 4] = tiles[2 + kk // 4] + place(value, 1, kk % 4)
    folded[0:8, 0:128] = tiles[0]
    folded[0:8, 128:256] = tiles[1]
    folded[8:16, 0:128] = tiles[2]
    folded[8:16, 128:256] = tiles[3]

    d_copies = remote_to([(folded, folded_in.at[j], i, c) for c in cols], d_send, d_recv)
    begin(d_copies)
    folded_in[j] = folded[...]

    arrive(r_copies)
    value = sum_c[0]
    for k in range(1, n_col):
        value = value + sum_c[k]
    chunk_c[...] = value
    rq_copies = remote_to(
        [(chunk_c, sum_q.at[quarter], row_at(a, z, b), j) for a, b in quarters], rq_send, rq_recv
    )
    begin(rq_copies)
    sum_q[quarter] = value

    arrive(rq_copies)
    value = sum_q[0] + sum_q[1] + sum_q[2] + sum_q[3]
    chunk_q[...] = value
    rz_copies = remote_to(
        [(chunk_q, sum_z.at[z], row_at(y, l, core), j) for l in levels], rz_send, rz_recv
    )
    begin(rz_copies)
    sum_z[z] = value

    arrive(d_copies)
    waves = (folded_in[0:4] + folded_in[4:8]).reshape(64, 256)
    upper, lower = parts_of(waves, 2)
    smooth = dot(
        jnp.concatenate([upper, upper, lower], axis=0),
        jnp.concatenate([tab[1], tab[1, 0:64]], axis=0),
        TN,
    )[0:192]
    upper = smooth.astype(BF16)
    high[...] = upper
    low[...] = (smooth - upper.astype(F32)).astype(BF16)

    def window(t):
        coarse = slice(32 * t, 32 * t + 96)
        rest = [h_shift[v, 8 * t + 8 : 8 * t + 10].reshape(64, 512) for v in range(3)]
        rest = jnp.concatenate(rest + [high[coarse, :], low[coarse, :]], axis=0)
        total = dot(band_tail[...], rest, NN)
        for v in range(3):
            total = total + dot(band_two[v], h_shift[v, 8 * t : 8 * t + 8].reshape(256, 512), NN)
        return total.reshape(32, 8, 512)

    results = []
    for t in range(2):
        rows = slice(16 * t, 16 * t + 16)
        value = jnp.concatenate([window(2 * t), window(2 * t + 1)], axis=1)
        stage[:, rows, :] = value.astype(BF16)
        results.append(
            pltpu.make_async_copy(stage.at[:, rows], stage_out.at[:, rows], local_sem.at[14 + t])
        )
        results[t].start()

    arrive(rz_copies)
    value = sum_z[0]
    for k in range(1, n_z):
        value = value + sum_z[k]
    value = value * scale
    done[...] = value
    g_copies = remote_to([(done, gathered.at[j], i, c) for c in cols], g_send, g_recv)
    begin(g_copies)
    gathered[j] = value
    for copies in (
        a_copies, halos, bz_copies, bq_copies, cq_copies, cz_copies, r_copies, d_copies, rq_copies, rz_copies
    ):
        leave(copies)
    arrive(g_copies)
    total_out[...] = gathered[...]
    leave(g_copies)
    for copy in results:
        copy.wait()


def finish_kernel(stage, total, outer, out, out_one, out_two, g_real, g_imag, held, sem):
    pieces = [slice(8 * n, 8 * n + 8) for n in range(4)]
    inward = [pltpu.make_async_copy(stage.at[p], held.at[p], sem.at[n]) for n, p in enumerate(pieces)]
    outward = [pltpu.make_async_copy(held.at[p], out.at[p], sem.at[4 + n]) for n, p in enumerate(pieces)]
    begin(inward)
    for n in range(4):
        inward[n].wait()
        outward[n].start()
    value = total[...].reshape(192, 128)
    for n, grad in enumerate((out_one, out_two)):
        for v in range(3):
            at = 96 * n + 32 * v
            for u in range(3):
                grad[3 * u + v] = value[at : at + 32, 32 * u : 32 * u + 32]
    g_real[...] = outer[:, 0:32].reshape(8, 32, 32)
    g_imag[...] = outer[:, 32:64].reshape(8, 32, 32)
    for copy in outward:
        copy.wait()


def body(n_row, n_col, features, mask, mask_gain, conv_one, conv_two, spec_real, spec_imag, cotangent):
    total_rows, total_cols = 32 * n_row, 512 * n_col
    scaling = 1.0 / math.sqrt((total_rows // RATIO) * (total_cols // RATIO))
    vmem = pl.BlockSpec(memory_space=pltpu.VMEM)
    hbm = pl.BlockSpec(memory_space=pl.ANY)
    col_tab = jnp.asarray(column_tables(n_col))
    row_tab = jnp.asarray(row_tables(n_row))
    spread = jnp.asarray(expand_table(), BF16)
    stretch = jnp.asarray(prolong_table(), BF16)
    turn = jnp.asarray(turn_table(), BF16)
    n_z = n_row // 4
    dma = pltpu.SemaphoreType.DMA
    stage, total, outer = pl.pallas_call(
        functools.partial(
            main_kernel, n_row, n_col, scaling, 1.0 / math.sqrt(total_rows * total_cols)
        ),
        out_shape=[
            jax.ShapeDtypeStruct((32, 32, 512), BF16),
            jax.ShapeDtypeStruct((n_col, 24, 128), F32),
            jax.ShapeDtypeStruct((256, 128), F32),
        ],
        in_specs=[hbm] * 2 + [pl.BlockSpec(memory_space=pltpu.SMEM)] + [hbm] * 10,
        out_specs=[hbm, vmem, vmem],
        scratch_shapes=[
            pltpu.VMEM((32, 32, 512), BF16),
            pltpu.VMEM((32, 512), jnp.int32),
            pltpu.VMEM((32, 32, 512), BF16),
            pltpu.VMEM((8, 32, 32), BF16),
            pltpu.VMEM((8, 32, 32), BF16),
            pltpu.VMEM((9, 32, 32), BF16),
            pltpu.VMEM((9, 32, 32), BF16),
            pltpu.VMEM(spread.shape, BF16),
            pltpu.VMEM(stretch.shape, BF16),
            pltpu.VMEM(turn.shape, BF16),
            pltpu.VMEM((32, 32, 512), BF16),
            pltpu.VMEM((40, 32, 640), BF16),
            pltpu.VMEM((40, 32, 640), BF16),
            pltpu.VMEM((192, 512), BF16),
            pltpu.VMEM((192, 512), BF16),
            pltpu.VMEM((10, 32, 512), F32),
            pltpu.VMEM((2, 128, 512), BF16),
            pltpu.SMEM(row_tab.shape[1:], F32),
            pltpu.VMEM((64, 384), F32),
            pltpu.VMEM((n_col, 16, 384), F32),
            pltpu.VMEM((n_row, 8, 128), F32),
            pltpu.VMEM((n_z, 4, 8, 128), F32),
            pltpu.VMEM((4, 8, 128), F32),
            pltpu.VMEM((4, 8, 128), F32),
            pltpu.VMEM((4, 8, 128), F32),
            pltpu.VMEM((n_row, 8, 128), F32),
            pltpu.VMEM((16, 256), F32),
            pltpu.VMEM((n_col, 16, 256), F32),
            pltpu.VMEM((4, 1024), F32),
            pltpu.VMEM((4, 1024), F32),
            pltpu.VMEM((2, 4, 1280), F32),
            pltpu.VMEM((2, 2, 32, 512), BF16),
            pltpu.VMEM((2, 1, 32, 512), BF16),
            pltpu.VMEM((2, 40, 32, 640), BF16),
            pltpu.VMEM((2, 40, 32, 512), BF16),
            pltpu.VMEM((3, 34, 32, 512), BF16),
            pltpu.VMEM((34, 32, 512), F32),
            pltpu.VMEM((3, 192, 256), BF16),
            pltpu.VMEM((3, 256, 256), BF16),
            pltpu.VMEM((256, 384), BF16),
            pltpu.VMEM((3, 192, 256), BF16),
            pltpu.VMEM((3, 192, 256), F32),
            pltpu.VMEM((3, 192, 256), F32),
            pltpu.VMEM((n_col, 24, 128), F32),
            pltpu.VMEM((n_col, 24, 128), F32),
            pltpu.VMEM((24, 128), F32),
            pltpu.VMEM((4, 24, 128), F32),
            pltpu.VMEM((24, 128), F32),
            pltpu.VMEM((n_z, 24, 128), F32),
            pltpu.VMEM((24, 128), F32),
            pltpu.VMEM((n_col, 24, 128), F32),
            dma((16,)),
            dma((10,)),
            dma((10,)),
            *[dma((7,))] * 20,
        ],
        compiler_params=pltpu.CompilerParams(
            collective_id=0, has_side_effects=True, vmem_limit_bytes=VMEM_LIMIT
        ),
        name="layer",
    )(
        features, mask, mask_gain, cotangent, spec_real, spec_imag, conv_one, conv_two,
        spread, stretch, turn, col_tab, row_tab,
    )
    return pl.pallas_call(
        finish_kernel,
        out_shape=[
            jax.ShapeDtypeStruct((32, 32, 512), BF16),
            jax.ShapeDtypeStruct((9, 32, 32), F32),
            jax.ShapeDtypeStruct((9, 32, 32), F32),
            jax.ShapeDtypeStruct((8, 32, 32), F32),
            jax.ShapeDtypeStruct((8, 32, 32), F32),
        ],
        in_specs=[hbm, vmem, vmem],
        out_specs=[hbm] + [vmem] * 4,
        scratch_shapes=[pltpu.VMEM((32, 32, 512), BF16), dma((8,))],
        compiler_params=pltpu.CompilerParams(vmem_limit_bytes=VMEM_LIMIT),
        name="finish",
    )(stage, total, outer)


def solution(mesh):
    n_row, n_col = mesh.shape["row"], mesh.shape["col"]
    placed = (
        P(None, "row", "col"),
        P("row", "col"),
        P(),
        P(),
        P(),
        P(("row", "col"), None, None),
        P(("row", "col"), None, None),
        P(None, "row", "col"),
    )
    return jax.shard_map(
        functools.partial(body, n_row, n_col),
        mesh=mesh,
        in_specs=placed,
        out_specs=(
            P(None, "row", "col"),
            P(),
            P(),
            P(("row", "col"), None, None),
            P(("row", "col"), None, None),
        ),
        check_vma=False,
    )
```

```python
import functools
import math

import jax
import jax.numpy as jnp
import ml_dtypes
import numpy as np
from jax import lax
from jax.experimental import pallas as pl
from jax.experimental.pallas import tpu as pltpu
from jax.sharding import PartitionSpec as P

C = 32
M = 32
RATIO = 8
MESH = pl.DeviceIdType.MESH
HIGH = lax.Precision.HIGHEST
F32 = jnp.float32
BF16 = jnp.bfloat16
GELU_A = math.sqrt(2.0 / math.pi)
GELU_B = 0.044715
VMEM_LIMIT = 56 * 2**20
NT = (((1,), (1,)), ((), ()))
TN = (((0,), (0,)), ((), ()))
NN = (((1,), (0,)), ((), ()))


def dot(a, b, dims, precision=None):
    return lax.dot_general(a, b, dims, preferred_element_type=F32, precision=precision)


def weights_np():
    d = (np.arange(RATIO) + 0.5 - RATIO / 2) / RATIO
    return np.stack([np.maximum(-d, 0.0), 1.0 - np.abs(d), np.maximum(d, 0.0)])


def column_tables(n_col):
    w = weights_np()
    n_two = 64 * n_col
    r = np.arange(M)
    out = np.zeros((n_col, 2, 64, 512))
    for j in range(n_col):
        fine = np.arange(512)
        cell, s = 64 * j + fine // RATIO, fine % RATIO

        def wave(at):
            return np.exp(-2j * np.pi * ((r[:, None] * at[None, :]) % n_two) / n_two)

        mean = wave(cell) / 64.0
        restrict = sum(w[b + 1][s][None, :] * wave(cell + b) for b in (-1, 0, 1))
        for kind, value in enumerate((mean, restrict)):
            parts = np.stack([value.real, value.imag], axis=0).reshape(2, 4, 8, 512)
            out[j, kind] = parts.transpose(1, 0, 2, 3).reshape(64, 512)
    out = out.astype(np.float32)
    upper = out.astype(ml_dtypes.bfloat16)
    lower = (out - upper.astype(np.float32)).astype(ml_dtypes.bfloat16)
    return np.concatenate([upper, lower], axis=2)


def row_tables(n_row):
    n_one = 4 * n_row
    q_all = np.arange(2 * n_row)
    f1 = np.where(q_all < n_row, q_all, n_one - 2 * n_row + q_all)

    def waves(q, rows):
        phase = 2 * np.pi * ((f1[q][:, None] * rows[None, :]) % n_one) / n_one
        return np.stack([np.cos(phase), np.sin(phase)], axis=-1).reshape(len(q), -1)

    there, back = [], []
    for i in range(n_row):
        for h in range(2):
            peers = 2 * np.arange(n_row // 2) + i % 2
            value = waves(2 * peers + h, 8 * (i // 2) - 1 + np.arange(10))
            there.append(np.pad(value, ((0, 0), (0, 12))).reshape(-1, 128))
            value = waves(2 * np.arange(n_row) + h, 4 * i - 1 + np.arange(6))
            value = np.pad(value, ((0, 0), (0, 4))).reshape(-1, 64)
            back.append(np.pad(value, ((0, 0), (0, 64))))
    return np.stack(there).astype(np.float32), np.stack(back).astype(np.float32)


def prolong_table():
    w = weights_np()
    out = np.zeros((C, RATIO, 3, C))
    for c in range(C):
        out[c, :, :, c] = w.T
    return out.reshape(C * RATIO, 3 * C).astype(np.float32)


def turn_table():
    w = weights_np()
    sums = np.zeros((2, C, C, 16))
    turn = np.zeros((16, C, C, 16))
    restrict = np.zeros((4, C, C, 16))
    for c in range(C):
        for row in range(16):
            cell, p = row // RATIO, row % RATIO
            sums[cell, c, c, row] = 1.0
            turn[row, c, c, row] = 1.0
            for a in (-1, 0, 1):
                restrict[cell + a + 1, c, c, row] = w[a + 1][p]
    return np.concatenate([t.reshape(-1, C * 16) for t in (sums, turn, restrict)], axis=0).astype(np.float32)


def expand_table():
    return np.repeat(np.eye(C), RATIO, axis=0).astype(np.float32)


def lane_group(shape):
    return lax.broadcasted_iota(jnp.int32, shape, len(shape) - 1) // 32


def place(value, source, target):
    shift = (32 * (target - source)) % 128
    moved = pltpu.roll(value, shift, 1) if shift else value
    return jnp.where(lane_group(value.shape) == target, moved, 0.0)


def everywhere(value):
    value = value + pltpu.roll(value, 64, 1)
    return value + pltpu.roll(value, 32, 1)


def remote(src, dst, send, recv, row, col):
    return pltpu.make_async_remote_copy(
        src_ref=src,
        dst_ref=dst,
        send_sem=send,
        recv_sem=recv,
        device_id=(row, col),
        device_id_type=MESH,
    )


def remote_to(plan, send, recv):
    return [
        remote(src, dst, send.at[n], recv.at[n], row, col)
        for n, (src, dst, row, col) in enumerate(plan)
    ]


def begin(copies):
    for copy in copies:
        copy.start()


def arrive(copies):
    for copy in copies:
        copy.wait_recv()


def leave(copies):
    for copy in copies:
        copy.wait_send()


def prepare(feat, mask, gain, cot, turn, lext, cext, field, ready):
    for half in range(2):
        ready[half]()
        rows = slice(16 * half, 16 * half + 16)
        to = slice(4 + 16 * half, 20 + 16 * half)
        raised = mask[rows, :].astype(F32) - 0.5
        for c in range(C):
            feat[c, rows, :] = (feat[c, rows, :].astype(F32) + gain[c] * raised).astype(BF16)
        turned = dot(turn[0:576], feat[:, rows, :].reshape(512, 512), NN)
        field[2 * half : 2 * half + 2] = turned[0:64].reshape(2, 32, 512)
        lext[to, :, 0:512] = turned[64:576].astype(BF16).reshape(16, 32, 512)
        turned = dot(turn[64:704], cot[:, rows, :].reshape(512, 512), NN)
        cext[to, :, 0:512] = turned[0:512].astype(BF16).reshape(16, 32, 512)
        sums = turned[512:640].reshape(4, 32, 512)
        if half == 0:
            field[4:8] = sums
        else:
            field[6:8] = field[6:8] + sums[0:2]
            field[8:10] = sums[2:4]


def parts_of(value, count):
    out = []
    for _ in range(count):
        part = value.astype(BF16)
        out.append(part)
        value = value - part.astype(F32)
    return out


def transform(table, value):
    upper, lower = parts_of(value, 2)
    whole = dot(table, upper, NT)
    return whole[0:64] + whole[64:128] + dot(table[0:64], lower, NT)


def pick(shape, pairs):
    row = lax.broadcasted_iota(jnp.int32, shape, 0)
    lane = lax.broadcasted_iota(jnp.int32, shape, 1)
    hit = jnp.zeros(shape, jnp.bool_)
    for r, l in pairs:
        hit = hit | ((row == r) & (lane == l))
    return jnp.where(hit, 1.0, 0.0).astype(BF16)


def tiled(value):
    wide = jnp.concatenate([value, jnp.zeros((32, 96), value.dtype)], axis=1)
    return everywhere(wide)


def shifted(value, by):
    if by > 0:
        return jnp.concatenate([value[:, 640 - by :], value[:, : 640 - by]], axis=1)
    return jnp.concatenate([value[:, -by:], value[:, :-by]], axis=1)


def main_kernel(
    n_row, n_col, scaling, scale,
    feat_h, mask_h, gain, cot_h, real_h, imag_h, one_h, two_h, spread_h, stretch_h, turn_h, col_tab, row_tab, back_tab,
    stage_out, total_out, outer_out,
    feat, mask, cot, w_real, w_imag, w_one, w_two, spread, stretch, turn, stage,
    lext, cext, high, low, field, tab, twiddle, twiddle_back,
    share, share_in, pair_in, part, part_in, duo, mixed_in, folded, folded_in,
    left, right, side_in, rows_in, row_c_in,
    l_shift, c_shift, h_shift, slope, band_one, band_two, band_tail, band_back, sum_one, sum_two,
    mine, half_in, mine_half, sum_c, chunk, sum_g, done, gathered,
    local_sem, halo_send, halo_recv, a_send, a_recv, zp_send, zp_recv, b_send, b_recv, cp_send, cp_recv,
    c_send, c_recv, d_send, d_recv, rp_send, rp_recv, r_send, r_recv, rg_send, rg_recv, g_send, g_recv,
    gp_send, gp_recv,
):
    i = lax.axis_index("row")
    j = lax.axis_index("col")
    half = j // 4
    core = i % 2
    other = 1 - core
    pair = i + 1 - 2 * core
    n_chip = n_row // 2
    chip = i // 2
    up, down = (i + n_row - 1) % n_row, (i + 1) % n_row
    west, east = (j + n_col - 1) % n_col, (j + 1) % n_col
    cols = [(j + d) % n_col for d in range(1, n_col)]
    chips = [(chip + d) % n_chip for d in range(1, n_chip)]

    def here(chip):
        return 2 * chip + core

    loads = [
        pltpu.make_async_copy(src, dst, local_sem.at[n])
        for n, (src, dst) in enumerate(
            (
                (mask_h, mask),
                (feat_h.at[:, 0:16], feat.at[:, 0:16]),
                (turn_h, turn),
                (cot_h.at[:, 0:16], cot.at[:, 0:16]),
                (feat_h.at[:, 16:32], feat.at[:, 16:32]),
                (cot_h.at[:, 16:32], cot.at[:, 16:32]),
                (col_tab.at[j], tab),
                (row_tab.at[2 * i + half], twiddle),
                (back_tab.at[2 * i + half], twiddle_back),
                (one_h, w_one),
                (two_h, w_two),
                (spread_h, spread),
                (stretch_h, stretch),
                (real_h, w_real),
                (imag_h, w_imag),
            )
        )
    ]
    begin(loads)

    barrier = pltpu.get_barrier_semaphore()
    partners = (
        [(i, c) for c in cols]
        + [(here(g), j) for g in chips]
        + [(pair, j)]
        + [(r, c) for r in (up, down) for c in (j, west, east)]
    )
    for partner in partners:
        pl.semaphore_signal(barrier, inc=1, device_id=partner, device_id_type=MESH)

    def first_half():
        for load in loads[0:4]:
            load.wait()

    def second_half():
        for load in loads[4:6]:
            load.wait()

    prepare(feat, mask, gain, cot, turn, lext, cext, field, (first_half, second_half))

    loads[6].wait()
    share[:, 0:128] = transform(tab[0], field[0:4].reshape(128, 512))
    share[:, 128:320] = transform(tab[1], field[4:10].reshape(192, 512))
    share[:, 320:384] = jnp.zeros((64, 64), F32)
    pl.semaphore_wait(barrier, len(partners))

    def group(c):
        return pl.ds(pl.multiple_of(16 * (c % 4), 16), 16)

    a_copies = remote_to([(share.at[group(c)], share_in.at[j], i, c) for c in cols], a_send, a_recv)
    begin(a_copies)
    share_in[j] = share[group(j), :]

    first_l = lext[4:36, :, 0:128].reshape(1024, 128)
    last_l = lext[4:36, :, 384:512].reshape(1024, 128)
    first_c = cext[4:36, :, 0:128].reshape(1024, 128)
    last_c = cext[4:36, :, 384:512].reshape(1024, 128)
    sel = (16, 128)
    left[...] = (
        dot(pick(sel, ((0, 0), (1, 1))), first_l, NT) + dot(pick(sel, ((2, 0),)), first_c, NT)
    )[0:4]
    right[...] = (
        dot(pick(sel, ((0, 126), (1, 127))), last_l, NT) + dot(pick(sel, ((2, 127),)), last_c, NT)
    )[0:4]
    plan = [
        (lext.at[4:6, :, 0:512], rows_in.at[1], up, j),
        (lext.at[34:36, :, 0:512], rows_in.at[0], down, j),
        (cext.at[4:5, :, 0:512], row_c_in.at[1], up, j),
        (cext.at[35:36, :, 0:512], row_c_in.at[0], down, j),
        (left, side_in.at[1, :, 128:1152], i, west),
        (right, side_in.at[0, :, 128:1152], i, east),
        (left.at[:, 0:128], side_in.at[1, :, 1152:1280], up, west),
        (right.at[:, 0:128], side_in.at[0, :, 1152:1280], up, east),
        (left.at[:, 896:1024], side_in.at[1, :, 0:128], down, west),
        (right.at[:, 896:1024], side_in.at[0, :, 0:128], down, east),
    ]
    halos = remote_to(plan, halo_send, halo_recv)
    begin(halos)

    for load in loads[7:]:
        load.wait()
    eye = jnp.where(
        lax.broadcasted_iota(jnp.int32, (32, 32), 0) == lax.broadcasted_iota(jnp.int32, (32, 32), 1),
        1.0,
        0.0,
    ).astype(BF16)
    block = lane_group((32, 256))
    line = lax.broadcasted_iota(jnp.int32, (256, 384), 0) % 8
    wide_block = lane_group((256, 384))
    for v in range(3):
        ones, backs, twos = [], [], []
        for u in range(3):
            one = tiled(w_one[3 * u + v].astype(F32))
            ones.append(jnp.concatenate([one, one], axis=1))
            back = tiled(dot(eye, w_two[3 * u + v], NT))
            backs.append(jnp.concatenate([back, back], axis=1))
            two = tiled(w_two[3 * u + v].astype(F32))
            twos.append(jnp.concatenate([two, two, two], axis=1).astype(BF16))
        for r in range(6):
            one = jnp.zeros((32, 256), F32)
            back = jnp.zeros((32, 256), F32)
            for u in range(3):
                one = one + jnp.where(block == r + u, ones[u], 0.0)
                back = back + jnp.where(block == r + 2 - u, backs[u], 0.0)
            band_one[v, 32 * r : 32 * r + 32, :] = one.astype(BF16)
            band_back[v, 32 * r : 32 * r + 32, :] = back.astype(BF16)
        total = jnp.zeros((256, 384), F32)
        for u in range(3):
            total = total + jnp.where(
                wide_block - line == u, dot(spread[...], twos[u], NN), 0.0
            )
        band_two[v] = total[:, 0:256].astype(BF16)
        band_tail[:, 64 * v : 64 * v + 64] = total[:, 256:320].astype(BF16)
    band_tail[:, 192:288] = stretch[...]
    band_tail[:, 288:384] = stretch[...]

    arrive(a_copies)
    total_a = share_in[0]
    for k in range(1, n_col):
        total_a = total_a + share_in[k]
    pair_in[core] = total_a
    zp_copies = remote_to([(pair_in.at[core], pair_in.at[core], pair, j)], zp_send, zp_recv)
    begin(zp_copies)
    arrive(halos)
    lext[2:4, :, 0:512] = rows_in[0]
    lext[36:38, :, 0:512] = rows_in[1]
    cext[3:4, :, 0:512] = row_c_in[0]
    cext[36:37, :, 0:512] = row_c_in[1]
    sides = jnp.concatenate([side_in[0], side_in[1]], axis=0).astype(BF16)
    at_l = pick((8, 128), ((0, 126), (1, 127), (4, 0), (5, 1)))
    at_c = pick((8, 128), ((2, 127), (6, 0)))
    lext[:, :, 512:640] = dot(sides, at_l, TN).astype(BF16).reshape(40, 32, 128)
    cext[:, :, 512:640] = dot(sides, at_c, TN).astype(BF16).reshape(40, 32, 128)

    def move(k):
        rows = pl.ds(2 + 4 * k, 4)
        value = lext[rows].reshape(128, 640)
        l_shift[0, rows] = shifted(value, 1).reshape(4, 32, 640)
        l_shift[1, rows] = shifted(value, -1).reshape(4, 32, 640)
        value = cext[rows].reshape(128, 640)
        c_shift[0, rows] = shifted(value, 1)[:, 0:512].reshape(4, 32, 512)
        c_shift[1, rows] = shifted(value, -1)[:, 0:512].reshape(4, 32, 512)

    for k in range(9):
        move(k)

    arrive(zp_copies)
    ps, qs = [], []
    for n in range(10):
        p_sum = jnp.zeros((8, 128), F32)
        q_sum = jnp.zeros((8, 128), F32)
        for b in range(2):
            kk = n - 4 * b
            if not 0 <= kk <= 5:
                continue
            pieces = [(128 + 32 * kk, 1)]
            if 1 <= kk <= 4:
                pieces.append((32 * kk - 32, 0))
            for at, kind in pieces:
                lanes = slice(128 * (at // 128), 128 * (at // 128) + 128)
                re, im = pair_in[b, 0:8, lanes], pair_in[b, 8:16, lanes]
                source = (at % 128) // 32
                p_sum = p_sum + place(re, source, kind) + place(im, source, kind + 2)
                q_sum = q_sum + place(im, source, kind) - place(re, source, kind + 2)
        ps.append(p_sum)
        qs.append(q_sum)

    def row_transform(l, _):
        for b in range(4):
            out = jnp.zeros((8, 128), F32)
            for n in range(10):
                at = 32 * b + 2 * n
                out = out + twiddle[l, at] * ps[n] + twiddle[l, at + 1] * qs[n]
            part[4 * l + b] = out
        return 0

    lax.fori_loop(0, n_chip // 4, row_transform, 0)
    b_copies = remote_to([(part.at[g], part_in.at[chip], here(g), j) for g in chips], b_send, b_recv)
    begin(b_copies)
    part_in[chip] = part[chip]

    def forward(k):
        at = min(6 * k, 28)
        rows = pl.ds(at + 2, 8)
        pre = dot(band_one[1], lext[rows].reshape(256, 640), NN)
        pre = pre + dot(band_one[0], l_shift[0, rows].reshape(256, 640), NN)
        pre = pre + dot(band_one[2], l_shift[1, rows].reshape(256, 640), NN)
        square = pre * pre
        bend = jnp.tanh(pre * (GELU_A + (GELU_A * GELU_B) * square))
        half = 0.5 + 0.5 * bend
        hidden = (pre * half).astype(BF16)
        rise = half + pre * (0.5 - 0.5 * (bend * bend)) * (GELU_A + (3.0 * GELU_A * GELU_B) * square)
        slope[pl.ds(at, 6)] = rise[:, 0:512].reshape(6, 32, 512)
        to = pl.ds(at, 6)
        h_shift[1, to] = hidden[:, 0:512].reshape(6, 32, 512)
        h_shift[0, to] = shifted(hidden, 1)[:, 0:512].reshape(6, 32, 512)
        h_shift[2, to] = shifted(hidden, -1)[:, 0:512].reshape(6, 32, 512)

    for k in range(6):
        forward(k)
    sum_one[...] = jnp.zeros_like(sum_one)
    sum_two[...] = jnp.zeros_like(sum_two)
    counted = lax.broadcasted_iota(jnp.int32, (192, 512), 0) < 128

    def backward(k):
        at = min(6 * k, 26)
        rows = pl.ds(at + 3, 8)
        grad = dot(band_back[1], cext[rows, :, 0:512].reshape(256, 512), NN)
        grad = grad + dot(band_back[0], c_shift[1, rows].reshape(256, 512), NN)
        grad = grad + dot(band_back[2], c_shift[0, rows].reshape(256, 512), NN)
        pre_grad = grad * slope[pl.ds(at + 1, 6)].reshape(192, 512)
        if k == 5:
            pre_grad = jnp.where(counted, 0.0, pre_grad)
        pre_grad = pre_grad.astype(BF16)
        own = cext[pl.ds(at + 4, 6), :, 0:512].reshape(192, 512)
        if k == 5:
            own = jnp.where(counted, 0.0, own.astype(F32)).astype(BF16)
        for v in range(3):
            sum_two[v] += dot(own, h_shift[v, pl.ds(at, 8)].reshape(256, 512), NT)
            if v == 1:
                layer = lext[rows, :, 0:512]
            else:
                layer = l_shift[v // 2, rows, :, 0:512]
            sum_one[v] += dot(pre_grad, layer.reshape(256, 512), NT)

    for k in range(6):
        backward(k)
    for n, sums in enumerate((sum_one, sum_two)):
        for v in range(3):
            total = jnp.zeros((32, 256), F32)
            for r in range(6):
                value = sums[v, 32 * r : 32 * r + 32, :]
                total = total + (pltpu.roll(value, 256 - 32 * r, 1) if r else value)
            for e in range(8):
                at = 96 * n + 32 * v + 4 * e
                piece = at // 12
                mine[piece // n_col, piece % n_col, at % 12 : at % 12 + 4, :] = total[4 * e : 4 * e + 4, 0:128]
    rp_copies = remote_to([(mine.at[other], half_in, pair, j)], rp_send, rp_recv)
    begin(rp_copies)
    arrive(rp_copies)
    mine_half[...] = mine[core] + half_in[...]
    r_copies = remote_to([(mine_half.at[c], sum_c.at[j], i, c) for c in cols], r_send, r_recv)
    begin(r_copies)
    sum_c[j] = mine_half[j]

    arrive(b_copies)
    spectrum = part_in[0]
    for k in range(1, n_chip):
        spectrum = spectrum + part_in[k]

    groups = lane_group((8, 128))
    row = lax.broadcasted_iota(jnp.int32, (8, 128), 0)
    first = (row == 0) & (j % 4 == 0)
    twice = jnp.where(first, 1.0, 2.0)
    spectrum = spectrum * jnp.where(groups % 2 == 1, twice * scaling, scaling)
    s_re = everywhere(jnp.where(groups == 0, spectrum, 0.0))
    m_re = everywhere(jnp.where(groups == 1, spectrum, 0.0))
    s_im = everywhere(jnp.where(groups == 2, spectrum, 0.0))
    m_im = everywhere(jnp.where(groups == 3, spectrum, 0.0))
    wide = lane_group((16, 256)) == lax.broadcasted_iota(jnp.int32, (16, 256), 0) % 8
    both = jnp.concatenate([s_re, s_im], axis=0)[:, 0:32]
    both = jnp.concatenate(parts_of(both, 3), axis=0)
    by = dot(both, jnp.concatenate([w_real[...].reshape(256, 32), w_imag[...].reshape(256, 32)], axis=0), NT)
    by = by[0:16] + by[16:32] + by[32:48]
    by_real = jnp.where(wide, by[:, 0:256], 0.0)
    by_imag = jnp.where(wide, by[:, 256:512], 0.0)
    mixed_re = by_real[0:8] - by_imag[8:16]
    mixed_im = by_real[8:16] + by_imag[0:8]
    mixed_re = everywhere(mixed_re[:, 0:128] + mixed_re[:, 128:256])
    mixed_im = everywhere(mixed_im[:, 0:128] + mixed_im[:, 128:256])
    upper = jnp.where(groups == 0, mixed_re, mixed_im)
    duo[core] = jnp.where(groups[0:4] < 2, upper[0:4], jnp.where(groups[0:4] == 2, mixed_re[4:8], mixed_im[4:8]))

    cp_copies = remote_to([(duo.at[core], duo.at[core], pair, j)], cp_send, cp_recv)
    begin(cp_copies)
    arrive(cp_copies)

    def two(chip):
        return pl.ds(pl.multiple_of(2 * chip, 2), 2)

    c_copies = remote_to([(duo, mixed_in.at[two(chip)], here(g), j) for g in chips], c_send, c_recv)
    begin(c_copies)
    mixed_in[two(chip)] = duo[...]
    grads = jnp.concatenate(
        [jnp.concatenate([m_re, m_re], axis=1), jnp.concatenate([m_im, m_im], axis=1)], axis=0
    )
    grads = jnp.where(wide, grads, 0.0)
    fields = jnp.concatenate(
        [jnp.where(groups == 0, s_re, -s_im), jnp.where(groups == 0, s_im, s_re)], axis=0
    )
    outer = dot(grads, fields, TN, HIGH)
    outer_out[...] = outer

    arrive(r_copies)
    value = sum_c[0]
    for k in range(1, n_col):
        value = value + sum_c[k]
    chunk[...] = value
    rg_copies = remote_to([(chunk, sum_g.at[chip], here(g), j) for g in chips], rg_send, rg_recv)
    begin(rg_copies)
    sum_g[chip] = value

    arrive(c_copies)
    def inverse(l, sums):
        sums = list(sums)
        for b in range(4):
            value = mixed_in[4 * l + b]
            for n in range(12):
                sums[n] = sums[n] + twiddle_back[l, 16 * b + n] * value
        return tuple(sums)

    sums = lax.fori_loop(0, n_row // 4, inverse, (jnp.zeros((4, 128), F32),) * 12)
    folded[:, 192:256] = jnp.zeros((16, 64), F32)
    grown = jnp.where((groups[0:4] < 2), twice[0:4], 2.0) * scaling
    even = groups[0:4] % 2 == 0
    for kk in range(6):
        sines = sums[2 * kk + 1]
        sines = jnp.where(even, -pltpu.roll(sines, 96, 1), pltpu.roll(sines, 32, 1))
        value = (sums[2 * kk] + sines) * grown
        for n in range(4):
            at = 8 * (n % 2) + 4 * (n // 2)
            folded[at : at + 4, 32 * kk : 32 * kk + 32] = value[:, 32 * n : 32 * n + 32]

    d_copies = remote_to([(folded, folded_in.at[j], i, c) for c in cols], d_send, d_recv)
    begin(d_copies)
    folded_in[j] = folded[...]

    arrive(rg_copies)
    value = sum_g[0]
    for k in range(1, n_chip):
        value = value + sum_g[k]
    value = value * scale
    done[...] = value
    g_copies = remote_to([(done, gathered.at[core, j], i, c) for c in cols], g_send, g_recv)
    begin(g_copies)
    gathered[core, j] = value
    arrive(d_copies)
    waves = (folded_in[0:4] + folded_in[4:8]).reshape(64, 256)
    upper, lower = parts_of(waves, 2)
    smooth = dot(
        jnp.concatenate([upper, upper, lower], axis=0),
        jnp.concatenate([tab[1], tab[1, 0:64]], axis=0),
        TN,
    )[0:192]
    upper = smooth.astype(BF16)
    high[...] = upper
    low[...] = (smooth - upper.astype(F32)).astype(BF16)

    def window(t):
        coarse = slice(32 * t, 32 * t + 96)
        rest = [h_shift[v, 8 * t + 8 : 8 * t + 10].reshape(64, 512) for v in range(3)]
        rest = jnp.concatenate(rest + [high[coarse, :], low[coarse, :]], axis=0)
        total = dot(band_tail[...], rest, NN)
        for v in range(3):
            total = total + dot(band_two[v], h_shift[v, 8 * t : 8 * t + 8].reshape(256, 512), NN)
        return total.reshape(32, 8, 512)

    results = []
    for t in range(2):
        rows = slice(16 * t, 16 * t + 16)
        value = jnp.concatenate([window(2 * t), window(2 * t + 1)], axis=1)
        stage[:, rows, :] = value.astype(BF16)
        results.append(
            pltpu.make_async_copy(stage.at[:, rows], stage_out.at[:, rows], local_sem.at[15 + t])
        )
        results[t].start()

    for copies in (
        a_copies, halos, zp_copies, b_copies, cp_copies, c_copies, d_copies, rp_copies, r_copies, rg_copies
    ):
        leave(copies)
    arrive(g_copies)
    gp_copies = remote_to([(gathered.at[core], gathered.at[core], pair, j)], gp_send, gp_recv)
    begin(gp_copies)
    leave(g_copies)
    for copy in results:
        copy.wait()
    arrive(gp_copies)
    for e in range(48):
        piece, at = divmod(4 * e, 12)
        total_out[4 * e : 4 * e + 4, :] = gathered[piece // n_col, piece % n_col, at : at + 4, :]
    leave(gp_copies)


def finish_kernel(stage, total, outer, out, out_one, out_two, g_real, g_imag):
    out[...] = stage[...]
    value = total[...]
    for n, grad in enumerate((out_one, out_two)):
        for v in range(3):
            at = 96 * n + 32 * v
            for u in range(3):
                grad[3 * u + v] = value[at : at + 32, 32 * u : 32 * u + 32]
    g_real[...] = outer[:, 0:32].reshape(8, 32, 32)
    g_imag[...] = outer[:, 32:64].reshape(8, 32, 32)


def body(n_row, n_col, features, mask, mask_gain, conv_one, conv_two, spec_real, spec_imag, cotangent):
    total_rows, total_cols = 32 * n_row, 512 * n_col
    scaling = 1.0 / math.sqrt((total_rows // RATIO) * (total_cols // RATIO))
    vmem = pl.BlockSpec(memory_space=pltpu.VMEM)
    hbm = pl.BlockSpec(memory_space=pl.ANY)
    col_tab = jnp.asarray(column_tables(n_col))
    row_tab, back_tab = (jnp.asarray(table) for table in row_tables(n_row))
    spread = jnp.asarray(expand_table(), BF16)
    stretch = jnp.asarray(prolong_table(), BF16)
    turn = jnp.asarray(turn_table(), BF16)
    dma = pltpu.SemaphoreType.DMA
    stage, total, outer = pl.pallas_call(
        functools.partial(
            main_kernel, n_row, n_col, scaling, 1.0 / math.sqrt(total_rows * total_cols)
        ),
        out_shape=[
            jax.ShapeDtypeStruct((32, 32, 512), BF16),
            jax.ShapeDtypeStruct((192, 128), F32),
            jax.ShapeDtypeStruct((256, 128), F32),
        ],
        in_specs=[hbm] * 2 + [pl.BlockSpec(memory_space=pltpu.SMEM)] + [hbm] * 11,
        out_specs=[hbm, vmem, vmem],
        scratch_shapes=[
            pltpu.VMEM((32, 32, 512), BF16),
            pltpu.VMEM((32, 512), jnp.int32),
            pltpu.VMEM((32, 32, 512), BF16),
            pltpu.VMEM((8, 32, 32), BF16),
            pltpu.VMEM((8, 32, 32), BF16),
            pltpu.VMEM((9, 32, 32), BF16),
            pltpu.VMEM((9, 32, 32), BF16),
            pltpu.VMEM(spread.shape, BF16),
            pltpu.VMEM(stretch.shape, BF16),
            pltpu.VMEM(turn.shape, BF16),
            pltpu.VMEM((32, 32, 512), BF16),
            pltpu.VMEM((40, 32, 640), BF16),
            pltpu.VMEM((40, 32, 640), BF16),
            pltpu.VMEM((192, 512), BF16),
            pltpu.VMEM((192, 512), BF16),
            pltpu.VMEM((10, 32, 512), F32),
            pltpu.VMEM((2, 128, 512), BF16),
            pltpu.SMEM(row_tab.shape[1:], F32),
            pltpu.SMEM(back_tab.shape[1:], F32),
            pltpu.VMEM((64, 384), F32),
            pltpu.VMEM((n_col, 16, 384), F32),
            pltpu.VMEM((2, 16, 384), F32),
            pltpu.VMEM((n_row // 2, 8, 128), F32),
            pltpu.VMEM((n_row // 2, 8, 128), F32),
            pltpu.VMEM((2, 4, 128), F32),
            pltpu.VMEM((n_row, 4, 128), F32),
            pltpu.VMEM((16, 256), F32),
            pltpu.VMEM((n_col, 16, 256), F32),
            pltpu.VMEM((4, 1024), F32),
            pltpu.VMEM((4, 1024), F32),
            pltpu.VMEM((2, 4, 1280), F32),
            pltpu.VMEM((2, 2, 32, 512), BF16),
            pltpu.VMEM((2, 1, 32, 512), BF16),
            pltpu.VMEM((2, 40, 32, 640), BF16),
            pltpu.VMEM((2, 40, 32, 512), BF16),
            pltpu.VMEM((3, 34, 32, 512), BF16),
            pltpu.VMEM((34, 32, 512), F32),
            pltpu.VMEM((3, 192, 256), BF16),
            pltpu.VMEM((3, 256, 256), BF16),
            pltpu.VMEM((256, 384), BF16),
            pltpu.VMEM((3, 192, 256), BF16),
            pltpu.VMEM((3, 192, 256), F32),
            pltpu.VMEM((3, 192, 256), F32),
            pltpu.VMEM((2, n_col, 12, 128), F32),
            pltpu.VMEM((n_col, 12, 128), F32),
            pltpu.VMEM((n_col, 12, 128), F32),
            pltpu.VMEM((n_col, 12, 128), F32),
            pltpu.VMEM((12, 128), F32),
            pltpu.VMEM((n_row // 2, 12, 128), F32),
            pltpu.VMEM((12, 128), F32),
            pltpu.VMEM((2, n_col, 12, 128), F32),
            dma((17,)),
            dma((10,)),
            dma((10,)),
            *[dma((16,))] * 22,
        ],
        compiler_params=pltpu.CompilerParams(
            collective_id=0, has_side_effects=True, vmem_limit_bytes=VMEM_LIMIT
        ),
        name="layer",
    )(
        features, mask, mask_gain, cotangent, spec_real, spec_imag, conv_one, conv_two,
        spread, stretch, turn, col_tab, row_tab, back_tab,
    )
    return pl.pallas_call(
        finish_kernel,
        out_shape=[
            jax.ShapeDtypeStruct((32, 32, 512), BF16),
            jax.ShapeDtypeStruct((9, 32, 32), F32),
            jax.ShapeDtypeStruct((9, 32, 32), F32),
            jax.ShapeDtypeStruct((8, 32, 32), F32),
            jax.ShapeDtypeStruct((8, 32, 32), F32),
        ],
        in_specs=[vmem] * 3,
        out_specs=[vmem] * 5,
        compiler_params=pltpu.CompilerParams(vmem_limit_bytes=VMEM_LIMIT),
        name="finish",
    )(stage, total, outer)


def solution(mesh):
    n_row, n_col = mesh.shape["row"], mesh.shape["col"]
    placed = (
        P(None, "row", "col"),
        P("row", "col"),
        P(),
        P(),
        P(),
        P(("row", "col"), None, None),
        P(("row", "col"), None, None),
        P(None, "row", "col"),
    )
    return jax.shard_map(
        functools.partial(body, n_row, n_col),
        mesh=mesh,
        in_specs=placed,
        out_specs=(
            P(None, "row", "col"),
            P(),
            P(),
            P(("row", "col"), None, None),
            P(("row", "col"), None, None),
        ),
        check_vma=False,
    )
```

```python
import functools
import math

import jax
import jax.numpy as jnp
import ml_dtypes
import numpy as np
from jax import lax
from jax.experimental import pallas as pl
from jax.experimental.pallas import tpu as pltpu
from jax.sharding import PartitionSpec as P

C = 32
M = 32
RATIO = 8
MESH = pl.DeviceIdType.MESH
HIGH = lax.Precision.HIGHEST
F32 = jnp.float32
BF16 = jnp.bfloat16
GELU_A = math.sqrt(2.0 / math.pi)
GELU_B = 0.044715
VMEM_LIMIT = 56 * 2**20
NT = (((1,), (1,)), ((), ()))
TN = (((0,), (0,)), ((), ()))
NN = (((1,), (0,)), ((), ()))


def dot(a, b, dims, precision=None):
    return lax.dot_general(a, b, dims, preferred_element_type=F32, precision=precision)


def weights_np():
    d = (np.arange(RATIO) + 0.5 - RATIO / 2) / RATIO
    return np.stack([np.maximum(-d, 0.0), 1.0 - np.abs(d), np.maximum(d, 0.0)])


def column_tables(n_col):
    w = weights_np()
    n_two = 64 * n_col
    r = np.arange(M)
    out = np.zeros((n_col, 2, 64, 512))
    for j in range(n_col):
        fine = np.arange(512)
        cell, s = 64 * j + fine // RATIO, fine % RATIO

        def wave(at):
            return np.exp(-2j * np.pi * ((r[:, None] * at[None, :]) % n_two) / n_two)

        mean = wave(cell) / 64.0
        restrict = sum(w[b + 1][s][None, :] * wave(cell + b) for b in (-1, 0, 1))
        for kind, value in enumerate((mean, restrict)):
            parts = np.stack([value.real, value.imag], axis=0).reshape(2, 4, 8, 512)
            out[j, kind] = parts.transpose(1, 0, 2, 3).reshape(64, 512)
    out = out.astype(np.float32)
    upper = out.astype(ml_dtypes.bfloat16)
    lower = (out - upper.astype(np.float32)).astype(ml_dtypes.bfloat16)
    return np.concatenate([upper, lower], axis=2)


def row_tables(n_row):
    n_one = 4 * n_row
    q_all = np.arange(2 * n_row)
    f1 = np.where(q_all < n_row, q_all, n_one - 2 * n_row + q_all)

    def waves(q, rows):
        phase = 2 * np.pi * ((f1[q][:, None] * rows[None, :]) % n_one) / n_one
        return np.stack([np.cos(phase), np.sin(phase)], axis=-1).reshape(len(q), -1)

    there, back = [], []
    for i in range(n_row):
        for h in range(2):
            peers = 2 * np.arange(n_row // 2) + i % 2
            value = waves(2 * peers + h, 8 * (i // 2) - 1 + np.arange(10))
            there.append(np.pad(value, ((0, 0), (0, 12))).reshape(-1, 128))
            value = waves(2 * np.arange(n_row) + h, 4 * i - 1 + np.arange(6))
            value = np.pad(value, ((0, 0), (0, 4))).reshape(-1, 64)
            back.append(np.pad(value, ((0, 0), (0, 64))))
    return np.stack(there).astype(np.float32), np.stack(back).astype(np.float32)


def prolong_table():
    w = weights_np()
    out = np.zeros((C, RATIO, 3, C))
    for c in range(C):
        out[c, :, :, c] = w.T
    return out.reshape(C * RATIO, 3 * C).astype(np.float32)


def turn_table():
    w = weights_np()
    sums = np.zeros((2, C, C, 16))
    turn = np.zeros((16, C, C, 16))
    restrict = np.zeros((4, C, C, 16))
    for c in range(C):
        for row in range(16):
            cell, p = row // RATIO, row % RATIO
            sums[cell, c, c, row] = 1.0
            turn[row, c, c, row] = 1.0
            for a in (-1, 0, 1):
                restrict[cell + a + 1, c, c, row] = w[a + 1][p]
    return np.concatenate([t.reshape(-1, C * 16) for t in (sums, turn, restrict)], axis=0).astype(np.float32)


def expand_table():
    return np.repeat(np.eye(C), RATIO, axis=0).astype(np.float32)


def lane_group(shape):
    return lax.broadcasted_iota(jnp.int32, shape, len(shape) - 1) // 32


def place(value, source, target):
    shift = (32 * (target - source)) % 128
    moved = pltpu.roll(value, shift, 1) if shift else value
    return jnp.where(lane_group(value.shape) == target, moved, 0.0)


def everywhere(value):
    value = value + pltpu.roll(value, 64, 1)
    return value + pltpu.roll(value, 32, 1)


def remote(src, dst, send, recv, row, col):
    return pltpu.make_async_remote_copy(
        src_ref=src,
        dst_ref=dst,
        send_sem=send,
        recv_sem=recv,
        device_id=(row, col),
        device_id_type=MESH,
    )


def remote_to(plan, send, recv):
    return [
        remote(src, dst, send.at[n], recv.at[n], row, col)
        for n, (src, dst, row, col) in enumerate(plan)
    ]


def begin(copies):
    for copy in copies:
        copy.start()


def arrive(copies):
    for copy in copies:
        copy.wait_recv()


def leave(copies):
    for copy in copies:
        copy.wait_send()


def prepare(feat, mask, gain, cot, turn, lext, cext, field, ready):
    for half in range(2):
        ready[half]()
        rows = slice(16 * half, 16 * half + 16)
        to = slice(4 + 16 * half, 20 + 16 * half)
        raised = mask[rows, :].astype(F32) - 0.5
        for c in range(C):
            feat[c, rows, :] = (feat[c, rows, :].astype(F32) + gain[c] * raised).astype(BF16)
        turned = dot(turn[0:576], feat[:, rows, :].reshape(512, 512), NN)
        field[2 * half : 2 * half + 2] = turned[0:64].reshape(2, 32, 512)
        lext[to, :, 0:512] = turned[64:576].astype(BF16).reshape(16, 32, 512)
        turned = dot(turn[64:704], cot[:, rows, :].reshape(512, 512), NN)
        cext[to, :, 0:512] = turned[0:512].astype(BF16).reshape(16, 32, 512)
        sums = turned[512:640].reshape(4, 32, 512)
        if half == 0:
            field[4:8] = sums
        else:
            field[6:8] = field[6:8] + sums[0:2]
            field[8:10] = sums[2:4]


def parts_of(value, count):
    out = []
    for _ in range(count):
        part = value.astype(BF16)
        out.append(part)
        value = value - part.astype(F32)
    return out


def transform(table, value):
    upper, lower = parts_of(value, 2)
    whole = dot(table, upper, NT)
    return whole[0:64] + whole[64:128] + dot(table[0:64], lower, NT)


def pick(shape, pairs):
    row = lax.broadcasted_iota(jnp.int32, shape, 0)
    lane = lax.broadcasted_iota(jnp.int32, shape, 1)
    hit = jnp.zeros(shape, jnp.bool_)
    for r, l in pairs:
        hit = hit | ((row == r) & (lane == l))
    return jnp.where(hit, 1.0, 0.0).astype(BF16)


def tiled(value):
    wide = jnp.concatenate([value, jnp.zeros((32, 96), value.dtype)], axis=1)
    return everywhere(wide)


def shifted(value, by):
    if by > 0:
        return jnp.concatenate([value[:, 640 - by :], value[:, : 640 - by]], axis=1)
    return jnp.concatenate([value[:, -by:], value[:, :-by]], axis=1)


def main_kernel(
    n_row, n_col, scaling, scale,
    feat_h, mask_h, gain, cot_h, real_h, imag_h, one_h, two_h, spread_h, stretch_h, turn_h, col_tab, row_tab, back_tab,
    stage_out, total_out, outer_out,
    feat, mask, cot, w_real, w_imag, w_one, w_two, spread, stretch, turn,
    lext, cext, high, low, field, tab, twiddle, twiddle_back,
    share, share_in, pair_in, part, part_in, duo, mixed_in, folded, folded_in,
    left, right, side_in, rows_in, row_c_in,
    l_shift, c_shift, h_shift, slope, band_one, band_two, band_tail, band_back, sum_one, sum_two,
    mine, sum_c, chunk, sum_g, done, gathered,
    local_sem, halo_send, halo_recv, a_send, a_recv, zp_send, zp_recv, b_send, b_recv, cp_send, cp_recv,
    c_send, c_recv, d_send, d_recv, r_send, r_recv, rg_send, rg_recv, g_send, g_recv,
):
    i = lax.axis_index("row")
    j = lax.axis_index("col")
    half = j // 4
    core = i % 2
    other = 1 - core
    pair = i + 1 - 2 * core
    n_chip = n_row // 2
    chip = i // 2
    up, down = (i + n_row - 1) % n_row, (i + 1) % n_row
    west, east = (j + n_col - 1) % n_col, (j + 1) % n_col
    cols = [(j + d) % n_col for d in range(1, n_col)]
    chips = [(chip + d) % n_chip for d in range(1, n_chip)]

    flock = [(core, c) for c in cols] + [(other, c) for c in cols] + [(other, j)]

    def here(chip):
        return 2 * chip + core

    loads = [
        pltpu.make_async_copy(src, dst, local_sem.at[n])
        for n, (src, dst) in enumerate(
            (
                (mask_h, mask),
                (feat_h.at[:, 0:16], feat.at[:, 0:16]),
                (turn_h, turn),
                (cot_h.at[:, 0:16], cot.at[:, 0:16]),
                (feat_h.at[:, 16:32], feat.at[:, 16:32]),
                (cot_h.at[:, 16:32], cot.at[:, 16:32]),
                (col_tab.at[j], tab),
                (row_tab.at[2 * i + half], twiddle),
                (back_tab.at[2 * i + half], twiddle_back),
                (one_h, w_one),
                (two_h, w_two),
                (spread_h, spread),
                (stretch_h, stretch),
                (real_h, w_real),
                (imag_h, w_imag),
            )
        )
    ]
    begin(loads)

    barrier = pltpu.get_barrier_semaphore()
    partners = (
        [(i, c) for c in cols]
        + [(here(g), j) for g in chips]
        + [(pair, j)]
        + [(pair, c) for c in cols]
        + [(r, c) for r in (up, down) for c in (j, west, east)]
    )
    for partner in partners:
        pl.semaphore_signal(barrier, inc=1, device_id=partner, device_id_type=MESH)

    def first_half():
        for load in loads[0:4]:
            load.wait()

    def second_half():
        for load in loads[4:6]:
            load.wait()

    prepare(feat, mask, gain, cot, turn, lext, cext, field, (first_half, second_half))

    first_l = lext[4:36, :, 0:128].reshape(1024, 128)
    last_l = lext[4:36, :, 384:512].reshape(1024, 128)
    first_c = cext[4:36, :, 0:128].reshape(1024, 128)
    last_c = cext[4:36, :, 384:512].reshape(1024, 128)
    sel = (16, 128)
    left[...] = (
        dot(pick(sel, ((0, 0), (1, 1))), first_l, NT) + dot(pick(sel, ((2, 0),)), first_c, NT)
    )[0:4]
    right[...] = (
        dot(pick(sel, ((0, 126), (1, 127))), last_l, NT) + dot(pick(sel, ((2, 127),)), last_c, NT)
    )[0:4]
    pl.semaphore_wait(barrier, len(partners))

    plan = [
        (lext.at[4:6, :, 0:512], rows_in.at[1], up, j),
        (lext.at[34:36, :, 0:512], rows_in.at[0], down, j),
        (cext.at[4:5, :, 0:512], row_c_in.at[1], up, j),
        (cext.at[35:36, :, 0:512], row_c_in.at[0], down, j),
        (left, side_in.at[1, :, 128:1152], i, west),
        (right, side_in.at[0, :, 128:1152], i, east),
        (left.at[:, 0:128], side_in.at[1, :, 1152:1280], up, west),
        (right.at[:, 0:128], side_in.at[0, :, 1152:1280], up, east),
        (left.at[:, 896:1024], side_in.at[1, :, 0:128], down, west),
        (right.at[:, 896:1024], side_in.at[0, :, 0:128], down, east),
    ]
    halos = remote_to(plan, halo_send, halo_recv)
    begin(halos)

    loads[6].wait()
    share[:, 0:128] = transform(tab[0], field[0:4].reshape(128, 512))
    share[:, 128:320] = transform(tab[1], field[4:10].reshape(192, 512))
    share[:, 320:384] = jnp.zeros((64, 64), F32)

    def group(c):
        return pl.ds(pl.multiple_of(16 * (c % 4), 16), 16)

    a_copies = remote_to([(share.at[group(c)], share_in.at[j], i, c) for c in cols], a_send, a_recv)
    begin(a_copies)
    share_in[j] = share[group(j), :]

    for load in loads[7:]:
        load.wait()
    eye = jnp.where(
        lax.broadcasted_iota(jnp.int32, (32, 32), 0) == lax.broadcasted_iota(jnp.int32, (32, 32), 1),
        1.0,
        0.0,
    ).astype(BF16)
    block = lane_group((32, 256))
    line = lax.broadcasted_iota(jnp.int32, (256, 384), 0) % 8
    wide_block = lane_group((256, 384))
    for v in range(3):
        ones, backs, twos = [], [], []
        for u in range(3):
            one = tiled(w_one[3 * u + v].astype(F32))
            ones.append(jnp.concatenate([one, one], axis=1))
            back = tiled(dot(eye, w_two[3 * u + v], NT))
            backs.append(jnp.concatenate([back, back], axis=1))
            two = tiled(w_two[3 * u + v].astype(F32))
            twos.append(jnp.concatenate([two, two, two], axis=1).astype(BF16))
        for r in range(6):
            one = jnp.zeros((32, 256), F32)
            back = jnp.zeros((32, 256), F32)
            for u in range(3):
                one = one + jnp.where(block == r + u, ones[u], 0.0)
                back = back + jnp.where(block == r + 2 - u, backs[u], 0.0)
            band_one[v, 32 * r : 32 * r + 32, :] = one.astype(BF16)
            band_back[v, 32 * r : 32 * r + 32, :] = back.astype(BF16)
        total = jnp.zeros((256, 384), F32)
        for u in range(3):
            total = total + jnp.where(
                wide_block - line == u, dot(spread[...], twos[u], NN), 0.0
            )
        band_two[v] = total[:, 0:256].astype(BF16)
        band_tail[:, 64 * v : 64 * v + 64] = total[:, 256:320].astype(BF16)
    band_tail[:, 192:288] = stretch[...]
    band_tail[:, 288:384] = stretch[...]

    arrive(a_copies)
    total_a = share_in[0]
    for k in range(1, n_col):
        total_a = total_a + share_in[k]
    pair_in[core] = total_a
    zp_copies = remote_to([(pair_in.at[core], pair_in.at[core], pair, j)], zp_send, zp_recv)
    begin(zp_copies)
    arrive(halos)
    lext[2:4, :, 0:512] = rows_in[0]
    lext[36:38, :, 0:512] = rows_in[1]
    cext[3:4, :, 0:512] = row_c_in[0]
    cext[36:37, :, 0:512] = row_c_in[1]
    sides = jnp.concatenate([side_in[0], side_in[1]], axis=0).astype(BF16)
    at_l = pick((8, 128), ((0, 126), (1, 127), (4, 0), (5, 1)))
    at_c = pick((8, 128), ((2, 127), (6, 0)))
    lext[:, :, 512:640] = dot(sides, at_l, TN).astype(BF16).reshape(40, 32, 128)
    cext[:, :, 512:640] = dot(sides, at_c, TN).astype(BF16).reshape(40, 32, 128)

    def move(k):
        rows = pl.ds(2 + 4 * k, 4)
        value = lext[rows].reshape(128, 640)
        l_shift[0, rows] = shifted(value, 1).reshape(4, 32, 640)
        l_shift[1, rows] = shifted(value, -1).reshape(4, 32, 640)
        value = cext[rows].reshape(128, 640)
        c_shift[0, rows] = shifted(value, 1)[:, 0:512].reshape(4, 32, 512)
        c_shift[1, rows] = shifted(value, -1)[:, 0:512].reshape(4, 32, 512)

    for k in range(9):
        move(k)

    arrive(zp_copies)
    ps, qs = [], []
    for n in range(10):
        p_sum = jnp.zeros((8, 128), F32)
        q_sum = jnp.zeros((8, 128), F32)
        for b in range(2):
            kk = n - 4 * b
            if not 0 <= kk <= 5:
                continue
            pieces = [(128 + 32 * kk, 1)]
            if 1 <= kk <= 4:
                pieces.append((32 * kk - 32, 0))
            for at, kind in pieces:
                lanes = slice(128 * (at // 128), 128 * (at // 128) + 128)
                re, im = pair_in[b, 0:8, lanes], pair_in[b, 8:16, lanes]
                source = (at % 128) // 32
                p_sum = p_sum + place(re, source, kind) + place(im, source, kind + 2)
                q_sum = q_sum + place(im, source, kind) - place(re, source, kind + 2)
        ps.append(p_sum)
        qs.append(q_sum)

    def row_transform(l, _):
        for b in range(4):
            out = jnp.zeros((8, 128), F32)
            for n in range(10):
                at = 32 * b + 2 * n
                out = out + twiddle[l, at] * ps[n] + twiddle[l, at + 1] * qs[n]
            part[4 * l + b] = out
        return 0

    lax.fori_loop(0, n_chip // 4, row_transform, 0)
    b_copies = remote_to([(part.at[g], part_in.at[chip], here(g), j) for g in chips], b_send, b_recv)
    begin(b_copies)
    part_in[chip] = part[chip]

    def forward(k):
        at = min(6 * k, 28)
        rows = pl.ds(at + 2, 8)
        pre = dot(band_one[1], lext[rows].reshape(256, 640), NN)
        pre = pre + dot(band_one[0], l_shift[0, rows].reshape(256, 640), NN)
        pre = pre + dot(band_one[2], l_shift[1, rows].reshape(256, 640), NN)
        square = pre * pre
        bend = jnp.tanh(pre * (GELU_A + (GELU_A * GELU_B) * square))
        half = 0.5 + 0.5 * bend
        hidden = (pre * half).astype(BF16)
        rise = half + pre * (0.5 - 0.5 * (bend * bend)) * (GELU_A + (3.0 * GELU_A * GELU_B) * square)
        slope[pl.ds(at, 6)] = rise[:, 0:512].reshape(6, 32, 512)
        to = pl.ds(at, 6)
        h_shift[1, to] = hidden[:, 0:512].reshape(6, 32, 512)
        h_shift[0, to] = shifted(hidden, 1)[:, 0:512].reshape(6, 32, 512)
        h_shift[2, to] = shifted(hidden, -1)[:, 0:512].reshape(6, 32, 512)

    for k in range(6):
        forward(k)
    sum_one[...] = jnp.zeros_like(sum_one)
    sum_two[...] = jnp.zeros_like(sum_two)
    counted = lax.broadcasted_iota(jnp.int32, (192, 512), 0) < 128

    def backward(k):
        at = min(6 * k, 26)
        rows = pl.ds(at + 3, 8)
        grad = dot(band_back[1], cext[rows, :, 0:512].reshape(256, 512), NN)
        grad = grad + dot(band_back[0], c_shift[1, rows].reshape(256, 512), NN)
        grad = grad + dot(band_back[2], c_shift[0, rows].reshape(256, 512), NN)
        pre_grad = grad * slope[pl.ds(at + 1, 6)].reshape(192, 512)
        if k == 5:
            pre_grad = jnp.where(counted, 0.0, pre_grad)
        pre_grad = pre_grad.astype(BF16)
        own = cext[pl.ds(at + 4, 6), :, 0:512].reshape(192, 512)
        if k == 5:
            own = jnp.where(counted, 0.0, own.astype(F32)).astype(BF16)
        for v in range(3):
            sum_two[v] += dot(own, h_shift[v, pl.ds(at, 8)].reshape(256, 512), NT)
            if v == 1:
                layer = lext[rows, :, 0:512]
            else:
                layer = l_shift[v // 2, rows, :, 0:512]
            sum_one[v] += dot(pre_grad, layer.reshape(256, 512), NT)

    for k in range(6):
        backward(k)
    for n, sums in enumerate((sum_one, sum_two)):
        for v in range(3):
            total = jnp.zeros((32, 256), F32)
            for r in range(6):
                value = sums[v, 32 * r : 32 * r + 32, :]
                total = total + (pltpu.roll(value, 256 - 32 * r, 1) if r else value)
            for e in range(8):
                at = 96 * n + 32 * v + 4 * e
                piece = at // 12
                mine[piece // n_col, piece % n_col, at % 12 : at % 12 + 4, :] = total[4 * e : 4 * e + 4, 0:128]
    r_copies = remote_to([(mine.at[b, c], sum_c.at[core, j], 2 * chip + b, c) for b, c in flock], r_send, r_recv)
    begin(r_copies)
    sum_c[core, j] = mine[core, j]

    arrive(b_copies)
    spectrum = part_in[0]
    for k in range(1, n_chip):
        spectrum = spectrum + part_in[k]

    groups = lane_group((8, 128))
    row = lax.broadcasted_iota(jnp.int32, (8, 128), 0)
    first = (row == 0) & (j % 4 == 0)
    twice = jnp.where(first, 1.0, 2.0)
    spectrum = spectrum * jnp.where(groups % 2 == 1, twice * scaling, scaling)
    s_re = everywhere(jnp.where(groups == 0, spectrum, 0.0))
    m_re = everywhere(jnp.where(groups == 1, spectrum, 0.0))
    s_im = everywhere(jnp.where(groups == 2, spectrum, 0.0))
    m_im = everywhere(jnp.where(groups == 3, spectrum, 0.0))
    wide = lane_group((16, 256)) == lax.broadcasted_iota(jnp.int32, (16, 256), 0) % 8
    both = jnp.concatenate([s_re, s_im], axis=0)[:, 0:32]
    both = jnp.concatenate(parts_of(both, 3), axis=0)
    by = dot(both, jnp.concatenate([w_real[...].reshape(256, 32), w_imag[...].reshape(256, 32)], axis=0), NT)
    by = by[0:16] + by[16:32] + by[32:48]
    by_real = jnp.where(wide, by[:, 0:256], 0.0)
    by_imag = jnp.where(wide, by[:, 256:512], 0.0)
    mixed_re = by_real[0:8] - by_imag[8:16]
    mixed_im = by_real[8:16] + by_imag[0:8]
    mixed_re = everywhere(mixed_re[:, 0:128] + mixed_re[:, 128:256])
    mixed_im = everywhere(mixed_im[:, 0:128] + mixed_im[:, 128:256])
    upper = jnp.where(groups == 0, mixed_re, mixed_im)
    duo[core] = jnp.where(groups[0:4] < 2, upper[0:4], jnp.where(groups[0:4] == 2, mixed_re[4:8], mixed_im[4:8]))

    cp_copies = remote_to([(duo.at[core], duo.at[core], pair, j)], cp_send, cp_recv)
    begin(cp_copies)
    arrive(cp_copies)

    def two(chip):
        return pl.ds(pl.multiple_of(2 * chip, 2), 2)

    c_copies = remote_to([(duo, mixed_in.at[two(chip)], here(g), j) for g in chips], c_send, c_recv)
    begin(c_copies)
    mixed_in[two(chip)] = duo[...]
    grads = jnp.concatenate(
        [jnp.concatenate([m_re, m_re], axis=1), jnp.concatenate([m_im, m_im], axis=1)], axis=0
    )
    grads = jnp.where(wide, grads, 0.0)
    fields = jnp.concatenate(
        [jnp.where(groups == 0, s_re, -s_im), jnp.where(groups == 0, s_im, s_re)], axis=0
    )
    outer = dot(grads, fields, TN, HIGH)
    outer_out[...] = outer

    arrive(r_copies)
    value = sum_c[0, 0]
    for k in range(1, 2 * n_col):
        value = value + sum_c[k // n_col, k % n_col]
    chunk[...] = value
    rg_copies = remote_to([(chunk, sum_g.at[chip], here(g), j) for g in chips], rg_send, rg_recv)
    begin(rg_copies)
    sum_g[chip] = value

    arrive(c_copies)
    def inverse(l, sums):
        sums = list(sums)
        for b in range(4):
            value = mixed_in[4 * l + b]
            for n in range(12):
                sums[n] = sums[n] + twiddle_back[l, 16 * b + n] * value
        return tuple(sums)

    sums = lax.fori_loop(0, n_row // 4, inverse, (jnp.zeros((4, 128), F32),) * 12)
    folded[:, 192:256] = jnp.zeros((16, 64), F32)
    grown = jnp.where((groups[0:4] < 2), twice[0:4], 2.0) * scaling
    even = groups[0:4] % 2 == 0
    for kk in range(6):
        sines = sums[2 * kk + 1]
        sines = jnp.where(even, -pltpu.roll(sines, 96, 1), pltpu.roll(sines, 32, 1))
        value = (sums[2 * kk] + sines) * grown
        for n in range(4):
            at = 8 * (n % 2) + 4 * (n // 2)
            folded[at : at + 4, 32 * kk : 32 * kk + 32] = value[:, 32 * n : 32 * n + 32]

    d_copies = remote_to([(folded, folded_in.at[j], i, c) for c in cols], d_send, d_recv)
    begin(d_copies)
    folded_in[j] = folded[...]

    arrive(rg_copies)
    value = sum_g[0]
    for k in range(1, n_chip):
        value = value + sum_g[k]
    value = value * scale
    done[...] = value
    g_copies = remote_to([(done, gathered.at[core, j], 2 * chip + b, c) for b, c in flock], g_send, g_recv)
    begin(g_copies)
    gathered[core, j] = value
    arrive(d_copies)
    waves = (folded_in[0:4] + folded_in[4:8]).reshape(64, 256)
    upper, lower = parts_of(waves, 2)
    smooth = dot(
        jnp.concatenate([upper, upper, lower], axis=0),
        jnp.concatenate([tab[1], tab[1, 0:64]], axis=0),
        TN,
    )[0:192]
    upper = smooth.astype(BF16)
    high[...] = upper
    low[...] = (smooth - upper.astype(F32)).astype(BF16)

    def window(t):
        coarse = slice(32 * t, 32 * t + 96)
        rest = [h_shift[v, 8 * t + 8 : 8 * t + 10].reshape(64, 512) for v in range(3)]
        rest = jnp.concatenate(rest + [high[coarse, :], low[coarse, :]], axis=0)
        total = dot(band_tail[...], rest, NN)
        for v in range(3):
            total = total + dot(band_two[v], h_shift[v, 8 * t : 8 * t + 8].reshape(256, 512), NN)
        return total.reshape(32, 8, 512)

    for t in range(2):
        rows = slice(16 * t, 16 * t + 16)
        value = jnp.concatenate([window(2 * t), window(2 * t + 1)], axis=1)
        stage_out[:, rows, :] = value.astype(BF16)

    for copies in (
        a_copies, halos, zp_copies, b_copies, cp_copies, c_copies, d_copies, r_copies, rg_copies
    ):
        leave(copies)
    arrive(g_copies)
    for e in range(48):
        piece, at = divmod(4 * e, 12)
        total_out[4 * e : 4 * e + 4, :] = gathered[piece // n_col, piece % n_col, at : at + 4, :]
    leave(g_copies)


def finish_kernel(stage, total, outer, out, out_one, out_two, g_real, g_imag, sem):
    copy = pltpu.make_async_copy(stage, out, sem)
    copy.start()
    value = total[...]
    for n, grad in enumerate((out_one, out_two)):
        for v in range(3):
            at = 96 * n + 32 * v
            for u in range(3):
                grad[3 * u + v] = value[at : at + 32, 32 * u : 32 * u + 32]
    g_real[...] = outer[:, 0:32].reshape(8, 32, 32)
    g_imag[...] = outer[:, 32:64].reshape(8, 32, 32)
    copy.wait()


def body(n_row, n_col, features, mask, mask_gain, conv_one, conv_two, spec_real, spec_imag, cotangent):
    total_rows, total_cols = 32 * n_row, 512 * n_col
    scaling = 1.0 / math.sqrt((total_rows // RATIO) * (total_cols // RATIO))
    vmem = pl.BlockSpec(memory_space=pltpu.VMEM)
    hbm = pl.BlockSpec(memory_space=pl.ANY)
    col_tab = jnp.asarray(column_tables(n_col))
    row_tab, back_tab = (jnp.asarray(table) for table in row_tables(n_row))
    spread = jnp.asarray(expand_table(), BF16)
    stretch = jnp.asarray(prolong_table(), BF16)
    turn = jnp.asarray(turn_table(), BF16)
    dma = pltpu.SemaphoreType.DMA
    stage, total, outer = pl.pallas_call(
        functools.partial(
            main_kernel, n_row, n_col, scaling, 1.0 / math.sqrt(total_rows * total_cols)
        ),
        out_shape=[
            pltpu.VMEM((32, 32, 512), BF16),
            pltpu.VMEM((192, 128), F32),
            pltpu.VMEM((256, 128), F32),
        ],
        in_specs=[hbm] * 2 + [pl.BlockSpec(memory_space=pltpu.SMEM)] + [hbm] * 11,
        out_specs=[vmem] * 3,
        scratch_shapes=[
            pltpu.VMEM((32, 32, 512), BF16),
            pltpu.VMEM((32, 512), jnp.int32),
            pltpu.VMEM((32, 32, 512), BF16),
            pltpu.VMEM((8, 32, 32), BF16),
            pltpu.VMEM((8, 32, 32), BF16),
            pltpu.VMEM((9, 32, 32), BF16),
            pltpu.VMEM((9, 32, 32), BF16),
            pltpu.VMEM(spread.shape, BF16),
            pltpu.VMEM(stretch.shape, BF16),
            pltpu.VMEM(turn.shape, BF16),
            pltpu.VMEM((40, 32, 640), BF16),
            pltpu.VMEM((40, 32, 640), BF16),
            pltpu.VMEM((192, 512), BF16),
            pltpu.VMEM((192, 512), BF16),
            pltpu.VMEM((10, 32, 512), F32),
            pltpu.VMEM((2, 128, 512), BF16),
            pltpu.SMEM(row_tab.shape[1:], F32),
            pltpu.SMEM(back_tab.shape[1:], F32),
            pltpu.VMEM((64, 384), F32),
            pltpu.VMEM((n_col, 16, 384), F32),
            pltpu.VMEM((2, 16, 384), F32),
            pltpu.VMEM((n_row // 2, 8, 128), F32),
            pltpu.VMEM((n_row // 2, 8, 128), F32),
            pltpu.VMEM((2, 4, 128), F32),
            pltpu.VMEM((n_row, 4, 128), F32),
            pltpu.VMEM((16, 256), F32),
            pltpu.VMEM((n_col, 16, 256), F32),
            pltpu.VMEM((4, 1024), F32),
            pltpu.VMEM((4, 1024), F32),
            pltpu.VMEM((2, 4, 1280), F32),
            pltpu.VMEM((2, 2, 32, 512), BF16),
            pltpu.VMEM((2, 1, 32, 512), BF16),
            pltpu.VMEM((2, 40, 32, 640), BF16),
            pltpu.VMEM((2, 40, 32, 512), BF16),
            pltpu.VMEM((3, 34, 32, 512), BF16),
            pltpu.VMEM((34, 32, 512), F32),
            pltpu.VMEM((3, 192, 256), BF16),
            pltpu.VMEM((3, 256, 256), BF16),
            pltpu.VMEM((256, 384), BF16),
            pltpu.VMEM((3, 192, 256), BF16),
            pltpu.VMEM((3, 192, 256), F32),
            pltpu.VMEM((3, 192, 256), F32),
            pltpu.VMEM((2, n_col, 12, 128), F32),
            pltpu.VMEM((2, n_col, 12, 128), F32),
            pltpu.VMEM((12, 128), F32),
            pltpu.VMEM((n_row // 2, 12, 128), F32),
            pltpu.VMEM((12, 128), F32),
            pltpu.VMEM((2, n_col, 12, 128), F32),
            dma((17,)),
            dma((10,)),
            dma((10,)),
            *[dma((16,))] * 18,
        ],
        compiler_params=pltpu.CompilerParams(
            collective_id=0, has_side_effects=True, vmem_limit_bytes=VMEM_LIMIT
        ),
        name="layer",
    )(
        features, mask, mask_gain, cotangent, spec_real, spec_imag, conv_one, conv_two,
        spread, stretch, turn, col_tab, row_tab, back_tab,
    )
    return pl.pallas_call(
        finish_kernel,
        out_shape=[
            jax.ShapeDtypeStruct((32, 32, 512), BF16),
            jax.ShapeDtypeStruct((9, 32, 32), F32),
            jax.ShapeDtypeStruct((9, 32, 32), F32),
            jax.ShapeDtypeStruct((8, 32, 32), F32),
            jax.ShapeDtypeStruct((8, 32, 32), F32),
        ],
        in_specs=[vmem] * 3,
        out_specs=[hbm] + [vmem] * 4,
        scratch_shapes=[dma],
        compiler_params=pltpu.CompilerParams(vmem_limit_bytes=VMEM_LIMIT),
        name="finish",
    )(*(pltpu.with_memory_space_constraint(value, pltpu.VMEM) for value in (stage, total, outer)))


def solution(mesh):
    n_row, n_col = mesh.shape["row"], mesh.shape["col"]
    placed = (
        P(None, "row", "col"),
        P("row", "col"),
        P(),
        P(),
        P(),
        P(("row", "col"), None, None),
        P(("row", "col"), None, None),
        P(None, "row", "col"),
    )
    return jax.shard_map(
        functools.partial(body, n_row, n_col),
        mesh=mesh,
        in_specs=placed,
        out_specs=(
            P(None, "row", "col"),
            P(),
            P(),
            P(("row", "col"), None, None),
            P(("row", "col"), None, None),
        ),
        check_vma=False,
    )
```

```python
import functools
import math

import jax
import jax.numpy as jnp
import ml_dtypes
import numpy as np
from jax import lax
from jax.experimental import pallas as pl
from jax.experimental.pallas import tpu as pltpu
from jax.sharding import PartitionSpec as P

C = 32
M = 32
RATIO = 8
MESH = pl.DeviceIdType.MESH
HIGH = lax.Precision.HIGHEST
F32 = jnp.float32
BF16 = jnp.bfloat16
GELU_A = math.sqrt(2.0 / math.pi)
GELU_B = 0.044715
VMEM_LIMIT = 56 * 2**20
NT = (((1,), (1,)), ((), ()))
TN = (((0,), (0,)), ((), ()))
NN = (((1,), (0,)), ((), ()))


def dot(a, b, dims, precision=None):
    return lax.dot_general(a, b, dims, preferred_element_type=F32, precision=precision)


def weights_np():
    d = (np.arange(RATIO) + 0.5 - RATIO / 2) / RATIO
    return np.stack([np.maximum(-d, 0.0), 1.0 - np.abs(d), np.maximum(d, 0.0)])


def column_tables(n_col):
    w = weights_np()
    n_two = 64 * n_col
    r = np.arange(M)
    out = np.zeros((n_col, 2, 64, 512))
    for j in range(n_col):
        fine = np.arange(512)
        cell, s = 64 * j + fine // RATIO, fine % RATIO

        def wave(at):
            return np.exp(-2j * np.pi * ((r[:, None] * at[None, :]) % n_two) / n_two)

        mean = wave(cell) / 64.0
        restrict = sum(w[b + 1][s][None, :] * wave(cell + b) for b in (-1, 0, 1))
        for kind, value in enumerate((mean, restrict)):
            parts = np.stack([value.real, value.imag], axis=0).reshape(2, 4, 8, 512)
            out[j, kind] = parts.transpose(1, 0, 2, 3).reshape(64, 512)
    out = out.astype(np.float32)
    upper = out.astype(ml_dtypes.bfloat16)
    lower = (out - upper.astype(np.float32)).astype(ml_dtypes.bfloat16)
    return np.concatenate([upper, lower], axis=2)


def row_tables(n_row):
    n_one = 4 * n_row
    q_all = np.arange(2 * n_row)
    f1 = np.where(q_all < n_row, q_all, n_one - 2 * n_row + q_all)

    def waves(q, rows):
        phase = 2 * np.pi * ((f1[q][:, None] * rows[None, :]) % n_one) / n_one
        return np.stack([np.cos(phase), np.sin(phase)], axis=-1).reshape(len(q), -1)

    there, back = [], []
    for i in range(n_row):
        for h in range(2):
            peers = 2 * np.arange(n_row // 2) + i % 2
            value = waves(2 * peers + h, 8 * (i // 2) - 1 + np.arange(10))
            there.append(np.pad(value, ((0, 0), (0, 12))).reshape(-1, 128))
            value = waves(2 * np.arange(n_row) + h, 4 * i - 1 + np.arange(6))
            value = np.pad(value, ((0, 0), (0, 4))).reshape(-1, 64)
            back.append(np.pad(value, ((0, 0), (0, 64))))
    return np.stack(there).astype(np.float32), np.stack(back).astype(np.float32)


def prolong_table():
    w = weights_np()
    out = np.zeros((C, RATIO, 3, C))
    for c in range(C):
        out[c, :, :, c] = w.T
    return out.reshape(C * RATIO, 3 * C).astype(np.float32)


def turn_table():
    w = weights_np()
    sums = np.zeros((2, C, C, 16))
    turn = np.zeros((16, C, C, 16))
    restrict = np.zeros((4, C, C, 16))
    for c in range(C):
        for row in range(16):
            cell, p = row // RATIO, row % RATIO
            sums[cell, c, c, row] = 1.0
            turn[row, c, c, row] = 1.0
            for a in (-1, 0, 1):
                restrict[cell + a + 1, c, c, row] = w[a + 1][p]
    return np.concatenate([t.reshape(-1, C * 16) for t in (sums, turn, restrict)], axis=0).astype(np.float32)


def expand_table():
    return np.repeat(np.eye(C), RATIO, axis=0).astype(np.float32)


def lane_group(shape):
    return lax.broadcasted_iota(jnp.int32, shape, len(shape) - 1) // 32


def place(value, source, target):
    shift = (32 * (target - source)) % 128
    moved = pltpu.roll(value, shift, 1) if shift else value
    return jnp.where(lane_group(value.shape) == target, moved, 0.0)


def everywhere(value):
    value = value + pltpu.roll(value, 64, 1)
    return value + pltpu.roll(value, 32, 1)


def remote(src, dst, send, recv, row, col):
    return pltpu.make_async_remote_copy(
        src_ref=src,
        dst_ref=dst,
        send_sem=send,
        recv_sem=recv,
        device_id=(row, col),
        device_id_type=MESH,
    )


def remote_to(plan, send, recv):
    return [
        remote(src, dst, send.at[n], recv.at[n], row, col)
        for n, (src, dst, row, col) in enumerate(plan)
    ]


def begin(copies):
    for copy in copies:
        copy.start()


def arrive(copies):
    for copy in copies:
        copy.wait_recv()


def leave(copies):
    for copy in copies:
        copy.wait_send()


def prepare(feat, mask, gain, cot, turn, lext, cext, field, ready):
    for half in range(2):
        ready[half]()
        rows = slice(16 * half, 16 * half + 16)
        to = slice(4 + 16 * half, 20 + 16 * half)
        raised = mask[rows, :].astype(F32) - 0.5
        for c in range(C):
            feat[c, rows, :] = (feat[c, rows, :].astype(F32) + gain[c] * raised).astype(BF16)
        turned = dot(turn[0:576], feat[:, rows, :].reshape(512, 512), NN)
        field[2 * half : 2 * half + 2] = turned[0:64].reshape(2, 32, 512)
        lext[to, :, 0:512] = turned[64:576].astype(BF16).reshape(16, 32, 512)
        turned = dot(turn[64:704], cot[:, rows, :].reshape(512, 512), NN)
        cext[to, :, 0:512] = turned[0:512].astype(BF16).reshape(16, 32, 512)
        sums = turned[512:640].reshape(4, 32, 512)
        if half == 0:
            field[4:8] = sums
        else:
            field[6:8] = field[6:8] + sums[0:2]
            field[8:10] = sums[2:4]


def parts_of(value, count):
    out = []
    for _ in range(count):
        part = value.astype(BF16)
        out.append(part)
        value = value - part.astype(F32)
    return out


def transform(table, value):
    upper, lower = parts_of(value, 2)
    whole = dot(table, upper, NT)
    return whole[0:64] + whole[64:128] + dot(table[0:64], lower, NT)


def pick(shape, pairs):
    row = lax.broadcasted_iota(jnp.int32, shape, 0)
    lane = lax.broadcasted_iota(jnp.int32, shape, 1)
    hit = jnp.zeros(shape, jnp.bool_)
    for r, l in pairs:
        hit = hit | ((row == r) & (lane == l))
    return jnp.where(hit, 1.0, 0.0).astype(BF16)


def tiled(value):
    wide = jnp.concatenate([value, jnp.zeros((32, 96), value.dtype)], axis=1)
    return everywhere(wide)


def shifted(value, by):
    width = value.shape[1]
    if by > 0:
        return jnp.concatenate([value[:, width - by :], value[:, : width - by]], axis=1)
    return jnp.concatenate([value[:, -by:], value[:, :-by]], axis=1)


def main_kernel(
    n_row, n_col, scaling, scale,
    feat_h, mask_h, gain, cot_h, real_h, imag_h, one_h, two_h, spread_h, stretch_h, turn_h, col_tab, row_tab, back_tab,
    stage_out, total_out, outer_out,
    feat, mask, cot, w_real, w_imag, w_one, w_two, spread, stretch, turn,
    lext, cext, high, low, field, tab, twiddle, twiddle_back,
    share, share_in, pair_in, part, part_in, duo, mixed_in, folded, folded_in,
    left, right, side_in, rows_in, row_c_in,
    l_shift, c_shift, h_shift, slope, band_one, band_two, band_tail, band_back, sum_one, sum_two,
    mine, sum_c, chunk, sum_g, done, gathered,
    local_sem, halo_send, halo_recv, a_send, a_recv, zp_send, zp_recv, b_send, b_recv, cp_send, cp_recv,
    c_send, c_recv, d_send, d_recv, r_send, r_recv, rg_send, rg_recv, g_send, g_recv,
):
    i = lax.axis_index("row")
    j = lax.axis_index("col")
    half = j // 4
    core = i % 2
    other = 1 - core
    pair = i + 1 - 2 * core
    n_chip = n_row // 2
    chip = i // 2
    up, down = (i + n_row - 1) % n_row, (i + 1) % n_row
    west, east = (j + n_col - 1) % n_col, (j + 1) % n_col
    cols = [(j + d) % n_col for d in range(1, n_col)]
    chips = [(chip + d) % n_chip for d in range(1, n_chip)]

    flock = [(core, c) for c in cols] + [(other, c) for c in cols] + [(other, j)]

    def here(chip):
        return 2 * chip + core

    loads = [
        pltpu.make_async_copy(src, dst, local_sem.at[n])
        for n, (src, dst) in enumerate(
            (
                (mask_h, mask),
                (feat_h.at[:, 0:16], feat.at[:, 0:16]),
                (turn_h, turn),
                (cot_h.at[:, 0:16], cot.at[:, 0:16]),
                (feat_h.at[:, 16:32], feat.at[:, 16:32]),
                (cot_h.at[:, 16:32], cot.at[:, 16:32]),
                (col_tab.at[j], tab),
                (row_tab.at[2 * i + half], twiddle),
                (back_tab.at[2 * i + half], twiddle_back),
                (one_h, w_one),
                (two_h, w_two),
                (spread_h, spread),
                (stretch_h, stretch),
                (real_h, w_real),
                (imag_h, w_imag),
            )
        )
    ]
    begin(loads)

    barrier = pltpu.get_barrier_semaphore()
    partners = (
        [(i, c) for c in cols]
        + [(here(g), j) for g in chips]
        + [(pair, j)]
        + [(pair, c) for c in cols]
        + [(r, c) for r in (up, down) for c in (j, west, east)]
    )
    for partner in partners:
        pl.semaphore_signal(barrier, inc=1, device_id=partner, device_id_type=MESH)

    def first_half():
        for load in loads[0:4]:
            load.wait()

    def second_half():
        for load in loads[4:6]:
            load.wait()

    prepare(feat, mask, gain, cot, turn, lext, cext, field, (first_half, second_half))

    first_l = lext[4:36, :, 0:128].reshape(1024, 128)
    last_l = lext[4:36, :, 384:512].reshape(1024, 128)
    first_c = cext[4:36, :, 0:128].reshape(1024, 128)
    last_c = cext[4:36, :, 384:512].reshape(1024, 128)
    sel = (16, 128)
    left[...] = (
        dot(pick(sel, ((0, 0), (1, 1))), first_l, NT) + dot(pick(sel, ((2, 0),)), first_c, NT)
    )[0:4]
    right[...] = (
        dot(pick(sel, ((0, 126), (1, 127))), last_l, NT) + dot(pick(sel, ((2, 127),)), last_c, NT)
    )[0:4]
    pl.semaphore_wait(barrier, len(partners))

    plan = [
        (lext.at[4:6, :, 0:512], rows_in.at[1], up, j),
        (lext.at[34:36, :, 0:512], rows_in.at[0], down, j),
        (cext.at[4:5, :, 0:512], row_c_in.at[1], up, j),
        (cext.at[35:36, :, 0:512], row_c_in.at[0], down, j),
        (left, side_in.at[1, :, 128:1152], i, west),
        (right, side_in.at[0, :, 128:1152], i, east),
        (left.at[:, 0:128], side_in.at[1, :, 1152:1280], up, west),
        (right.at[:, 0:128], side_in.at[0, :, 1152:1280], up, east),
        (left.at[:, 896:1024], side_in.at[1, :, 0:128], down, west),
        (right.at[:, 896:1024], side_in.at[0, :, 0:128], down, east),
    ]
    halos = remote_to(plan, halo_send, halo_recv)
    begin(halos)

    loads[6].wait()
    share[:, 0:128] = transform(tab[0], field[0:4].reshape(128, 512))
    share[:, 128:320] = transform(tab[1], field[4:10].reshape(192, 512))
    share[:, 320:384] = jnp.zeros((64, 64), F32)

    def group(c):
        return pl.ds(pl.multiple_of(16 * (c % 4), 16), 16)

    a_copies = remote_to([(share.at[group(c)], share_in.at[j], i, c) for c in cols], a_send, a_recv)
    begin(a_copies)
    share_in[j] = share[group(j), :]

    for load in loads[7:]:
        load.wait()
    eye = jnp.where(
        lax.broadcasted_iota(jnp.int32, (32, 32), 0) == lax.broadcasted_iota(jnp.int32, (32, 32), 1),
        1.0,
        0.0,
    ).astype(BF16)
    block = lane_group((32, 256))
    line = lax.broadcasted_iota(jnp.int32, (256, 384), 0) % 8
    wide_block = lane_group((256, 384))
    for v in range(3):
        ones, backs, twos = [], [], []
        for u in range(3):
            one = tiled(w_one[3 * u + v].astype(F32))
            ones.append(jnp.concatenate([one, one], axis=1))
            back = tiled(dot(eye, w_two[3 * u + v], NT))
            backs.append(jnp.concatenate([back, back], axis=1))
            two = tiled(w_two[3 * u + v].astype(F32))
            twos.append(jnp.concatenate([two, two, two], axis=1).astype(BF16))
        for r in range(6):
            one = jnp.zeros((32, 256), F32)
            back = jnp.zeros((32, 256), F32)
            for u in range(3):
                one = one + jnp.where(block == r + u, ones[u], 0.0)
                back = back + jnp.where(block == r + 2 - u, backs[u], 0.0)
            band_one[v, 32 * r : 32 * r + 32, :] = one.astype(BF16)
            band_back[v, 32 * r : 32 * r + 32, :] = back.astype(BF16)
        total = jnp.zeros((256, 384), F32)
        for u in range(3):
            total = total + jnp.where(
                wide_block - line == u, dot(spread[...], twos[u], NN), 0.0
            )
        band_two[v] = total[:, 0:256].astype(BF16)
        band_tail[:, 64 * v : 64 * v + 64] = total[:, 256:320].astype(BF16)
    band_tail[:, 192:288] = stretch[...]
    band_tail[:, 288:384] = stretch[...]

    arrive(a_copies)
    total_a = share_in[0]
    for k in range(1, n_col):
        total_a = total_a + share_in[k]
    pair_in[core] = total_a
    zp_copies = remote_to([(pair_in.at[core], pair_in.at[core], pair, j)], zp_send, zp_recv)
    begin(zp_copies)
    for k in range(8):
        rows = slice(4 + 4 * k, 8 + 4 * k)
        for ref, shift in ((lext, l_shift), (cext, c_shift)):
            value = ref[rows, :, 0:512].reshape(128, 512)
            shift[0, rows, :, 0:512] = shifted(value, 1).reshape(4, 32, 512)
            shift[1, rows, :, 0:512] = shifted(value, -1).reshape(4, 32, 512)

    arrive(halos)
    lext[2:4, :, 0:512] = rows_in[0]
    lext[36:38, :, 0:512] = rows_in[1]
    cext[3:4, :, 0:512] = row_c_in[0]
    cext[36:37, :, 0:512] = row_c_in[1]
    sides = jnp.concatenate([side_in[0], side_in[1]], axis=0).astype(BF16)
    at_l = pick((8, 128), ((0, 126), (1, 127), (4, 0), (5, 1)))
    at_c = pick((8, 128), ((2, 127), (6, 0)))
    lext[:, :, 512:640] = dot(sides, at_l, TN).astype(BF16).reshape(40, 32, 128)
    cext[:, :, 512:640] = dot(sides, at_c, TN).astype(BF16).reshape(40, 32, 128)

    def column_tile(ref, rows, t):
        return ref[rows, :, 128 * t : 128 * t + 128].reshape(-1, 128)

    def joined(pieces):
        return jnp.concatenate(pieces, axis=1).reshape(-1, 32, 128)

    for ref, shift, rows in ((lext, l_shift, slice(2, 38)), (cext, c_shift, slice(3, 37))):
        for row in (slice(rows.start, 4), slice(36, rows.stop)):
            value = ref[row].reshape(-1, 640)
            shift[0, row, :, 0:512] = shifted(value, 1)[:, 0:512].reshape(-1, 32, 512)
            shift[1, row, :, 0:512] = shifted(value, -1)[:, 0:512].reshape(-1, 32, 512)
        start, last, side = (column_tile(ref, rows, t) for t in (0, 3, 4))
        shift[0, rows, :, 0:128] = joined([side[:, 127:128], start[:, 0:127]])
        shift[1, rows, :, 384:512] = joined([last[:, 1:128], side[:, 0:1]])
        if ref is lext:
            shift[0, rows, :, 512:640] = joined([last[:, 127:128], side[:, 0:127]])
            shift[1, rows, :, 512:640] = joined([side[:, 1:128], start[:, 0:1]])

    arrive(zp_copies)
    ps, qs = [], []
    for n in range(10):
        p_sum = jnp.zeros((8, 128), F32)
        q_sum = jnp.zeros((8, 128), F32)
        for b in range(2):
            kk = n - 4 * b
            if not 0 <= kk <= 5:
                continue
            pieces = [(128 + 32 * kk, 1)]
            if 1 <= kk <= 4:
                pieces.append((32 * kk - 32, 0))
            for at, kind in pieces:
                lanes = slice(128 * (at // 128), 128 * (at // 128) + 128)
                re, im = pair_in[b, 0:8, lanes], pair_in[b, 8:16, lanes]
                source = (at % 128) // 32
                p_sum = p_sum + place(re, source, kind) + place(im, source, kind + 2)
                q_sum = q_sum + place(im, source, kind) - place(re, source, kind + 2)
        ps.append(p_sum)
        qs.append(q_sum)

    def row_transform(l, _):
        for b in range(4):
            out = jnp.zeros((8, 128), F32)
            for n in range(10):
                at = 32 * b + 2 * n
                out = out + twiddle[l, at] * ps[n] + twiddle[l, at + 1] * qs[n]
            part[4 * l + b] = out
        return 0

    lax.fori_loop(0, n_chip // 4, row_transform, 0)
    b_copies = remote_to([(part.at[g], part_in.at[chip], here(g), j) for g in chips], b_send, b_recv)
    begin(b_copies)
    part_in[chip] = part[chip]

    def forward(k):
        at = min(6 * k, 28)
        rows = pl.ds(at + 2, 8)
        pre = dot(band_one[1], lext[rows].reshape(256, 640), NN)
        pre = pre + dot(band_one[0], l_shift[0, rows].reshape(256, 640), NN)
        pre = pre + dot(band_one[2], l_shift[1, rows].reshape(256, 640), NN)
        square = pre * pre
        bend = jnp.tanh(pre * (GELU_A + (GELU_A * GELU_B) * square))
        half = 0.5 + 0.5 * bend
        hidden = (pre * half).astype(BF16)
        rise = half + pre * (0.5 - 0.5 * (bend * bend)) * (GELU_A + (3.0 * GELU_A * GELU_B) * square)
        slope[pl.ds(at, 6)] = rise[:, 0:512].reshape(6, 32, 512)
        to = pl.ds(at, 6)
        h_shift[1, to] = hidden[:, 0:512].reshape(6, 32, 512)
        h_shift[0, to] = shifted(hidden, 1)[:, 0:512].reshape(6, 32, 512)
        h_shift[2, to] = shifted(hidden, -1)[:, 0:512].reshape(6, 32, 512)

    for k in range(6):
        forward(k)
    sum_one[...] = jnp.zeros_like(sum_one)
    sum_two[...] = jnp.zeros_like(sum_two)
    counted = lax.broadcasted_iota(jnp.int32, (192, 512), 0) < 128

    def backward(k):
        at = min(6 * k, 26)
        rows = pl.ds(at + 3, 8)
        grad = dot(band_back[1], cext[rows, :, 0:512].reshape(256, 512), NN)
        grad = grad + dot(band_back[0], c_shift[1, rows].reshape(256, 512), NN)
        grad = grad + dot(band_back[2], c_shift[0, rows].reshape(256, 512), NN)
        pre_grad = grad * slope[pl.ds(at + 1, 6)].reshape(192, 512)
        if k == 5:
            pre_grad = jnp.where(counted, 0.0, pre_grad)
        pre_grad = pre_grad.astype(BF16)
        own = cext[pl.ds(at + 4, 6), :, 0:512].reshape(192, 512)
        if k == 5:
            own = jnp.where(counted, 0.0, own.astype(F32)).astype(BF16)
        for v in range(3):
            sum_two[v] += dot(own, h_shift[v, pl.ds(at, 8)].reshape(256, 512), NT)
            if v == 1:
                layer = lext[rows, :, 0:512]
            else:
                layer = l_shift[v // 2, rows, :, 0:512]
            sum_one[v] += dot(pre_grad, layer.reshape(256, 512), NT)

    for k in range(6):
        backward(k)
    column = lax.broadcasted_iota(jnp.int32, (32, 128), 1)
    for n, sums in enumerate((sum_one, sum_two)):
        for v in range(3):
            near = [sums[v, 32 * r : 32 * r + 32, 0:128] for r in range(4)]
            far = [sums[v, 32 * r : 32 * r + 32, 128:256] for r in range(2, 6)]
            total = near[0] + far[2]
            total = total + pltpu.roll(near[1] + far[3], 96, 1)
            total = total + pltpu.roll(jnp.where(column >= 64, near[2], far[0]), 64, 1)
            total = total + pltpu.roll(jnp.where(column >= 96, near[3], far[1]), 32, 1)
            for e in range(8):
                at = 96 * n + 32 * v + 4 * e
                piece = at // 12
                mine[piece // n_col, piece % n_col, at % 12 : at % 12 + 4, :] = total[4 * e : 4 * e + 4, :]
    r_copies = remote_to([(mine.at[b, c], sum_c.at[core, j], 2 * chip + b, c) for b, c in flock], r_send, r_recv)
    begin(r_copies)
    sum_c[core, j] = mine[core, j]

    arrive(b_copies)
    spectrum = part_in[0]
    for k in range(1, n_chip):
        spectrum = spectrum + part_in[k]

    groups = lane_group((8, 128))
    row = lax.broadcasted_iota(jnp.int32, (8, 128), 0)
    first = (row == 0) & (j % 4 == 0)
    twice = jnp.where(first, 1.0, 2.0)
    spectrum = spectrum * jnp.where(groups % 2 == 1, twice * scaling, scaling)
    s_re = everywhere(jnp.where(groups == 0, spectrum, 0.0))
    m_re = everywhere(jnp.where(groups == 1, spectrum, 0.0))
    s_im = everywhere(jnp.where(groups == 2, spectrum, 0.0))
    m_im = everywhere(jnp.where(groups == 3, spectrum, 0.0))
    wide = lane_group((16, 256)) == lax.broadcasted_iota(jnp.int32, (16, 256), 0) % 8
    both = jnp.concatenate([s_re, s_im], axis=0)[:, 0:32]
    both = jnp.concatenate(parts_of(both, 3), axis=0)
    by = dot(both, jnp.concatenate([w_real[...].reshape(256, 32), w_imag[...].reshape(256, 32)], axis=0), NT)
    by = by[0:16] + by[16:32] + by[32:48]
    by_real = jnp.where(wide, by[:, 0:256], 0.0)
    by_imag = jnp.where(wide, by[:, 256:512], 0.0)
    mixed_re = by_real[0:8] - by_imag[8:16]
    mixed_im = by_real[8:16] + by_imag[0:8]
    mixed_re = everywhere(mixed_re[:, 0:128] + mixed_re[:, 128:256])
    mixed_im = everywhere(mixed_im[:, 0:128] + mixed_im[:, 128:256])
    upper = jnp.where(groups == 0, mixed_re, mixed_im)
    duo[core] = jnp.where(groups[0:4] < 2, upper[0:4], jnp.where(groups[0:4] == 2, mixed_re[4:8], mixed_im[4:8]))

    cp_copies = remote_to([(duo.at[core], duo.at[core], pair, j)], cp_send, cp_recv)
    begin(cp_copies)
    arrive(cp_copies)

    def two(chip):
        return pl.ds(pl.multiple_of(2 * chip, 2), 2)

    c_copies = remote_to([(duo, mixed_in.at[two(chip)], here(g), j) for g in chips], c_send, c_recv)
    begin(c_copies)
    mixed_in[two(chip)] = duo[...]
    grads = jnp.concatenate(
        [jnp.concatenate([m_re, m_re], axis=1), jnp.concatenate([m_im, m_im], axis=1)], axis=0
    )
    grads = jnp.where(wide, grads, 0.0)
    fields = jnp.concatenate(
        [jnp.where(groups == 0, s_re, -s_im), jnp.where(groups == 0, s_im, s_re)], axis=0
    )
    outer = dot(grads, fields, TN, HIGH)
    outer_out[...] = outer

    arrive(r_copies)
    value = sum_c[0, 0]
    for k in range(1, 2 * n_col):
        value = value + sum_c[k // n_col, k % n_col]
    chunk[...] = value
    rg_copies = remote_to([(chunk, sum_g.at[chip], here(g), j) for g in chips], rg_send, rg_recv)
    begin(rg_copies)
    sum_g[chip] = value

    arrive(c_copies)
    def inverse(l, sums):
        sums = list(sums)
        for b in range(4):
            value = mixed_in[4 * l + b]
            for n in range(12):
                sums[n] = sums[n] + twiddle_back[l, 16 * b + n] * value
        return tuple(sums)

    sums = lax.fori_loop(0, n_row // 4, inverse, (jnp.zeros((4, 128), F32),) * 12)
    folded[:, 192:256] = jnp.zeros((16, 64), F32)
    grown = jnp.where((groups[0:4] < 2), twice[0:4], 2.0) * scaling
    even = groups[0:4] % 2 == 0
    for kk in range(6):
        sines = sums[2 * kk + 1]
        sines = jnp.where(even, -pltpu.roll(sines, 96, 1), pltpu.roll(sines, 32, 1))
        value = (sums[2 * kk] + sines) * grown
        for n in range(4):
            at = 8 * (n % 2) + 4 * (n // 2)
            folded[at : at + 4, 32 * kk : 32 * kk + 32] = value[:, 32 * n : 32 * n + 32]

    d_copies = remote_to([(folded, folded_in.at[j], i, c) for c in cols], d_send, d_recv)
    begin(d_copies)
    folded_in[j] = folded[...]

    arrive(rg_copies)
    value = sum_g[0]
    for k in range(1, n_chip):
        value = value + sum_g[k]
    value = value * scale
    done[...] = value
    g_copies = remote_to([(done, gathered.at[core, j], 2 * chip + b, c) for b, c in flock], g_send, g_recv)
    begin(g_copies)
    gathered[core, j] = value
    arrive(d_copies)
    waves = (folded_in[0:4] + folded_in[4:8]).reshape(64, 256)
    upper, lower = parts_of(waves, 2)
    smooth = dot(
        jnp.concatenate([upper, upper, lower], axis=0),
        jnp.concatenate([tab[1], tab[1, 0:64]], axis=0),
        TN,
    )[0:192]
    upper = smooth.astype(BF16)
    high[...] = upper
    low[...] = (smooth - upper.astype(F32)).astype(BF16)

    def window(t):
        coarse = slice(32 * t, 32 * t + 96)
        rest = [h_shift[v, 8 * t + 8 : 8 * t + 10].reshape(64, 512) for v in range(3)]
        rest = jnp.concatenate(rest + [high[coarse, :], low[coarse, :]], axis=0)
        total = dot(band_tail[...], rest, NN)
        for v in range(3):
            total = total + dot(band_two[v], h_shift[v, 8 * t : 8 * t + 8].reshape(256, 512), NN)
        return total.reshape(32, 8, 512)

    for t in range(2):
        rows = slice(16 * t, 16 * t + 16)
        value = jnp.concatenate([window(2 * t), window(2 * t + 1)], axis=1)
        stage_out[:, rows, :] = value.astype(BF16)

    for copies in (
        a_copies, halos, zp_copies, b_copies, cp_copies, c_copies, d_copies, r_copies, rg_copies
    ):
        leave(copies)
    arrive(g_copies)
    for e in range(48):
        piece, at = divmod(4 * e, 12)
        total_out[4 * e : 4 * e + 4, :] = gathered[piece // n_col, piece % n_col, at : at + 4, :]
    leave(g_copies)


def finish_kernel(stage, total, outer, out, out_one, out_two, g_real, g_imag, sem):
    copy = pltpu.make_async_copy(stage, out, sem)
    copy.start()
    value = total[...]
    for n, grad in enumerate((out_one, out_two)):
        for v in range(3):
            at = 96 * n + 32 * v
            for u in range(3):
                grad[3 * u + v] = value[at : at + 32, 32 * u : 32 * u + 32]
    g_real[...] = outer[:, 0:32].reshape(8, 32, 32)
    g_imag[...] = outer[:, 32:64].reshape(8, 32, 32)
    copy.wait()


def body(n_row, n_col, features, mask, mask_gain, conv_one, conv_two, spec_real, spec_imag, cotangent):
    total_rows, total_cols = 32 * n_row, 512 * n_col
    scaling = 1.0 / math.sqrt((total_rows // RATIO) * (total_cols // RATIO))
    vmem = pl.BlockSpec(memory_space=pltpu.VMEM)
    hbm = pl.BlockSpec(memory_space=pl.ANY)
    col_tab = jnp.asarray(column_tables(n_col))
    row_tab, back_tab = (jnp.asarray(table) for table in row_tables(n_row))
    spread = jnp.asarray(expand_table(), BF16)
    stretch = jnp.asarray(prolong_table(), BF16)
    turn = jnp.asarray(turn_table(), BF16)
    dma = pltpu.SemaphoreType.DMA
    stage, total, outer = pl.pallas_call(
        functools.partial(
            main_kernel, n_row, n_col, scaling, 1.0 / math.sqrt(total_rows * total_cols)
        ),
        out_shape=[
            pltpu.VMEM((32, 32, 512), BF16),
            pltpu.VMEM((192, 128), F32),
            pltpu.VMEM((256, 128), F32),
        ],
        in_specs=[hbm] * 2 + [pl.BlockSpec(memory_space=pltpu.SMEM)] + [hbm] * 11,
        out_specs=[vmem] * 3,
        scratch_shapes=[
            pltpu.VMEM((32, 32, 512), BF16),
            pltpu.VMEM((32, 512), jnp.int32),
            pltpu.VMEM((32, 32, 512), BF16),
            pltpu.VMEM((8, 32, 32), BF16),
            pltpu.VMEM((8, 32, 32), BF16),
            pltpu.VMEM((9, 32, 32), BF16),
            pltpu.VMEM((9, 32, 32), BF16),
            pltpu.VMEM(spread.shape, BF16),
            pltpu.VMEM(stretch.shape, BF16),
            pltpu.VMEM(turn.shape, BF16),
            pltpu.VMEM((40, 32, 640), BF16),
            pltpu.VMEM((40, 32, 640), BF16),
            pltpu.VMEM((192, 512), BF16),
            pltpu.VMEM((192, 512), BF16),
            pltpu.VMEM((10, 32, 512), F32),
            pltpu.VMEM((2, 128, 512), BF16),
            pltpu.SMEM(row_tab.shape[1:], F32),
            pltpu.SMEM(back_tab.shape[1:], F32),
            pltpu.VMEM((64, 384), F32),
            pltpu.VMEM((n_col, 16, 384), F32),
            pltpu.VMEM((2, 16, 384), F32),
            pltpu.VMEM((n_row // 2, 8, 128), F32),
            pltpu.VMEM((n_row // 2, 8, 128), F32),
            pltpu.VMEM((2, 4, 128), F32),
            pltpu.VMEM((n_row, 4, 128), F32),
            pltpu.VMEM((16, 256), F32),
            pltpu.VMEM((n_col, 16, 256), F32),
            pltpu.VMEM((4, 1024), F32),
            pltpu.VMEM((4, 1024), F32),
            pltpu.VMEM((2, 4, 1280), F32),
            pltpu.VMEM((2, 2, 32, 512), BF16),
            pltpu.VMEM((2, 1, 32, 512), BF16),
            pltpu.VMEM((2, 40, 32, 640), BF16),
            pltpu.VMEM((2, 40, 32, 512), BF16),
            pltpu.VMEM((3, 34, 32, 512), BF16),
            pltpu.VMEM((34, 32, 512), F32),
            pltpu.VMEM((3, 192, 256), BF16),
            pltpu.VMEM((3, 256, 256), BF16),
            pltpu.VMEM((256, 384), BF16),
            pltpu.VMEM((3, 192, 256), BF16),
            pltpu.VMEM((3, 192, 256), F32),
            pltpu.VMEM((3, 192, 256), F32),
            pltpu.VMEM((2, n_col, 12, 128), F32),
            pltpu.VMEM((2, n_col, 12, 128), F32),
            pltpu.VMEM((12, 128), F32),
            pltpu.VMEM((n_row // 2, 12, 128), F32),
            pltpu.VMEM((12, 128), F32),
            pltpu.VMEM((2, n_col, 12, 128), F32),
            dma((17,)),
            dma((10,)),
            dma((10,)),
            *[dma((16,))] * 18,
        ],
        compiler_params=pltpu.CompilerParams(
            collective_id=0, has_side_effects=True, vmem_limit_bytes=VMEM_LIMIT
        ),
        name="layer",
    )(
        features, mask, mask_gain, cotangent, spec_real, spec_imag, conv_one, conv_two,
        spread, stretch, turn, col_tab, row_tab, back_tab,
    )
    return pl.pallas_call(
        finish_kernel,
        out_shape=[
            jax.ShapeDtypeStruct((32, 32, 512), BF16),
            jax.ShapeDtypeStruct((9, 32, 32), F32),
            jax.ShapeDtypeStruct((9, 32, 32), F32),
            jax.ShapeDtypeStruct((8, 32, 32), F32),
            jax.ShapeDtypeStruct((8, 32, 32), F32),
        ],
        in_specs=[vmem] * 3,
        out_specs=[hbm] + [vmem] * 4,
        scratch_shapes=[dma],
        compiler_params=pltpu.CompilerParams(vmem_limit_bytes=VMEM_LIMIT),
        name="finish",
    )(*(pltpu.with_memory_space_constraint(value, pltpu.VMEM) for value in (stage, total, outer)))


def solution(mesh):
    n_row, n_col = mesh.shape["row"], mesh.shape["col"]
    placed = (
        P(None, "row", "col"),
        P("row", "col"),
        P(),
        P(),
        P(),
        P(("row", "col"), None, None),
        P(("row", "col"), None, None),
        P(None, "row", "col"),
    )
    return jax.shard_map(
        functools.partial(body, n_row, n_col),
        mesh=mesh,
        in_specs=placed,
        out_specs=(
            P(None, "row", "col"),
            P(),
            P(),
            P(("row", "col"), None, None),
            P(("row", "col"), None, None),
        ),
        check_vma=False,
    )
```

```python
import functools
import math

import jax
import jax.numpy as jnp
import ml_dtypes
import numpy as np
from jax import lax
from jax.experimental import pallas as pl
from jax.experimental.pallas import tpu as pltpu
from jax.sharding import PartitionSpec as P

C = 32
M = 32
RATIO = 8
MESH = pl.DeviceIdType.MESH
HIGH = lax.Precision.HIGHEST
F32 = jnp.float32
BF16 = jnp.bfloat16
GELU_A = math.sqrt(2.0 / math.pi)
GELU_B = 0.044715
VMEM_LIMIT = 56 * 2**20
NT = (((1,), (1,)), ((), ()))
TN = (((0,), (0,)), ((), ()))
NN = (((1,), (0,)), ((), ()))


def dot(a, b, dims, precision=None):
    return lax.dot_general(a, b, dims, preferred_element_type=F32, precision=precision)


def weights_np():
    d = (np.arange(RATIO) + 0.5 - RATIO / 2) / RATIO
    return np.stack([np.maximum(-d, 0.0), 1.0 - np.abs(d), np.maximum(d, 0.0)])


def column_tables(n_col):
    w = weights_np()
    n_two = 64 * n_col
    r = np.arange(M)
    out = np.zeros((n_col, 2, 64, 512))
    for j in range(n_col):
        fine = np.arange(512)
        cell, s = 64 * j + fine // RATIO, fine % RATIO

        def wave(at):
            return np.exp(-2j * np.pi * ((r[:, None] * at[None, :]) % n_two) / n_two)

        mean = wave(cell) / 64.0
        restrict = sum(w[b + 1][s][None, :] * wave(cell + b) for b in (-1, 0, 1))
        for kind, value in enumerate((mean, restrict)):
            parts = np.stack([value.real, value.imag], axis=0).reshape(2, 4, 8, 512)
            out[j, kind] = parts.transpose(1, 0, 2, 3).reshape(64, 512)
    out = out.astype(np.float32)
    upper = out.astype(ml_dtypes.bfloat16)
    lower = (out - upper.astype(np.float32)).astype(ml_dtypes.bfloat16)
    return np.concatenate([upper, lower], axis=2)


def row_tables(n_row):
    n_one = 4 * n_row
    q_all = np.arange(2 * n_row)
    f1 = np.where(q_all < n_row, q_all, n_one - 2 * n_row + q_all)

    def waves(q, rows):
        phase = 2 * np.pi * ((f1[q][:, None] * rows[None, :]) % n_one) / n_one
        return np.stack([np.cos(phase), np.sin(phase)], axis=-1).reshape(len(q), -1)

    there, back = [], []
    for i in range(n_row):
        for h in range(2):
            peers = 2 * np.arange(n_row // 2) + i % 2
            value = waves(2 * peers + h, 8 * (i // 2) - 1 + np.arange(10))
            there.append(np.pad(value, ((0, 0), (0, 12))).reshape(-1, 128))
            value = waves(2 * np.arange(n_row) + h, 4 * i - 1 + np.arange(6))
            value = np.pad(value, ((0, 0), (0, 4))).reshape(-1, 64)
            back.append(np.pad(value, ((0, 0), (0, 64))))
    return np.stack(there).astype(np.float32), np.stack(back).astype(np.float32)


def prolong_table():
    w = weights_np()
    out = np.zeros((C, RATIO, 3, C))
    for c in range(C):
        out[c, :, :, c] = w.T
    return out.reshape(C * RATIO, 3 * C).astype(np.float32)


def turn_table():
    w = weights_np()
    sums = np.zeros((2, C, C, 16))
    turn = np.zeros((16, C, C, 16))
    restrict = np.zeros((4, C, C, 16))
    for c in range(C):
        for row in range(16):
            cell, p = row // RATIO, row % RATIO
            sums[cell, c, c, row] = 1.0
            turn[row, c, c, row] = 1.0
            for a in (-1, 0, 1):
                restrict[cell + a + 1, c, c, row] = w[a + 1][p]
    return np.concatenate([t.reshape(-1, C * 16) for t in (sums, turn, restrict)], axis=0).astype(np.float32)


def expand_table():
    return np.repeat(np.eye(C), RATIO, axis=0).astype(np.float32)


def lane_group(shape):
    return lax.broadcasted_iota(jnp.int32, shape, len(shape) - 1) // 32


def place(value, source, target):
    shift = (32 * (target - source)) % 128
    moved = pltpu.roll(value, shift, 1) if shift else value
    return jnp.where(lane_group(value.shape) == target, moved, 0.0)


def everywhere(value):
    value = value + pltpu.roll(value, 64, 1)
    return value + pltpu.roll(value, 32, 1)


def remote(src, dst, send, recv, row, col):
    return pltpu.make_async_remote_copy(
        src_ref=src,
        dst_ref=dst,
        send_sem=send,
        recv_sem=recv,
        device_id=(row, col),
        device_id_type=MESH,
    )


def remote_to(plan, send, recv):
    return [
        remote(src, dst, send.at[n], recv.at[n], row, col)
        for n, (src, dst, row, col) in enumerate(plan)
    ]


def begin(copies):
    for copy in copies:
        copy.start()


def arrive(copies):
    for copy in copies:
        copy.wait_recv()


def leave(copies):
    for copy in copies:
        copy.wait_send()


def prepare(feat, mask, gain, cot, turn, lext, cext, field, ready):
    for half in range(2):
        ready[half]()
        rows = slice(16 * half, 16 * half + 16)
        to = slice(4 + 16 * half, 20 + 16 * half)
        raised = mask[rows, :].astype(F32) - 0.5
        for c in range(C):
            feat[c, rows, :] = (feat[c, rows, :].astype(F32) + gain[c] * raised).astype(BF16)
        turned = dot(turn[0:576], feat[:, rows, :].reshape(512, 512), NN)
        field[2 * half : 2 * half + 2] = turned[0:64].reshape(2, 32, 512)
        lext[to, :, 0:512] = turned[64:576].astype(BF16).reshape(16, 32, 512)
        turned = dot(turn[64:704], cot[:, rows, :].reshape(512, 512), NN)
        cext[to, :, 0:512] = turned[0:512].astype(BF16).reshape(16, 32, 512)
        sums = turned[512:640].reshape(4, 32, 512)
        if half == 0:
            field[4:8] = sums
        else:
            field[6:8] = field[6:8] + sums[0:2]
            field[8:10] = sums[2:4]


def parts_of(value, count):
    out = []
    for _ in range(count):
        part = value.astype(BF16)
        out.append(part)
        value = value - part.astype(F32)
    return out


def transform(table, value):
    upper, lower = parts_of(value, 2)
    whole = dot(table, upper, NT)
    return whole[0:64] + whole[64:128] + dot(table[0:64], lower, NT)


def pick(shape, pairs):
    row = lax.broadcasted_iota(jnp.int32, shape, 0)
    lane = lax.broadcasted_iota(jnp.int32, shape, 1)
    hit = jnp.zeros(shape, jnp.bool_)
    for r, l in pairs:
        hit = hit | ((row == r) & (lane == l))
    return jnp.where(hit, 1.0, 0.0).astype(BF16)


def tiled(value):
    wide = jnp.concatenate([value, jnp.zeros((32, 96), value.dtype)], axis=1)
    return everywhere(wide)


def shifted(value, by):
    width = value.shape[1]
    if by > 0:
        return jnp.concatenate([value[:, width - by :], value[:, : width - by]], axis=1)
    return jnp.concatenate([value[:, -by:], value[:, :-by]], axis=1)


def main_kernel(
    n_row, n_col, scaling, scale,
    feat_h, mask_h, gain, cot_h, real_h, imag_h, one_h, two_h, spread_h, stretch_h, turn_h, col_tab, row_tab, back_tab,
    stage_out, total_out, outer_out,
    feat, mask, cot, w_real, w_imag, w_one, w_two, spread, stretch, turn,
    lext, cext, high, low, field, tab, twiddle, twiddle_back,
    share, share_in, pair_in, part, part_in, duo, mixed_in, folded, folded_in,
    left, right, side_in, rows_in, row_c_in,
    l_shift, c_shift, h_shift, slope, band_one, band_two, band_tail, band_back, sum_one, sum_two,
    mine, sum_c, chunk, sum_g, done, gathered,
    local_sem, halo_send, halo_recv, a_send, a_recv, zp_send, zp_recv, b_send, b_recv, cp_send, cp_recv,
    c_send, c_recv, d_send, d_recv, r_send, r_recv, rg_send, rg_recv, g_send, g_recv,
):
    i = lax.axis_index("row")
    j = lax.axis_index("col")
    half = j // 4
    core = i % 2
    other = 1 - core
    pair = i + 1 - 2 * core
    n_chip = n_row // 2
    chip = i // 2
    up, down = (i + n_row - 1) % n_row, (i + 1) % n_row
    west, east = (j + n_col - 1) % n_col, (j + 1) % n_col
    cols = [(j + d) % n_col for d in range(1, n_col)]
    chips = [(chip + d) % n_chip for d in range(1, n_chip)]

    flock = [(core, c) for c in cols] + [(other, c) for c in cols] + [(other, j)]

    def here(chip):
        return 2 * chip + core

    loads = [
        pltpu.make_async_copy(src, dst, local_sem.at[n])
        for n, (src, dst) in enumerate(
            (
                (mask_h, mask),
                (feat_h.at[:, 0:16], feat.at[:, 0:16]),
                (turn_h, turn),
                (cot_h.at[:, 0:16], cot.at[:, 0:16]),
                (feat_h.at[:, 16:32], feat.at[:, 16:32]),
                (cot_h.at[:, 16:32], cot.at[:, 16:32]),
                (col_tab.at[j], tab),
                (row_tab.at[2 * i + half], twiddle),
                (back_tab.at[2 * i + half], twiddle_back),
                (one_h, w_one),
                (two_h, w_two),
                (spread_h, spread),
                (stretch_h, stretch),
                (real_h, w_real),
                (imag_h, w_imag),
            )
        )
    ]
    begin(loads)

    barrier = pltpu.get_barrier_semaphore()
    partners = (
        [(i, c) for c in cols]
        + [(here(g), j) for g in chips]
        + [(pair, j)]
        + [(pair, c) for c in cols]
        + [(r, c) for r in (up, down) for c in (j, west, east)]
    )
    for partner in partners:
        pl.semaphore_signal(barrier, inc=1, device_id=partner, device_id_type=MESH)

    def first_half():
        for load in loads[0:4]:
            load.wait()

    def second_half():
        for load in loads[4:6]:
            load.wait()

    prepare(feat, mask, gain, cot, turn, lext, cext, field, (first_half, second_half))

    first_l = lext[4:36, :, 0:128].reshape(1024, 128)
    last_l = lext[4:36, :, 384:512].reshape(1024, 128)
    first_c = cext[4:36, :, 0:128].reshape(1024, 128)
    last_c = cext[4:36, :, 384:512].reshape(1024, 128)
    sel = (16, 128)
    left[...] = (
        dot(pick(sel, ((0, 0), (1, 1))), first_l, NT) + dot(pick(sel, ((2, 0),)), first_c, NT)
    )[0:4]
    right[...] = (
        dot(pick(sel, ((0, 126), (1, 127))), last_l, NT) + dot(pick(sel, ((2, 127),)), last_c, NT)
    )[0:4]
    pl.semaphore_wait(barrier, len(partners))

    plan = [
        (lext.at[4:6, :, 0:512], rows_in.at[1], up, j),
        (lext.at[34:36, :, 0:512], rows_in.at[0], down, j),
        (cext.at[4:5, :, 0:512], row_c_in.at[1], up, j),
        (cext.at[35:36, :, 0:512], row_c_in.at[0], down, j),
        (left, side_in.at[1, :, 128:1152], i, west),
        (right, side_in.at[0, :, 128:1152], i, east),
        (left.at[:, 0:128], side_in.at[1, :, 1152:1280], up, west),
        (right.at[:, 0:128], side_in.at[0, :, 1152:1280], up, east),
        (left.at[:, 896:1024], side_in.at[1, :, 0:128], down, west),
        (right.at[:, 896:1024], side_in.at[0, :, 0:128], down, east),
    ]
    halos = remote_to(plan, halo_send, halo_recv)
    begin(halos)

    loads[6].wait()
    share[:, 0:128] = transform(tab[0], field[0:4].reshape(128, 512))
    share[:, 128:320] = transform(tab[1], field[4:10].reshape(192, 512))
    share[:, 320:384] = jnp.zeros((64, 64), F32)

    def group(c):
        return pl.ds(pl.multiple_of(16 * (c % 4), 16), 16)

    a_copies = remote_to([(share.at[group(c)], share_in.at[j], i, c) for c in cols], a_send, a_recv)
    begin(a_copies)
    share_in[j] = share[group(j), :]

    for load in loads[7:]:
        load.wait()
    eye = jnp.where(
        lax.broadcasted_iota(jnp.int32, (32, 32), 0) == lax.broadcasted_iota(jnp.int32, (32, 32), 1),
        1.0,
        0.0,
    ).astype(BF16)
    block = lane_group((32, 256))
    line = lax.broadcasted_iota(jnp.int32, (256, 384), 0) % 8
    wide_block = lane_group((256, 384))
    for v in range(3):
        ones, backs, twos = [], [], []
        for u in range(3):
            one = tiled(w_one[3 * u + v].astype(F32))
            ones.append(jnp.concatenate([one, one], axis=1))
            back = tiled(dot(eye, w_two[3 * u + v], NT))
            backs.append(jnp.concatenate([back, back], axis=1))
            two = tiled(w_two[3 * u + v].astype(F32))
            twos.append(jnp.concatenate([two, two, two], axis=1).astype(BF16))
        for r in range(6):
            one = jnp.zeros((32, 256), F32)
            back = jnp.zeros((32, 256), F32)
            for u in range(3):
                one = one + jnp.where(block == r + u, ones[u], 0.0)
                back = back + jnp.where(block == r + 2 - u, backs[u], 0.0)
            band_one[v, 32 * r : 32 * r + 32, :] = one.astype(BF16)
            band_back[v, 32 * r : 32 * r + 32, :] = back.astype(BF16)
        total = jnp.zeros((256, 384), F32)
        for u in range(3):
            total = total + jnp.where(
                wide_block - line == u, dot(spread[...], twos[u], NN), 0.0
            )
        band_two[v] = total[:, 0:256].astype(BF16)
        band_tail[:, 64 * v : 64 * v + 64] = total[:, 256:320].astype(BF16)
    band_tail[:, 192:288] = stretch[...]
    band_tail[:, 288:384] = stretch[...]

    arrive(a_copies)
    total_a = share_in[0]
    for k in range(1, n_col):
        total_a = total_a + share_in[k]
    pair_in[core] = total_a
    zp_copies = remote_to([(pair_in.at[core], pair_in.at[core], pair, j)], zp_send, zp_recv)
    begin(zp_copies)
    for k in range(8):
        rows = slice(4 + 4 * k, 8 + 4 * k)
        for ref, shift in ((lext, l_shift), (cext, c_shift)):
            value = ref[rows, :, 0:512].reshape(128, 512)
            shift[0, rows, :, 0:512] = shifted(value, 1).reshape(4, 32, 512)
            shift[1, rows, :, 0:512] = shifted(value, -1).reshape(4, 32, 512)

    arrive(halos)
    lext[2:4, :, 0:512] = rows_in[0]
    lext[36:38, :, 0:512] = rows_in[1]
    cext[3:4, :, 0:512] = row_c_in[0]
    cext[36:37, :, 0:512] = row_c_in[1]
    sides = jnp.concatenate([side_in[0], side_in[1]], axis=0).astype(BF16)
    at_l = pick((8, 128), ((0, 126), (1, 127), (4, 0), (5, 1)))
    at_c = pick((8, 128), ((2, 127), (6, 0)))
    lext[:, :, 512:640] = dot(sides, at_l, TN).astype(BF16).reshape(40, 32, 128)
    cext[:, :, 512:640] = dot(sides, at_c, TN).astype(BF16).reshape(40, 32, 128)

    def column_tile(ref, rows, t):
        return ref[rows, :, 128 * t : 128 * t + 128].reshape(-1, 128)

    def joined(pieces):
        return jnp.concatenate(pieces, axis=1).reshape(-1, 32, 128)

    for ref, shift, rows in ((lext, l_shift, slice(2, 38)), (cext, c_shift, slice(3, 37))):
        for row in (slice(rows.start, 4), slice(36, rows.stop)):
            value = ref[row].reshape(-1, 640)
            shift[0, row, :, 0:512] = shifted(value, 1)[:, 0:512].reshape(-1, 32, 512)
            shift[1, row, :, 0:512] = shifted(value, -1)[:, 0:512].reshape(-1, 32, 512)
        start, last, side = (column_tile(ref, rows, t) for t in (0, 3, 4))
        shift[0, rows, :, 0:128] = joined([side[:, 127:128], start[:, 0:127]])
        shift[1, rows, :, 384:512] = joined([last[:, 1:128], side[:, 0:1]])
        if ref is lext:
            shift[0, rows, :, 512:640] = joined([last[:, 127:128], side[:, 0:127]])
            shift[1, rows, :, 512:640] = joined([side[:, 1:128], start[:, 0:1]])

    arrive(zp_copies)
    ps, qs = [], []
    for n in range(10):
        p_sum = jnp.zeros((8, 128), F32)
        q_sum = jnp.zeros((8, 128), F32)
        for b in range(2):
            kk = n - 4 * b
            if not 0 <= kk <= 5:
                continue
            pieces = [(128 + 32 * kk, 1)]
            if 1 <= kk <= 4:
                pieces.append((32 * kk - 32, 0))
            for at, kind in pieces:
                lanes = slice(128 * (at // 128), 128 * (at // 128) + 128)
                re, im = pair_in[b, 0:8, lanes], pair_in[b, 8:16, lanes]
                source = (at % 128) // 32
                p_sum = p_sum + place(re, source, kind) + place(im, source, kind + 2)
                q_sum = q_sum + place(im, source, kind) - place(re, source, kind + 2)
        ps.append(p_sum)
        qs.append(q_sum)

    def row_transform(l, _):
        for b in range(4):
            out = jnp.zeros((8, 128), F32)
            for n in range(10):
                at = 32 * b + 2 * n
                out = out + twiddle[l, at] * ps[n] + twiddle[l, at + 1] * qs[n]
            part[4 * l + b] = out
        return 0

    lax.fori_loop(0, n_chip // 4, row_transform, 0, unroll=True)
    b_copies = remote_to([(part.at[g], part_in.at[chip], here(g), j) for g in chips], b_send, b_recv)
    begin(b_copies)
    part_in[chip] = part[chip]

    def forward(k):
        at = min(6 * k, 28)
        rows = pl.ds(at + 2, 8)
        pre = dot(band_one[1], lext[rows].reshape(256, 640), NN)
        pre = pre + dot(band_one[0], l_shift[0, rows].reshape(256, 640), NN)
        pre = pre + dot(band_one[2], l_shift[1, rows].reshape(256, 640), NN)
        square = pre * pre
        bend = jnp.tanh(pre * (GELU_A + (GELU_A * GELU_B) * square))
        half = 0.5 + 0.5 * bend
        hidden = (pre * half).astype(BF16)
        rise = half + pre * (0.5 - 0.5 * (bend * bend)) * (GELU_A + (3.0 * GELU_A * GELU_B) * square)
        slope[pl.ds(at, 6)] = rise[:, 0:512].reshape(6, 32, 512)
        to = pl.ds(at, 6)
        h_shift[1, to] = hidden[:, 0:512].reshape(6, 32, 512)
        h_shift[0, to] = shifted(hidden, 1)[:, 0:512].reshape(6, 32, 512)
        h_shift[2, to] = shifted(hidden, -1)[:, 0:512].reshape(6, 32, 512)

    for k in range(6):
        forward(k)
    sum_one[...] = jnp.zeros_like(sum_one)
    sum_two[...] = jnp.zeros_like(sum_two)
    counted = lax.broadcasted_iota(jnp.int32, (192, 512), 0) < 128

    def backward(k):
        at = min(6 * k, 26)
        rows = pl.ds(at + 3, 8)
        grad = dot(band_back[1], cext[rows, :, 0:512].reshape(256, 512), NN)
        grad = grad + dot(band_back[0], c_shift[1, rows].reshape(256, 512), NN)
        grad = grad + dot(band_back[2], c_shift[0, rows].reshape(256, 512), NN)
        pre_grad = grad * slope[pl.ds(at + 1, 6)].reshape(192, 512)
        if k == 5:
            pre_grad = jnp.where(counted, 0.0, pre_grad)
        pre_grad = pre_grad.astype(BF16)
        own = cext[pl.ds(at + 4, 6), :, 0:512].reshape(192, 512)
        if k == 5:
            own = jnp.where(counted, 0.0, own.astype(F32)).astype(BF16)
        for v in range(3):
            sum_two[v] += dot(own, h_shift[v, pl.ds(at, 8)].reshape(256, 512), NT)
            if v == 1:
                layer = lext[rows, :, 0:512]
            else:
                layer = l_shift[v // 2, rows, :, 0:512]
            sum_one[v] += dot(pre_grad, layer.reshape(256, 512), NT)

    for k in range(6):
        backward(k)
    column = lax.broadcasted_iota(jnp.int32, (32, 128), 1)
    for n, sums in enumerate((sum_one, sum_two)):
        for v in range(3):
            near = [sums[v, 32 * r : 32 * r + 32, 0:128] for r in range(4)]
            far = [sums[v, 32 * r : 32 * r + 32, 128:256] for r in range(2, 6)]
            total = near[0] + far[2]
            total = total + pltpu.roll(near[1] + far[3], 96, 1)
            total = total + pltpu.roll(jnp.where(column >= 64, near[2], far[0]), 64, 1)
            total = total + pltpu.roll(jnp.where(column >= 96, near[3], far[1]), 32, 1)
            for e in range(8):
                at = 96 * n + 32 * v + 4 * e
                piece = at // 12
                mine[piece // n_col, piece % n_col, at % 12 : at % 12 + 4, :] = total[4 * e : 4 * e + 4, :]
    r_copies = remote_to([(mine.at[b, c], sum_c.at[core, j], 2 * chip + b, c) for b, c in flock], r_send, r_recv)
    begin(r_copies)
    sum_c[core, j] = mine[core, j]

    arrive(b_copies)
    spectrum = part_in[0]
    for k in range(1, n_chip):
        spectrum = spectrum + part_in[k]

    groups = lane_group((8, 128))
    row = lax.broadcasted_iota(jnp.int32, (8, 128), 0)
    first = (row == 0) & (j % 4 == 0)
    twice = jnp.where(first, 1.0, 2.0)
    spectrum = spectrum * jnp.where(groups % 2 == 1, twice * scaling, scaling)
    s_re = everywhere(jnp.where(groups == 0, spectrum, 0.0))
    m_re = everywhere(jnp.where(groups == 1, spectrum, 0.0))
    s_im = everywhere(jnp.where(groups == 2, spectrum, 0.0))
    m_im = everywhere(jnp.where(groups == 3, spectrum, 0.0))
    wide = lane_group((16, 256)) == lax.broadcasted_iota(jnp.int32, (16, 256), 0) % 8
    both = jnp.concatenate([s_re, s_im], axis=0)[:, 0:32]
    both = jnp.concatenate(parts_of(both, 3), axis=0)
    by = dot(both, jnp.concatenate([w_real[...].reshape(256, 32), w_imag[...].reshape(256, 32)], axis=0), NT)
    by = by[0:16] + by[16:32] + by[32:48]
    by_real = jnp.where(wide, by[:, 0:256], 0.0)
    by_imag = jnp.where(wide, by[:, 256:512], 0.0)
    mixed_re = by_real[0:8] - by_imag[8:16]
    mixed_im = by_real[8:16] + by_imag[0:8]
    mixed_re = everywhere(mixed_re[:, 0:128] + mixed_re[:, 128:256])
    mixed_im = everywhere(mixed_im[:, 0:128] + mixed_im[:, 128:256])
    upper = jnp.where(groups == 0, mixed_re, mixed_im)
    duo[core] = jnp.where(groups[0:4] < 2, upper[0:4], jnp.where(groups[0:4] == 2, mixed_re[4:8], mixed_im[4:8]))

    cp_copies = remote_to([(duo.at[core], duo.at[core], pair, j)], cp_send, cp_recv)
    begin(cp_copies)
    arrive(cp_copies)

    def two(chip):
        return pl.ds(pl.multiple_of(2 * chip, 2), 2)

    c_copies = remote_to([(duo, mixed_in.at[two(chip)], here(g), j) for g in chips], c_send, c_recv)
    begin(c_copies)
    mixed_in[two(chip)] = duo[...]
    grads = jnp.concatenate(
        [jnp.concatenate([m_re, m_re], axis=1), jnp.concatenate([m_im, m_im], axis=1)], axis=0
    )
    grads = jnp.where(wide, grads, 0.0)
    fields = jnp.concatenate(
        [jnp.where(groups == 0, s_re, -s_im), jnp.where(groups == 0, s_im, s_re)], axis=0
    )
    outer = dot(grads, fields, TN, HIGH)
    outer_out[...] = outer

    arrive(r_copies)
    value = sum_c[0, 0]
    for k in range(1, 2 * n_col):
        value = value + sum_c[k // n_col, k % n_col]
    chunk[...] = value
    rg_copies = remote_to([(chunk, sum_g.at[chip], here(g), j) for g in chips], rg_send, rg_recv)
    begin(rg_copies)
    sum_g[chip] = value

    arrive(c_copies)
    def inverse(l, sums):
        sums = list(sums)
        for b in range(4):
            value = mixed_in[4 * l + b]
            for n in range(12):
                sums[n] = sums[n] + twiddle_back[l, 16 * b + n] * value
        return tuple(sums)

    sums = lax.fori_loop(0, n_row // 4, inverse, (jnp.zeros((4, 128), F32),) * 12, unroll=True)
    folded[:, 192:256] = jnp.zeros((16, 64), F32)
    grown = jnp.where((groups[0:4] < 2), twice[0:4], 2.0) * scaling
    even = groups[0:4] % 2 == 0
    for kk in range(6):
        sines = sums[2 * kk + 1]
        sines = jnp.where(even, -pltpu.roll(sines, 96, 1), pltpu.roll(sines, 32, 1))
        value = (sums[2 * kk] + sines) * grown
        for n in range(4):
            at = 8 * (n % 2) + 4 * (n // 2)
            folded[at : at + 4, 32 * kk : 32 * kk + 32] = value[:, 32 * n : 32 * n + 32]

    d_copies = remote_to([(folded, folded_in.at[j], i, c) for c in cols], d_send, d_recv)
    begin(d_copies)
    folded_in[j] = folded[...]

    arrive(rg_copies)
    value = sum_g[0]
    for k in range(1, n_chip):
        value = value + sum_g[k]
    value = value * scale
    done[...] = value
    g_copies = remote_to([(done, gathered.at[core, j], 2 * chip + b, c) for b, c in flock], g_send, g_recv)
    begin(g_copies)
    gathered[core, j] = value
    arrive(d_copies)
    waves = (folded_in[0:4] + folded_in[4:8]).reshape(64, 256)
    upper, lower = parts_of(waves, 2)
    smooth = dot(
        jnp.concatenate([upper, upper, lower], axis=0),
        jnp.concatenate([tab[1], tab[1, 0:64]], axis=0),
        TN,
    )[0:192]
    upper = smooth.astype(BF16)
    high[...] = upper
    low[...] = (smooth - upper.astype(F32)).astype(BF16)

    def window(t):
        coarse = slice(32 * t, 32 * t + 96)
        rest = [h_shift[v, 8 * t + 8 : 8 * t + 10].reshape(64, 512) for v in range(3)]
        rest = jnp.concatenate(rest + [high[coarse, :], low[coarse, :]], axis=0)
        total = dot(band_tail[...], rest, NN)
        for v in range(3):
            total = total + dot(band_two[v], h_shift[v, 8 * t : 8 * t + 8].reshape(256, 512), NN)
        return total.reshape(32, 8, 512)

    for t in range(2):
        rows = slice(16 * t, 16 * t + 16)
        value = jnp.concatenate([window(2 * t), window(2 * t + 1)], axis=1)
        stage_out[:, rows, :] = value.astype(BF16)

    for copies in (
        a_copies, halos, zp_copies, b_copies, cp_copies, c_copies, d_copies, r_copies, rg_copies
    ):
        leave(copies)
    arrive(g_copies)
    for e in range(48):
        piece, at = divmod(4 * e, 12)
        total_out[4 * e : 4 * e + 4, :] = gathered[piece // n_col, piece % n_col, at : at + 4, :]
    leave(g_copies)


def finish_kernel(stage, total, outer, out, out_one, out_two, g_real, g_imag, sem):
    copy = pltpu.make_async_copy(stage, out, sem)
    copy.start()
    value = total[...]
    for n, grad in enumerate((out_one, out_two)):
        for v in range(3):
            at = 96 * n + 32 * v
            for u in range(3):
                grad[3 * u + v] = value[at : at + 32, 32 * u : 32 * u + 32]
    g_real[...] = outer[:, 0:32].reshape(8, 32, 32)
    g_imag[...] = outer[:, 32:64].reshape(8, 32, 32)
    copy.wait()


def body(n_row, n_col, features, mask, mask_gain, conv_one, conv_two, spec_real, spec_imag, cotangent):
    total_rows, total_cols = 32 * n_row, 512 * n_col
    scaling = 1.0 / math.sqrt((total_rows // RATIO) * (total_cols // RATIO))
    vmem = pl.BlockSpec(memory_space=pltpu.VMEM)
    hbm = pl.BlockSpec(memory_space=pl.ANY)
    col_tab = jnp.asarray(column_tables(n_col))
    row_tab, back_tab = (jnp.asarray(table) for table in row_tables(n_row))
    spread = jnp.asarray(expand_table(), BF16)
    stretch = jnp.asarray(prolong_table(), BF16)
    turn = jnp.asarray(turn_table(), BF16)
    dma = pltpu.SemaphoreType.DMA
    stage, total, outer = pl.pallas_call(
        functools.partial(
            main_kernel, n_row, n_col, scaling, 1.0 / math.sqrt(total_rows * total_cols)
        ),
        out_shape=[
            pltpu.VMEM((32, 32, 512), BF16),
            pltpu.VMEM((192, 128), F32),
            pltpu.VMEM((256, 128), F32),
        ],
        in_specs=[hbm] * 2 + [pl.BlockSpec(memory_space=pltpu.SMEM)] + [hbm] * 11,
        out_specs=[vmem] * 3,
        scratch_shapes=[
            pltpu.VMEM((32, 32, 512), BF16),
            pltpu.VMEM((32, 512), jnp.int32),
            pltpu.VMEM((32, 32, 512), BF16),
            pltpu.VMEM((8, 32, 32), BF16),
            pltpu.VMEM((8, 32, 32), BF16),
            pltpu.VMEM((9, 32, 32), BF16),
            pltpu.VMEM((9, 32, 32), BF16),
            pltpu.VMEM(spread.shape, BF16),
            pltpu.VMEM(stretch.shape, BF16),
            pltpu.VMEM(turn.shape, BF16),
            pltpu.VMEM((40, 32, 640), BF16),
            pltpu.VMEM((40, 32, 640), BF16),
            pltpu.VMEM((192, 512), BF16),
            pltpu.VMEM((192, 512), BF16),
            pltpu.VMEM((10, 32, 512), F32),
            pltpu.VMEM((2, 128, 512), BF16),
            pltpu.SMEM(row_tab.shape[1:], F32),
            pltpu.SMEM(back_tab.shape[1:], F32),
            pltpu.VMEM((64, 384), F32),
            pltpu.VMEM((n_col, 16, 384), F32),
            pltpu.VMEM((2, 16, 384), F32),
            pltpu.VMEM((n_row // 2, 8, 128), F32),
            pltpu.VMEM((n_row // 2, 8, 128), F32),
            pltpu.VMEM((2, 4, 128), F32),
            pltpu.VMEM((n_row, 4, 128), F32),
            pltpu.VMEM((16, 256), F32),
            pltpu.VMEM((n_col, 16, 256), F32),
            pltpu.VMEM((4, 1024), F32),
            pltpu.VMEM((4, 1024), F32),
            pltpu.VMEM((2, 4, 1280), F32),
            pltpu.VMEM((2, 2, 32, 512), BF16),
            pltpu.VMEM((2, 1, 32, 512), BF16),
            pltpu.VMEM((2, 40, 32, 640), BF16),
            pltpu.VMEM((2, 40, 32, 512), BF16),
            pltpu.VMEM((3, 34, 32, 512), BF16),
            pltpu.VMEM((34, 32, 512), F32),
            pltpu.VMEM((3, 192, 256), BF16),
            pltpu.VMEM((3, 256, 256), BF16),
            pltpu.VMEM((256, 384), BF16),
            pltpu.VMEM((3, 192, 256), BF16),
            pltpu.VMEM((3, 192, 256), F32),
            pltpu.VMEM((3, 192, 256), F32),
            pltpu.VMEM((2, n_col, 12, 128), F32),
            pltpu.VMEM((2, n_col, 12, 128), F32),
            pltpu.VMEM((12, 128), F32),
            pltpu.VMEM((n_row // 2, 12, 128), F32),
            pltpu.VMEM((12, 128), F32),
            pltpu.VMEM((2, n_col, 12, 128), F32),
            dma((17,)),
            dma((10,)),
            dma((10,)),
            *[dma((16,))] * 18,
        ],
        compiler_params=pltpu.CompilerParams(
            collective_id=0, has_side_effects=True, vmem_limit_bytes=VMEM_LIMIT
        ),
        name="layer",
    )(
        features, mask, mask_gain, cotangent, spec_real, spec_imag, conv_one, conv_two,
        spread, stretch, turn, col_tab, row_tab, back_tab,
    )
    return pl.pallas_call(
        finish_kernel,
        out_shape=[
            jax.ShapeDtypeStruct((32, 32, 512), BF16),
            jax.ShapeDtypeStruct((9, 32, 32), F32),
            jax.ShapeDtypeStruct((9, 32, 32), F32),
            jax.ShapeDtypeStruct((8, 32, 32), F32),
            jax.ShapeDtypeStruct((8, 32, 32), F32),
        ],
        in_specs=[vmem] * 3,
        out_specs=[hbm] + [vmem] * 4,
        scratch_shapes=[dma],
        compiler_params=pltpu.CompilerParams(vmem_limit_bytes=VMEM_LIMIT),
        name="finish",
    )(*(pltpu.with_memory_space_constraint(value, pltpu.VMEM) for value in (stage, total, outer)))


def solution(mesh):
    n_row, n_col = mesh.shape["row"], mesh.shape["col"]
    placed = (
        P(None, "row", "col"),
        P("row", "col"),
        P(),
        P(),
        P(),
        P(("row", "col"), None, None),
        P(("row", "col"), None, None),
        P(None, "row", "col"),
    )
    return jax.shard_map(
        functools.partial(body, n_row, n_col),
        mesh=mesh,
        in_specs=placed,
        out_specs=(
            P(None, "row", "col"),
            P(),
            P(),
            P(("row", "col"), None, None),
            P(("row", "col"), None, None),
        ),
        check_vma=False,
    )
```
